128 devices in a mesh: pix: 16 (over x, y_hi, core), tm: 8 (over y_lo, z).
Axes of the slice: x: 4, y: 4 (y_hi: 2, y_lo: 2; y = y_hi * 2 + y_lo), z: 4, core: 2. Of those that a mesh axis runs over, the one named last changes fastest.
Arguments:
- movie: bfloat16 [32768, 8192], P('pix', 'tm'), may hold values from -6 to 6
- offsets: int32 [8], replicated, may hold values from -129 to 129, as said below
- spatial: bfloat16 [512, 32768], P('tm', 'pix'), may hold values from -6 to 6
- temporal: bfloat16 [512, 8192], P('pix', 'tm'), may hold values from -6 to 6
- step_spatial: float32 [512], replicated, may hold values from 0.3 to 1
- step_temporal: float32 [512], replicated, may hold values from 0.3 to 1
- thresh_spatial: float32 [512], replicated, may hold values from 0.01 to 0.2
- thresh_temporal: float32 [512], replicated, may hold values from 0.01 to 0.2
Outputs:
- spatial_out: bfloat16 [512, 32768], P('tm', 'pix')
- temporal_out: bfloat16 [512, 8192], P('pix', 'tm')
The draws below stay inside these ranges and needn't reach their ends.
Inputs may be any that keep to these rules, and one draw needn't show every extreme that they name: `offsets`: every offset is a nonzero pixel step of magnitude at most 129; both 129 and -129 occur among them.
All inputs are finite; a program needn't handle non-finite values.
Results may differ from the reference program's by a relative error of at most 0.0052.
Values may be sent and summed in bfloat16 or wider, within the bound.
No kernel may reach another device: no remote copies, remote signals or barrier semaphores. Data moves between devices by JAX's collectives and lax.ppermute only.
A program may use at most 64 MiB of HBM per device.

```python
import math
import jax
import jax.numpy as jnp
from jax import lax

RANK = 512
HALO = 129
NBR = 8
ROUNDS = 2
PIXELS = 32768
FRAMES = 8192


def draw_offsets(key, part):
    first = jax.random.fold_in(key, 11)
    second = jax.random.fold_in(key, 23)
    third = jax.random.fold_in(key, 37)
    magnitude = jax.random.randint(first, (NBR,), 1, HALO + 1)
    signs = jax.random.randint(second, (NBR,), 0, 2) * 2 - 1
    values = (magnitude * signs).astype(jnp.int32)
    order = jax.random.permutation(third, NBR)
    values = values.at[order[0]].set(HALO)
    values = values.at[order[1]].set(-HALO)
    return values.astype(jnp.int32)


def block_scale(key, shape, split, least, high):
    def one(position, blocks):
        heights = jax.random.uniform(jax.random.fold_in(jax.random.fold_in(key, 6), position), (blocks,), jnp.float32, least / len(split), high / len(split))
        return jnp.repeat(jnp.exp(heights), shape[position] // blocks).reshape((-1,) + (1,) * (len(shape) - position - 1))

    level = one(*split[0])
    for cut in split[1:]:
        level = level * one(*cut)
    return level


def scatter_about(rng, dims, spread, most, shards=(), held_as=jnp.bfloat16):
    values = jax.random.normal(rng, dims, jnp.float32) * spread
    if len(shards) > 0:
        values = block_scale(rng, dims, shards, -0.22, 0.18) * values
    return jnp.clip(values, min=-most, max=most).astype(held_as)


def setup_inputs(seed: int = 0) -> dict:
    arg_keys = jax.random.split(jax.random.key(seed), 9)
    movie = scatter_about(arg_keys[0], (PIXELS, FRAMES), 1.0, 6.0, ((0, 16), (1, 8)))
    offsets = draw_offsets(jax.random.fold_in(arg_keys[8], 71), 0)
    spatial = scatter_about(arg_keys[2], (RANK, PIXELS), 1.0, 6.0, ((0, 8), (1, 16)))
    temporal = scatter_about(arg_keys[3], (RANK, FRAMES), 1.0, 6.0, ((0, 16), (1, 8)))
    step_spatial = jnp.clip(jnp.exp(jax.random.uniform(arg_keys[4], (RANK,), jnp.float32, math.log(0.3), math.log(1.0))), 0.3, 1.0)
    step_temporal = jnp.clip(jnp.exp(jax.random.uniform(arg_keys[5], (RANK,), jnp.float32, math.log(0.3), math.log(1.0))), 0.3, 1.0)
    thresh_spatial = jnp.clip(jnp.exp(jax.random.uniform(arg_keys[6], (RANK,), jnp.float32, math.log(0.01), math.log(0.2))), 0.01, 0.2)
    thresh_temporal = jnp.clip(jnp.exp(jax.random.uniform(arg_keys[7], (RANK,), jnp.float32, math.log(0.01), math.log(0.2))), 0.01, 0.2)
    return {"movie": movie, "offsets": offsets, "spatial": spatial, "temporal": temporal, "step_spatial": step_spatial, "step_temporal": step_temporal, "thresh_spatial": thresh_spatial, "thresh_temporal": thresh_temporal}


def soften(values, limit):
    return values - jnp.clip(values, -limit, limit)

def contrast(movie, offsets):
    count = movie.shape[0]
    padded = jnp.pad(movie, ((HALO, HALO), (0, 0)))
    total = jnp.zeros(movie.shape, jnp.float32)
    for neighbour in range(NBR):
        begin = (HALO + offsets[neighbour]).astype(jnp.int32)
        shifted = lax.dynamic_slice_in_dim(padded, begin, count, 0)
        total = total + shifted.astype(jnp.float32)
    return (movie.astype(jnp.float32) - total / NBR).astype(jnp.bfloat16)

def residual(contrasted, spatial_full, temporal_full, rank):
    model = lax.dot_general(spatial_full, temporal_full, (((0,), (0,)), ((), ())), preferred_element_type=jnp.float32)
    return (contrasted.astype(jnp.float32) - model * (1.0 / math.sqrt(rank))).astype(jnp.bfloat16)

def reference(movie, offsets, spatial, temporal, step_spatial, step_temporal, thresh_spatial, thresh_temporal):
    contrasted = contrast(movie, offsets)
    coef_temporal = step_temporal * (math.sqrt(RANK) / PIXELS)
    coef_spatial = step_spatial * (math.sqrt(RANK) / FRAMES)
    space_now = spatial
    time_now = temporal
    for turn in range(ROUNDS):
        errors = residual(contrasted, space_now, time_now, RANK)
        grad_temporal = jnp.dot(space_now, errors, preferred_element_type=jnp.float32)
        time_now = soften(time_now.astype(jnp.float32) + coef_temporal[:, None] * grad_temporal, thresh_temporal[:, None]).astype(jnp.bfloat16)
        errors = residual(contrasted, space_now, time_now, RANK)
        grad_spatial = lax.dot_general(time_now, errors, (((1,), (1,)), ((), ())), preferred_element_type=jnp.float32)
        space_now = soften(space_now.astype(jnp.float32) + coef_spatial[:, None] * grad_spatial, thresh_spatial[:, None]).astype(jnp.bfloat16)
    return (space_now, time_now)
```

```python
import functools
import math

import jax
import jax.numpy as jnp
from jax import lax
from jax.experimental import pallas as pl
from jax.experimental.pallas import tpu as pltpu
from jax.sharding import PartitionSpec as P

HALO = 129
EDGE = 144
BLOCK = 256
NBR = 8
ROUNDS = 2
BF16 = jnp.bfloat16
F32 = jnp.float32


def pix_pairs(move):
    pairs = []
    for x in range(4):
        for y in range(2):
            for c in range(2):
                to = move(x, y, c)
                pairs.append((x * 4 + y * 2 + c, (to[0] % 4) * 4 + (to[1] % 2) * 2 + to[2] % 2))
    return pairs


def tm_pairs(move):
    pairs = []
    for y in range(2):
        for z in range(4):
            to = move(y, z)
            pairs.append((y * 4 + z, (to[0] % 2) * 4 + to[1] % 4))
    return pairs


def by_core(a):
    return lax.ppermute(a, "pix", pix_pairs(lambda x, y, c: (x, y, c + 1)))


def by_yhi(a):
    return lax.ppermute(a, "pix", pix_pairs(lambda x, y, c: (x, y + 1, c)))


def by_x(a, d):
    return lax.ppermute(a, "pix", pix_pairs(lambda x, y, c: (x + d, y, c)))


def by_ylo(a):
    return lax.ppermute(a, "tm", tm_pairs(lambda y, z: (y + 1, z)))


def by_z(a, d):
    return lax.ppermute(a, "tm", tm_pairs(lambda y, z: (y, z + d)))


def pick(a, index, axis):
    return lax.dynamic_index_in_dim(a, index, axis, keepdims=False)


def gather_pair(own, here, send, axis):
    other = send(own)
    low = jnp.where(here == 0, own, other)
    high = jnp.where(here == 0, other, own)
    return jnp.stack([low, high], axis)


def gather_four(own, here, send, axis):
    got = [own] + [send(own, d) for d in (1, 2, 3)]
    slots = []
    for k in range(4):
        slots.append(lax.select_n(jnp.mod(here - k, 4), *got))
    return jnp.stack(slots, axis)


def reduce_pair(a, here, send, axis):
    got = send(pick(a, 1 - here, axis).astype(BF16))
    return pick(a, here, axis) + got.astype(F32)


def reduce_four(a, here, send, axis):
    total = pick(a, here, axis)
    got = [send(pick(a, jnp.mod(here + d, 4), axis).astype(BF16), d) for d in (1, 2, 3)]
    for g in got:
        total = total + g.astype(F32)
    return total


def soften(values, limit):
    return values - jnp.clip(values, -limit, limit)


def stencil(offsets_ref, movie_ref, before_ref, after_ref, out_ref):
    def band(columns, base):
        step = (
            lax.broadcasted_iota(jnp.int32, (BLOCK, columns), 1)
            - lax.broadcasted_iota(jnp.int32, (BLOCK, columns), 0)
            + base
        )
        weight = jnp.where(step == 0, 1.0, 0.0).astype(F32)
        for k in range(NBR):
            weight = weight - jnp.where(step == offsets_ref[k], 1.0 / NBR, 0.0).astype(F32)
        return weight.astype(BF16)

    rows = movie_ref.shape[0]
    blocks = rows // BLOCK
    main = band(3 * BLOCK, -BLOCK)
    for b in range(blocks):
        low = max(b - 1, 0) * BLOCK
        high = min(b + 2, blocks) * BLOCK
        first = low - (b - 1) * BLOCK
        total = jnp.dot(
            main[:, first : first + high - low], movie_ref[low:high, :], preferred_element_type=F32
        )
        if b == 0:
            total += jnp.dot(band(EDGE, -EDGE), before_ref[...], preferred_element_type=F32)
        if b == blocks - 1:
            total += jnp.dot(band(EDGE, BLOCK), after_ref[...], preferred_element_type=F32)
        out_ref[b * BLOCK : (b + 1) * BLOCK, :] = total.astype(BF16)


def contrast(movie, offsets):
    size = lax.axis_size("pix")
    rows = movie.shape[0]
    up = [(i, i + 1) for i in range(size - 1)]
    down = [(j, i) for i, j in up]
    before = lax.ppermute(movie[rows - EDGE :], "pix", up)
    after = lax.ppermute(movie[:EDGE], "pix", down)
    vmem = pl.BlockSpec(memory_space=pltpu.VMEM)
    return pl.pallas_call(
        stencil,
        out_shape=jax.ShapeDtypeStruct(movie.shape, BF16),
        in_specs=[pl.BlockSpec(memory_space=pltpu.SMEM), vmem, vmem, vmem],
        out_specs=vmem,
        compiler_params=pltpu.CompilerParams(vmem_limit_bytes=32 * 1024 * 1024),
    )(offsets, movie, before, after)


def dot(a, b, over):
    return lax.dot_general(a, b, ((over[0], over[1]), ((), ())), preferred_element_type=F32)


def per_device(
    movie, offsets, spatial, temporal, step_spatial, step_temporal, thresh_spatial, thresh_temporal
):
    spatial_rows, strip = spatial.shape
    temporal_rows, span = temporal.shape
    rank = spatial_rows * lax.axis_size("tm")
    pixels = strip * lax.axis_size("pix")
    frames = span * lax.axis_size("tm")
    half = strip // 2
    pix = lax.axis_index("pix")
    tm = lax.axis_index("tm")
    x, yhi, core = pix // 4, (pix // 2) % 2, pix % 2
    ylo, z = tm // 4, tm % 4

    def own(a, index, rows):
        return lax.dynamic_slice_in_dim(a, index * rows, rows, 0)[:, None]

    coef_temporal = own(step_temporal * (math.sqrt(rank) / pixels), pix, temporal_rows)
    coef_spatial = own(step_spatial * (math.sqrt(rank) / frames), tm, spatial_rows)
    limit_temporal = own(thresh_temporal, pix, temporal_rows)
    limit_spatial = own(thresh_spatial, tm, spatial_rows)
    scale = 1.0 / math.sqrt(rank)

    def gather_temporal(t):
        a = gather_pair(t, yhi, by_yhi, 0)
        a = gather_four(a, x, by_x, 0)
        a = gather_pair(a, core, by_core, 2)
        return a.reshape(rank, span)

    def gather_spatial(sa, sb):
        a = gather_pair(sa, ylo, by_ylo, 0)
        b = gather_four(sb, z, by_z, 0)
        a = gather_four(a, z, by_z, 1)
        b = gather_pair(b, ylo, by_ylo, 0)
        return a.reshape(rank, half), b.reshape(rank, half)

    def reduce_temporal(g):
        g = g.reshape(4, 2, 2, temporal_rows, span)
        g = reduce_pair(g, core, by_core, 2)
        g = reduce_four(g, x, by_x, 0)
        return reduce_pair(g, yhi, by_yhi, 0)

    def reduce_spatial(ga, gb):
        ga = ga.reshape(2, 4, spatial_rows, half)
        gb = gb.reshape(2, 4, spatial_rows, half)
        ga = reduce_four(ga, z, by_z, 1)
        gb = reduce_pair(gb, ylo, by_ylo, 0)
        ga = reduce_pair(ga, ylo, by_ylo, 0)
        gb = reduce_four(gb, z, by_z, 0)
        return ga, gb

    sa, sb = spatial[:, :half], spatial[:, half:]
    t = temporal
    full_a, full_b = gather_spatial(sa, sb)
    full_t = gather_temporal(t)
    contrasted = contrast(movie, offsets)
    ca, cb = contrasted[:half], contrasted[half:]
    for turn in range(ROUNDS):
        gram = dot(full_a, full_a, ((1,), (1,))) + dot(full_b, full_b, ((1,), (1,)))
        cross = dot(full_a, ca, ((1,), (0,))) + dot(full_b, cb, ((1,), (0,)))
        grad = cross - dot((gram * scale).astype(BF16), full_t, ((1,), (0,)))
        grad = reduce_temporal(grad)
        t = soften(t.astype(F32) + coef_temporal * grad, limit_temporal).astype(BF16)
        full_t = gather_temporal(t)
        gram = (dot(full_t, full_t, ((1,), (1,))) * scale).astype(BF16)
        grad_a = dot(full_t, ca, ((1,), (1,))) - dot(gram, full_a, ((1,), (0,)))
        grad_b = dot(full_t, cb, ((1,), (1,))) - dot(gram, full_b, ((1,), (0,)))
        grad_a, grad_b = reduce_spatial(grad_a, grad_b)
        sa = soften(sa.astype(F32) + coef_spatial * grad_a, limit_spatial).astype(BF16)
        sb = soften(sb.astype(F32) + coef_spatial * grad_b, limit_spatial).astype(BF16)
        if turn < ROUNDS - 1:
            full_a, full_b = gather_spatial(sa, sb)
    return jnp.concatenate([sa, sb], 1), t


def solution(mesh):
    placed = (P("pix", "tm"), P(), P("tm", "pix"), P("pix", "tm"), P(), P(), P(), P())
    return jax.shard_map(
        per_device,
        mesh=mesh,
        in_specs=placed,
        out_specs=(P("tm", "pix"), P("pix", "tm")),
        check_vma=False,
    )
```

```python
import math

import jax
import jax.numpy as jnp
from jax import lax
from jax.experimental import pallas as pl
from jax.experimental.pallas import tpu as pltpu
from jax.sharding import PartitionSpec as P

HALO = 129
EDGE = 144
BLOCK = 256
NBR = 8
ROUNDS = 2
BF16 = jnp.bfloat16
F32 = jnp.float32

PARTS = ((0, 640, (3, 4, 1)), (640, 768, (4, 1, 3)), (1408, 640, (1, 3, 4)))
SAME_X = [[x * 4 + rest for x in range(4)] for rest in range(4)]
VMEM = pl.BlockSpec(memory_space=pltpu.VMEM)
SMEM = pl.BlockSpec(memory_space=pltpu.SMEM)
PARAMS = pltpu.CompilerParams(vmem_limit_bytes=24 * 1024 * 1024)


def hop(a, axis, mask):
    size = lax.axis_size(axis)
    return lax.ppermute(a, axis, [(i, i ^ mask) for i in range(size)])


def hop_x(a, d):
    size = lax.axis_size("pix")
    return lax.ppermute(a, "pix", [(i, (i + 4 * d) % size) for i in range(size)])


def reach(order, position):
    first, second, third = order
    return first * (position // 4) ^ second * (position // 2 % 2) ^ third * (position % 2)


def soften(values, limit):
    return values - jnp.clip(values, -limit, limit)


def nn(a, b):
    return jnp.dot(a, b, preferred_element_type=F32)


def nt(a, b):
    return lax.dot_general(a, b, (((1,), (1,)), ((), ())), preferred_element_type=F32)


def stencil(offsets_ref, movie_ref, before_ref, after_ref, out_ref):
    def band(columns, base):
        step = (
            lax.broadcasted_iota(jnp.int32, (BLOCK, columns), 1)
            - lax.broadcasted_iota(jnp.int32, (BLOCK, columns), 0)
            + base
        )
        weight = jnp.where(step == 0, 1.0, 0.0).astype(F32)
        for k in range(NBR):
            weight = weight - jnp.where(step == offsets_ref[k], 1.0 / NBR, 0.0).astype(F32)
        return weight.astype(BF16)

    rows = movie_ref.shape[0]
    blocks = rows // BLOCK
    main = band(3 * BLOCK, -BLOCK)
    for b in range(blocks):
        low = max(b - 1, 0) * BLOCK
        high = min(b + 2, blocks) * BLOCK
        first = low - (b - 1) * BLOCK
        total = nn(main[:, first : first + high - low], movie_ref[low:high, :])
        if b == 0:
            total += nn(band(EDGE, -EDGE), before_ref[...])
        if b == blocks - 1:
            total += nn(band(EDGE, BLOCK), after_ref[...])
        out_ref[b * BLOCK : (b + 1) * BLOCK, :] = total.astype(BF16)


def contrast(movie, offsets):
    size = lax.axis_size("pix")
    rows = movie.shape[0]
    up = [(i, i + 1) for i in range(size - 1)]
    down = [(j, i) for i, j in up]
    before = lax.ppermute(movie[rows - EDGE :], "pix", up)
    after = lax.ppermute(movie[:EDGE], "pix", down)
    return pl.pallas_call(
        stencil,
        out_shape=jax.ShapeDtypeStruct(movie.shape, BF16),
        in_specs=[SMEM, VMEM, VMEM, VMEM],
        out_specs=VMEM,
        compiler_params=PARAMS,
    )(offsets, movie, before, after)


def place_temporal(place_ref, mine_ref, other_ref, full_ref):
    x, core = place_ref[1], place_ref[2]
    for d in range(4):
        for y in range(2):
            row = (((x + 4 - d) % 4) * 2 + y) * 64
            piece = pl.ds((d * 2 + y) * 32, 32)
            full_ref[pl.ds(pl.multiple_of(row + core * 32, 32), 32), :] = mine_ref[piece, :]
            full_ref[pl.ds(pl.multiple_of(row + 32 - core * 32, 32), 32), :] = other_ref[piece, :]


def temporal_step(
    place_ref, a0, b0, a1, b1, a2, b2, contrasted_ref, mine_ref, other_ref,
    full_ref, send_ref, keep_ref, time_ref, gram_ref, grad_ref,
):
    tm, core = place_ref[0], place_ref[2]
    for (begin, width, order), near, far in zip(PARTS, (a0, a1, a2), (b0, b1, b2)):
        for position in range(8):
            row = pl.multiple_of((tm ^ reach(order, position)) * 64, 64)
            piece = near if position < 4 else far
            full_ref[pl.ds(row, 64), begin : begin + width] = piece[pl.ds(position % 4 * 64, 64), :]
    place_temporal(place_ref, mine_ref, other_ref, time_ref)
    rank, span = time_ref.shape
    scale = 1.0 / math.sqrt(rank)
    for r in range(0, rank, BLOCK):
        gram_ref[r : r + BLOCK, :] = (nt(full_ref[r : r + BLOCK, :], full_ref[...]) * scale).astype(BF16)
    for f in range(0, span, BLOCK):
        columns = slice(f, f + BLOCK)
        grad_ref[...] = nn(full_ref[...], contrasted_ref[:, columns]) - nn(gram_ref[...], time_ref[:, columns])
        for i in range(8):
            piece = pl.ds(i * 32, 32)
            keep_ref[piece, columns] = grad_ref[pl.ds(pl.multiple_of(i * 64 + core * 32, 32), 32), :]
            send_ref[piece, columns] = grad_ref[
                pl.ds(pl.multiple_of(i * 64 + 32 - core * 32, 32), 32), :
            ].astype(BF16)


def spatial_step(
    place_ref, full_ref, contrasted_ref, mine_ref, other_ref,
    s0, k0, s1, k1, s2, k2, time_ref, gram_ref, grad_ref,
):
    tm = place_ref[0]
    place_temporal(place_ref, mine_ref, other_ref, time_ref)
    rank = time_ref.shape[0]
    scale = 1.0 / math.sqrt(rank)
    for r in range(0, rank, BLOCK):
        gram_ref[r : r + BLOCK, :] = (nt(time_ref[r : r + BLOCK, :], time_ref[...]) * scale).astype(BF16)
    for (begin, width, order), send_ref, keep_ref in zip(PARTS, (s0, s1, s2), (k0, k1, k2)):
        for low in range(0, width, BLOCK):
            size = min(BLOCK, width - low)
            pixels = slice(begin + low, begin + low + size)
            columns = slice(low, low + size)
            grad_ref[:, :size] = nt(time_ref[...], contrasted_ref[pixels, :]) - nn(
                gram_ref[...], full_ref[:, pixels]
            )
            for position in range(8):
                row = pl.multiple_of((tm ^ reach(order, position)) * 64, 64)
                piece = grad_ref[pl.ds(row, 64), :size]
                if position < 4:
                    keep_ref[position * 64 : position * 64 + 64, columns] = piece
                else:
                    send_ref[position * 64 - 256 : position * 64 - 192, columns] = piece.astype(BF16)


def per_device(
    movie, offsets, spatial, temporal, step_spatial, step_temporal, thresh_spatial, thresh_temporal
):
    spatial_rows, strip = spatial.shape
    temporal_rows, span = temporal.shape
    rank = spatial_rows * lax.axis_size("tm")
    pixels = strip * lax.axis_size("pix")
    frames = span * lax.axis_size("tm")
    pix = lax.axis_index("pix")
    tm = lax.axis_index("tm")
    x, yhi, core = pix // 4, (pix // 2) % 2, pix % 2
    place = jnp.stack([tm, x, core]).astype(jnp.int32)

    def own(a, index, rows):
        return lax.dynamic_slice_in_dim(a, index * rows, rows, 0)[:, None]

    all_temporal = step_temporal * (math.sqrt(rank) / pixels)
    all_spatial = step_spatial * (math.sqrt(rank) / frames)

    def own_pair(a):
        return jnp.concatenate([own(a, x * 4 + core, temporal_rows), own(a, x * 4 + 2 + core, temporal_rows)])

    def own_slabs(a, mask):
        return jnp.concatenate([own(a, tm, spatial_rows), own(a, tm ^ mask, spatial_rows)])

    coef_temporal, limit_temporal = own_pair(all_temporal), own_pair(thresh_temporal)
    coef_spatial = [own_slabs(all_spatial, order[2]) for _, _, order in PARTS]
    limit_spatial = [own_slabs(thresh_spatial, order[2]) for _, _, order in PARTS]

    def gather_spatial(slabs):
        near = [jnp.concatenate([s, hop(s, "tm", order[1])]) for s, (_, _, order) in zip(slabs, PARTS)]
        return [(a, hop(a, "tm", order[0])) for a, (_, _, order) in zip(near, PARTS)]

    def gather_temporal(pair):
        mine = jnp.concatenate([pair] + [hop_x(pair, d) for d in (1, 2, 3)])
        return mine, hop(mine, "pix", 1)

    shards = [spatial[:, begin : begin + width] for begin, width, _ in PARTS]
    slabs = [jnp.concatenate([s, hop(s, "tm", order[2])]) for s, (_, _, order) in zip(shards, PARTS)]
    pieces = gather_spatial(slabs)
    contrasted = contrast(movie, offsets)
    across = hop(temporal, "pix", 2)
    pair = jnp.concatenate([jnp.where(yhi == 0, temporal, across), jnp.where(yhi == 0, across, temporal)])
    mine, other = gather_temporal(pair)

    for turn in range(ROUNDS):
        full, send, keep = pl.pallas_call(
            temporal_step,
            out_shape=[
                jax.ShapeDtypeStruct((rank, strip), BF16),
                jax.ShapeDtypeStruct((rank // 2, span), BF16),
                jax.ShapeDtypeStruct((rank // 2, span), F32),
            ],
            in_specs=[SMEM] + [VMEM] * 9,
            out_specs=[VMEM] * 3,
            scratch_shapes=[
                pltpu.VMEM((rank, span), BF16),
                pltpu.VMEM((rank, rank), BF16),
                pltpu.VMEM((rank, BLOCK), F32),
            ],
            compiler_params=PARAMS,
        )(place, *[piece for both in pieces for piece in both], contrasted, mine, other)
        grad = (keep + hop(send, "pix", 1).astype(F32)).astype(BF16)
        grad = lax.all_to_all(
            grad.reshape(4, 2 * temporal_rows, span), "pix", 0, 0, axis_index_groups=SAME_X
        )
        grad = jnp.sum(grad.astype(F32), 0).astype(BF16)
        grad = grad.astype(F32) + hop(grad, "pix", 2).astype(F32)
        pair = soften(pair.astype(F32) + coef_temporal * grad, limit_temporal).astype(BF16)
        mine, other = gather_temporal(pair)
        outs = []
        for _, width, _ in PARTS:
            outs += [jax.ShapeDtypeStruct((rank // 2, width), BF16), jax.ShapeDtypeStruct((rank // 2, width), F32)]
        grads = pl.pallas_call(
            spatial_step,
            out_shape=outs,
            in_specs=[SMEM] + [VMEM] * 4,
            out_specs=[VMEM] * 6,
            scratch_shapes=[
                pltpu.VMEM((rank, span), BF16),
                pltpu.VMEM((rank, rank), BF16),
                pltpu.VMEM((rank, BLOCK), F32),
            ],
            compiler_params=PARAMS,
        )(place, full, contrasted, mine, other)
        totals = [
            keep + hop(send, "tm", order[0]).astype(F32)
            for send, keep, (_, _, order) in zip(grads[0::2], grads[1::2], PARTS)
        ]
        half = 2 * spatial_rows
        totals = [
            total[:half] + hop(total[half:].astype(BF16), "tm", order[1]).astype(F32)
            for total, (_, _, order) in zip(totals, PARTS)
        ]
        if turn < ROUNDS - 1:
            sums = []
            for total, (_, _, order) in zip(totals, PARTS):
                mine_sum = total.astype(BF16)
                got = hop(mine_sum, "tm", order[2])
                swapped = jnp.concatenate([got[spatial_rows:], got[:spatial_rows]])
                sums.append(mine_sum.astype(F32) + swapped.astype(F32))
            slabs = [
                soften(s.astype(F32) + coef * g, limit).astype(BF16)
                for s, g, coef, limit in zip(slabs, sums, coef_spatial, limit_spatial)
            ]
            pieces = gather_spatial(slabs)
        else:
            sums = [
                total[:spatial_rows] + hop(total[spatial_rows:].astype(BF16), "tm", order[2]).astype(F32)
                for total, (_, _, order) in zip(totals, PARTS)
            ]
            shards = [
                soften(s[:spatial_rows].astype(F32) + coef[:spatial_rows] * g, limit[:spatial_rows]).astype(BF16)
                for s, g, coef, limit in zip(slabs, sums, coef_spatial, limit_spatial)
            ]
    temporal_out = jnp.where(yhi == 0, pair[:temporal_rows], pair[temporal_rows:])
    return jnp.concatenate(shards, 1), temporal_out


def solution(mesh):
    placed = (P("pix", "tm"), P(), P("tm", "pix"), P("pix", "tm"), P(), P(), P(), P())
    return jax.shard_map(
        per_device,
        mesh=mesh,
        in_specs=placed,
        out_specs=(P("tm", "pix"), P("pix", "tm")),
        check_vma=False,
    )
```

```python
import functools
import math

import jax
import jax.numpy as jnp
from jax import lax
from jax.experimental import pallas as pl
from jax.experimental.pallas import tpu as pltpu
from jax.sharding import PartitionSpec as P

HALO = 129
EDGE = 144
BLOCK = 256
NBR = 8
ROUNDS = 2
BF16 = jnp.bfloat16
F32 = jnp.float32

PARTS = ((0, 640, (3, 4, 1)), (640, 768, (4, 1, 3)), (1408, 640, (1, 3, 4)))
VMEM = pl.BlockSpec(memory_space=pltpu.VMEM)
SMEM = pl.BlockSpec(memory_space=pltpu.SMEM)
ANY = pl.BlockSpec(memory_space=pl.ANY)
HBM = pl.BlockSpec(memory_space=pltpu.HBM)
COPIES = pltpu.SemaphoreType.DMA((64,))
PARAMS = pltpu.CompilerParams(vmem_limit_bytes=20 * 1024 * 1024)


def hop(a, axis, mask):
    size = lax.axis_size(axis)
    return lax.ppermute(a, axis, [(i, i ^ mask) for i in range(size)])


def hop_x(a, second):
    size = lax.axis_size("pix")
    return lax.ppermute(a, "pix", [(i, i ^ 4 * (1 if i % 2 == second else 3)) for i in range(size)])


def reach(order, position):
    first, second, third = order
    return first * (position // 4) ^ second * (position // 2 % 2) ^ third * (position % 2)


def soften(values, limit):
    return values - jnp.clip(values, -limit, limit)


def nn(a, b):
    return jnp.dot(a, b, preferred_element_type=F32)


def nt(a, b):
    return lax.dot_general(a, b, (((1,), (1,)), ((), ())), preferred_element_type=F32)


class Copies:
    def __init__(self, sems):
        self.sems = sems
        self.used = 0

    def start(self, source, target):
        copy = pltpu.make_async_copy(source, target, self.sems.at[self.used])
        self.used += 1
        copy.start()
        return copy


def stencil(offsets_ref, movie_ref, before_ref, after_ref, later_ref, out_ref, held_ref, made_ref, sems):
    del later_ref
    rows = movie_ref.shape[0]
    blocks = rows // BLOCK
    copies = Copies(sems)

    def block(b):
        return pl.ds(b * BLOCK, BLOCK)

    loads = [copies.start(movie_ref.at[block(b), :], held_ref.at[block(b), :]) for b in range(blocks)]

    def band(columns, base):
        step = (
            lax.broadcasted_iota(jnp.int32, (BLOCK, columns), 1)
            - lax.broadcasted_iota(jnp.int32, (BLOCK, columns), 0)
            + base
        )
        weight = jnp.where(step == 0, 1.0, 0.0).astype(F32)
        for k in range(NBR):
            weight = weight - jnp.where(step == offsets_ref[k], 1.0 / NBR, 0.0).astype(F32)
        return weight.astype(BF16)

    main = band(3 * BLOCK, -BLOCK)
    loads[0].wait()
    stores = []
    for b in range(blocks):
        if b + 1 < blocks:
            loads[b + 1].wait()
        low = max(b - 1, 0) * BLOCK
        high = min(b + 2, blocks) * BLOCK
        first = low - (b - 1) * BLOCK
        total = nn(main[:, first : first + high - low], held_ref[low:high, :])
        if b == 0:
            total += nn(band(EDGE, -EDGE), before_ref[...])
        if b == blocks - 1:
            total += nn(band(EDGE, BLOCK), after_ref[...])
        made_ref[b * BLOCK : (b + 1) * BLOCK, :] = total.astype(BF16)
        stores.append(copies.start(made_ref.at[block(b), :], out_ref.at[block(b), :]))
    for store in stores:
        store.wait()


def contrast(movie, before, after, offsets, later):
    return pl.pallas_call(
        stencil,
        out_shape=pltpu.HBM(movie.shape, BF16),
        in_specs=[SMEM, HBM, VMEM, VMEM, ANY],
        out_specs=HBM,
        scratch_shapes=[pltpu.VMEM(movie.shape, BF16), pltpu.VMEM(movie.shape, BF16), COPIES],
        compiler_params=PARAMS,
    )(offsets, in_hbm(movie), before, after, later)


def in_hbm(a):
    return pltpu.with_memory_space_constraint(a, pltpu.HBM)


def row_of(x, y, core):
    return pl.multiple_of((x * 2 + y) * 64 + core * 32, 32)


def near_x(x, core, position):
    first, second = 1 + 2 * core, 3 - 2 * core
    return x ^ (first * (position // 2)) ^ (second * (position % 2))


def temporal_rows(place_ref, source_ref, target_ref, flip):
    x, core = place_ref[1], place_ref[2] ^ flip
    for position in range(4):
        for y in range(2):
            piece = pl.ds(position * 64 + y * 32, 32)
            target_ref[piece, :] = source_ref[pl.ds(row_of(near_x(x, core, position), y, core), 32), :]


def place_temporal(place_ref, mine_ref, other_ref, time_ref, copies):
    x, core = place_ref[1], place_ref[2]
    loads = []
    for position in range(4):
        for y in range(2):
            piece = pl.ds(position * 64 + y * 32, 32)
            for from_ref, side in ((mine_ref, core), (other_ref, core ^ 1)):
                row = row_of(near_x(x, side, position), y, side)
                loads.append(copies.start(from_ref.at[piece, :], time_ref.at[pl.ds(row, 32), :]))
    return loads


def temporal_send(
    place_ref, a0, b0, a1, b1, a2, b2, contrasted_ref, mine_ref, other_ref,
    full_ref, time_ref, stored_ref, send_ref, rows_ref, gram_ref, held_ref, sems,
):
    tm = place_ref[0]
    copies = Copies(sems)
    loads = []
    for (begin, width, order), near, far in zip(PARTS, (a0, a1, a2), (b0, b1, b2)):
        for position in range(8):
            row = pl.multiple_of((tm ^ reach(order, position)) * 64, 64)
            piece = near if position < 4 else far
            loads.append(
                copies.start(
                    piece.at[pl.ds(position % 4 * 64, 64), :],
                    full_ref.at[pl.ds(row, 64), pl.ds(begin, width)],
                )
            )
    blocks = hold(contrasted_ref, held_ref, copies)
    times = place_temporal(place_ref, mine_ref, other_ref, time_ref, copies)
    for load in loads:
        load.wait()
    store = copies.start(full_ref, stored_ref)
    temporal_half(place_ref, full_ref, time_ref, send_ref, rows_ref, gram_ref, held_ref, blocks, times, 1)
    store.wait()


def temporal_keep(
    place_ref, full_ref, contrasted_ref, time_ref, keep_ref, rows_ref, gram_ref, held_ref, sems
):
    blocks = hold(contrasted_ref, held_ref, Copies(sems))
    temporal_half(place_ref, full_ref, time_ref, keep_ref, rows_ref, gram_ref, held_ref, blocks, [], 0)


def hold(contrasted_ref, held_ref, copies):
    span = held_ref.shape[1]
    return [
        copies.start(contrasted_ref.at[:, pl.ds(f, BLOCK)], held_ref.at[:, pl.ds(f, BLOCK)])
        for f in range(0, span, BLOCK)
    ]


def temporal_half(
    place_ref, full_ref, time_ref, out_ref, rows_ref, gram_ref, held_ref, blocks, times, flip
):
    temporal_rows(place_ref, full_ref, rows_ref, flip)
    rank, span = time_ref.shape
    gram_ref[...] = (nt(rows_ref[...], full_ref[...]) * (1.0 / math.sqrt(rank))).astype(BF16)
    for load in times:
        load.wait()
    for f in range(0, span, BLOCK):
        columns = slice(f, f + BLOCK)
        blocks[f // BLOCK].wait()
        grad = nn(rows_ref[...], held_ref[:, columns]) - nn(gram_ref[...], time_ref[:, columns])
        out_ref[:, columns] = grad.astype(out_ref.dtype)


def spatial_loads(part, full_ref, contrasted_ref, strip_ref, held_ref, copies):
    begin, width, _ = PARTS[part]
    return [
        copies.start(contrasted_ref.at[pl.ds(begin, width), :], held_ref.at[pl.ds(0, width), :]),
        copies.start(full_ref.at[:, pl.ds(begin, width)], strip_ref.at[:, pl.ds(0, width)]),
    ]


def spatial_half(
    part, place_ref, time_ref, gram_ref, send_ref, keep_ref, rows_ref, weight_ref, strip_ref, held_ref, loads
):
    _, width, order = PARTS[part]
    tm = place_ref[0]
    for position in range(8):
        row = pl.multiple_of((tm ^ reach(order, position)) * 64, 64)
        piece = pl.ds(position * 64, 64)
        rows_ref[piece, :] = time_ref[pl.ds(row, 64), :]
        weight_ref[piece, :] = gram_ref[pl.ds(row, 64), :]
    for load in loads:
        load.wait()
    half = rows_ref.shape[0] // 2
    for low in range(0, width, BLOCK):
        size = min(BLOCK, width - low)
        pixels = slice(low, low + size)
        for out_ref, first in ((send_ref, half), (keep_ref, 0)):
            rows = slice(first, first + half)
            grad = nt(rows_ref[rows, :], held_ref[pixels, :]) - nn(weight_ref[rows, :], strip_ref[:, pixels])
            out_ref[:, pixels] = grad.astype(out_ref.dtype)


def spatial_part(
    part, place_ref, full_ref, contrasted_ref, time_ref, gram_ref,
    send_ref, keep_ref, rows_ref, weight_ref, strip_ref, held_ref, sems,
):
    loads = spatial_loads(part, full_ref, contrasted_ref, strip_ref, held_ref, Copies(sems))
    spatial_half(
        part, place_ref, time_ref, gram_ref, send_ref, keep_ref, rows_ref, weight_ref, strip_ref, held_ref, loads
    )


def spatial_first(
    place_ref, full_ref, contrasted_ref, mine_ref, other_ref,
    send_ref, keep_ref, time_ref, gram_ref, rows_ref, weight_ref, strip_ref, held_ref, sems,
):
    copies = Copies(sems)
    times = place_temporal(place_ref, mine_ref, other_ref, time_ref, copies)
    loads = spatial_loads(0, full_ref, contrasted_ref, strip_ref, held_ref, copies)
    for load in times:
        load.wait()
    gram_ref[...] = (nt(time_ref[...], time_ref[...]) * (1.0 / math.sqrt(time_ref.shape[0]))).astype(BF16)
    spatial_half(
        0, place_ref, time_ref, gram_ref, send_ref, keep_ref, rows_ref, weight_ref, strip_ref, held_ref, loads
    )


def per_device(
    movie, offsets, spatial, temporal, step_spatial, step_temporal, thresh_spatial, thresh_temporal
):
    slab, strip = spatial.shape
    shard, span = temporal.shape
    rank = slab * lax.axis_size("tm")
    pixels = strip * lax.axis_size("pix")
    frames = span * lax.axis_size("tm")
    pix = lax.axis_index("pix")
    tm = lax.axis_index("tm")
    x, yhi, core = pix >> 2, (pix >> 1) & 1, pix & 1
    place = jnp.stack([tm, x, core]).astype(jnp.int32)

    def own(a, index, rows):
        return lax.dynamic_slice_in_dim(a, index * rows, rows, 0)[:, None]

    def own_temporal(a):
        across = x ^ (3 - 2 * core)
        return jnp.concatenate([own(a, at * 4 + y * 2 + core, shard) for at in (x, across) for y in range(2)])

    def own_spatial(a, mask):
        return jnp.concatenate([own(a, tm, slab), own(a, tm ^ mask, slab)])

    coef_temporal = own_temporal(step_temporal * (math.sqrt(rank) / pixels))
    limit_temporal = own_temporal(thresh_temporal)
    all_spatial = step_spatial * (math.sqrt(rank) / frames)
    coef_spatial = [own_spatial(all_spatial, order[2]) for _, _, order in PARTS]
    limit_spatial = [own_spatial(thresh_spatial, order[2]) for _, _, order in PARTS]

    def second_gather(slabs):
        return [jnp.concatenate([s, hop(s, "tm", order[1])]) for s, (_, _, order) in zip(slabs, PARTS)]

    def first_gather(near):
        return [(a, hop(a, "tm", order[0])) for a, (_, _, order) in zip(near, PARTS)]

    def gather_temporal(quad):
        mine = jnp.concatenate([quad, hop_x(quad, 0)])
        return mine, hop(mine, "pix", 1)

    shards = [spatial[:, begin : begin + width] for begin, width, _ in PARTS]
    size = lax.axis_size("pix")
    up = [(i, i + 1) for i in range(size - 1)]
    down = [(j, i) for i, j in up]
    before = lax.ppermute(movie[movie.shape[0] - EDGE :], "pix", up)
    after = lax.ppermute(movie[:EDGE], "pix", down)
    slabs = [jnp.concatenate([s, hop(s, "tm", order[2])]) for s, (_, _, order) in zip(shards, PARTS)]
    across = hop(temporal, "pix", 2)
    pair = jnp.concatenate([jnp.where(yhi == 0, temporal, across), jnp.where(yhi == 0, across, temporal)])
    near = second_gather(slabs)
    near, before, after = lax.optimization_barrier((near, before, after))
    pieces = first_gather(near)
    quad = jnp.concatenate([pair, hop_x(pair, 1)])
    contrasted = contrast(movie, before, after, offsets, near[1])
    mine, other = gather_temporal(quad)

    half = rank // 2
    for turn in range(ROUNDS):
        scratch = [
            pltpu.VMEM((half, strip), BF16),
            pltpu.VMEM((half, rank), BF16),
            pltpu.VMEM((strip, span), BF16),
            COPIES,
        ]
        full, time, stored, send = pl.pallas_call(
            temporal_send,
            out_shape=[
                jax.ShapeDtypeStruct((rank, strip), BF16),
                jax.ShapeDtypeStruct((rank, span), BF16),
                pltpu.HBM((rank, strip), BF16),
                jax.ShapeDtypeStruct((half, span), BF16),
            ],
            in_specs=[SMEM] + [ANY] * 6 + [HBM, ANY, ANY],
            out_specs=[VMEM, VMEM, HBM, VMEM],
            scratch_shapes=scratch,
            compiler_params=PARAMS,
        )(place, *[piece for both in pieces for piece in both], in_hbm(contrasted), mine, other)
        got = hop(send, "pix", 1)
        keep = pl.pallas_call(
            temporal_keep,
            out_shape=jax.ShapeDtypeStruct((half, span), F32),
            in_specs=[SMEM, VMEM, HBM, VMEM],
            out_specs=VMEM,
            scratch_shapes=scratch,
            compiler_params=PARAMS,
        )(place, full, in_hbm(contrasted), time)
        grad = keep + got.astype(F32)
        grad = grad[: half // 2] + hop_x(grad[half // 2 :].astype(BF16), 0).astype(F32)
        mine_sum = grad.astype(BF16)
        got = hop_x(mine_sum, 1)
        swapped = jnp.concatenate([got[half // 4 :], got[: half // 4]])
        mine_sum = (mine_sum.astype(F32) + swapped.astype(F32)).astype(BF16)
        grad = mine_sum.astype(F32) + hop(mine_sum, "pix", 2).astype(F32)
        quad = soften(quad.astype(F32) + coef_temporal * grad, limit_temporal).astype(BF16)
        mine, other = gather_temporal(quad)

        def part_shapes(part):
            width = PARTS[part][1]
            return [jax.ShapeDtypeStruct((half, width), BF16), jax.ShapeDtypeStruct((half, width), F32)]

        widest = max(width for _, width, _ in PARTS)
        scratch = [
            pltpu.VMEM((rank, span), BF16),
            pltpu.VMEM((rank, rank), BF16),
            pltpu.VMEM((rank, widest), BF16),
            pltpu.VMEM((widest, span), BF16),
            COPIES,
        ]
        send, keep, time, gram = pl.pallas_call(
            spatial_first,
            out_shape=part_shapes(0)
            + [jax.ShapeDtypeStruct((rank, span), BF16), jax.ShapeDtypeStruct((rank, rank), BF16)],
            in_specs=[SMEM, HBM, HBM, ANY, ANY],
            out_specs=[VMEM] * 4,
            scratch_shapes=scratch,
            compiler_params=PARAMS,
        )(place, in_hbm(stored), in_hbm(contrasted), mine, other)
        grads = [(send, keep)]
        for part in (1, 2):
            grads.append(
                pl.pallas_call(
                    functools.partial(spatial_part, part),
                    out_shape=part_shapes(part),
                    in_specs=[SMEM, HBM, HBM, VMEM, VMEM],
                    out_specs=[VMEM] * 2,
                    scratch_shapes=scratch,
                    compiler_params=PARAMS,
                )(place, in_hbm(stored), in_hbm(contrasted), time, gram)
            )
        totals = [
            keep + hop(send, "tm", order[0]).astype(F32) for (send, keep), (_, _, order) in zip(grads, PARTS)
        ]
        totals = [
            total[: 2 * slab] + hop(total[2 * slab :].astype(BF16), "tm", order[1]).astype(F32)
            for total, (_, _, order) in zip(totals, PARTS)
        ]
        if turn < ROUNDS - 1:
            sums = []
            for total, (_, _, order) in zip(totals, PARTS):
                mine_sum = total.astype(BF16)
                got = hop(mine_sum, "tm", order[2])
                swapped = jnp.concatenate([got[slab:], got[:slab]])
                sums.append(mine_sum.astype(F32) + swapped.astype(F32))
            slabs = [
                soften(s.astype(F32) + coef * g, limit).astype(BF16)
                for s, g, coef, limit in zip(slabs, sums, coef_spatial, limit_spatial)
            ]
            pieces = first_gather(second_gather(slabs))
        else:
            sums = [
                total[:slab] + hop(total[slab:].astype(BF16), "tm", order[2]).astype(F32)
                for total, (_, _, order) in zip(totals, PARTS)
            ]
            shards = [
                soften(s[:slab].astype(F32) + coef[:slab] * g, limit[:slab]).astype(BF16)
                for s, g, coef, limit in zip(slabs, sums, coef_spatial, limit_spatial)
            ]
    temporal_out = jnp.where(yhi == 0, quad[:shard], quad[shard : 2 * shard])
    return jnp.concatenate(shards, 1), temporal_out


def solution(mesh):
    placed = (P("pix", "tm"), P(), P("tm", "pix"), P("pix", "tm"), P(), P(), P(), P())
    return jax.shard_map(
        per_device,
        mesh=mesh,
        in_specs=placed,
        out_specs=(P("tm", "pix"), P("pix", "tm")),
        check_vma=False,
    )
```

```python
import functools
import math

import jax
import jax.numpy as jnp
from jax import lax
from jax.experimental import pallas as pl
from jax.experimental.pallas import tpu as pltpu
from jax.sharding import PartitionSpec as P

HALO = 129
EDGE = 144
BLOCK = 256
NBR = 8
ROUNDS = 2
BF16 = jnp.bfloat16
F32 = jnp.float32

PARTS = ((0, 640, (3, 4, 1)), (640, 768, (4, 1, 3)), (1408, 640, (1, 3, 4)))
FRAME_PARTS = ((0, 384, (4, 12, 2)), (384, 256, (12, 2, 4)), (640, 384, (2, 4, 12)))
START_PARTS = ((0, 1024, (12, 4, 2)),)
LANES = 128
VMEM = pl.BlockSpec(memory_space=pltpu.VMEM)
SMEM = pl.BlockSpec(memory_space=pltpu.SMEM)
ANY = pl.BlockSpec(memory_space=pl.ANY)
HBM = pl.BlockSpec(memory_space=pltpu.HBM)
COPIES = pltpu.SemaphoreType.DMA((64,))
PARAMS = pltpu.CompilerParams(vmem_limit_bytes=20 * 1024 * 1024)


def hop(a, axis, mask):
    size = lax.axis_size(axis)
    return lax.ppermute(a, axis, [(i, i ^ mask) for i in range(size)])


def reach(order, position):
    first, second, third = order
    return first * (position // 4) ^ second * (position // 2 % 2) ^ third * (position % 2)


def soften(values, limit):
    return values - jnp.clip(values, -limit, limit)


def nn(a, b):
    return jnp.dot(a, b, preferred_element_type=F32)


def nt(a, b):
    return lax.dot_general(a, b, (((1,), (1,)), ((), ())), preferred_element_type=F32)


class Copies:
    def __init__(self, sems):
        self.sems = sems
        self.used = 0

    def start(self, source, target):
        copy = pltpu.make_async_copy(source, target, self.sems.at[self.used])
        self.used += 1
        copy.start()
        return copy


def stencil(offsets_ref, movie_ref, before_ref, after_ref, later_ref, out_ref, held_ref, made_ref, sems):
    del later_ref
    rows = movie_ref.shape[0]
    blocks = rows // BLOCK
    copies = Copies(sems)

    def block(b):
        return pl.ds(b * BLOCK, BLOCK)

    loads = [copies.start(movie_ref.at[block(b), :], held_ref.at[block(b), :]) for b in range(blocks)]

    def band(columns, base):
        step = (
            lax.broadcasted_iota(jnp.int32, (BLOCK, columns), 1)
            - lax.broadcasted_iota(jnp.int32, (BLOCK, columns), 0)
            + base
        )
        weight = jnp.where(step == 0, 1.0, 0.0).astype(F32)
        for k in range(NBR):
            weight = weight - jnp.where(step == offsets_ref[k], 1.0 / NBR, 0.0).astype(F32)
        return weight.astype(BF16)

    main = band(3 * BLOCK, -BLOCK)
    loads[0].wait()
    stores = []
    for b in range(blocks):
        if b + 1 < blocks:
            loads[b + 1].wait()
        low = max(b - 1, 0) * BLOCK
        high = min(b + 2, blocks) * BLOCK
        first = low - (b - 1) * BLOCK
        total = nn(main[:, first : first + high - low], held_ref[low:high, :])
        if b == 0:
            total += nn(band(EDGE, -EDGE), before_ref[...])
        if b == blocks - 1:
            total += nn(band(EDGE, BLOCK), after_ref[...])
        made_ref[b * BLOCK : (b + 1) * BLOCK, :] = total.astype(BF16)
        stores.append(copies.start(made_ref.at[block(b), :], out_ref.at[block(b), :]))
    for store in stores:
        store.wait()


def contrast(movie, before, after, offsets, later):
    return pl.pallas_call(
        stencil,
        out_shape=pltpu.HBM(movie.shape, BF16),
        in_specs=[SMEM, HBM, VMEM, VMEM, ANY],
        out_specs=HBM,
        scratch_shapes=[pltpu.VMEM(movie.shape, BF16), pltpu.VMEM(movie.shape, BF16), COPIES],
        compiler_params=PARAMS,
    )(offsets, in_hbm(movie), before, after, later)


def in_hbm(a):
    return pltpu.with_memory_space_constraint(a, pltpu.HBM)


def place_temporal(parts, pix, mine_ref, other_ref, time_ref):
    for begin, width, order in parts:
        columns = slice(begin, begin + width)
        for position in range(8):
            piece = slice(position * 32, position * 32 + 32)
            for from_ref, side in ((mine_ref, 0), (other_ref, 1)):
                row = pl.multiple_of((pix ^ side ^ reach(order, position)) * 32, 32)
                time_ref[pl.ds(row, 32), columns] = from_ref[piece, columns]


def temporal_block(pix, full_ref, held_ref, gram_ref, time_ref, grad_ref, send_ref, keep_ref, at, begin):
    columns = slice(at, at + BLOCK)
    grad_ref[...] = nn(full_ref[...], held_ref[...]) - nn(gram_ref[...], time_ref[:, columns])
    for low in range(0, BLOCK, LANES):
        order = [o for b, w, o in FRAME_PARTS if b <= at + low < b + w][0]
        lanes = slice(low, low + LANES)
        target = slice(at - begin + low, at - begin + low + LANES)
        for position in range(8):
            piece = slice(position * 32, position * 32 + 32)
            row = pl.multiple_of((pix ^ reach(order, position)) * 32, 32)
            keep_ref[piece, target] = grad_ref[pl.ds(row, 32), lanes]
            row = pl.multiple_of((pix ^ 1 ^ reach(order, position)) * 32, 32)
            send_ref[piece, target] = grad_ref[pl.ds(row, 32), lanes].astype(BF16)


def hold(contrasted_ref, held_ref, begin, width, copies):
    return [
        copies.start(contrasted_ref.at[:, pl.ds(begin + f, BLOCK)], held_ref.at[f // BLOCK])
        for f in range(0, width, BLOCK)
    ]


def temporal_first(
    parts, place_ref, a0, b0, a1, b1, a2, b2, contrasted_ref, mine_ref, other_ref,
    full_ref, time_ref, gram_ref, stored_ref, send_ref, keep_ref, grad_ref, held_ref, sems,
):
    tm, pix = place_ref[0], place_ref[1]
    copies = Copies(sems)
    width = send_ref.shape[1]
    blocks = hold(contrasted_ref, held_ref, 0, width, copies)
    for (begin, size, order), near, far in zip(PARTS, (a0, a1, a2), (b0, b1, b2)):
        for position in range(8):
            row = pl.multiple_of((tm ^ reach(order, position)) * 64, 64)
            piece = near if position < 4 else far
            full_ref[pl.ds(row, 64), begin : begin + size] = piece[pl.ds(position % 4 * 64, 64), :]
    store = copies.start(full_ref, stored_ref)
    place_temporal(parts, pix, mine_ref, other_ref, time_ref)
    gram_ref[...] = (nt(full_ref[...], full_ref[...]) * (1.0 / math.sqrt(full_ref.shape[0]))).astype(BF16)
    for f in range(0, width, BLOCK):
        blocks[f // BLOCK].wait()
        temporal_block(
            pix, full_ref, held_ref.at[f // BLOCK], gram_ref, time_ref, grad_ref, send_ref, keep_ref, f, 0
        )
    store.wait()


def temporal_second(
    place_ref, full_ref, time_ref, gram_ref, contrasted_ref, send_ref, keep_ref, grad_ref, held_ref, sems
):
    pix = place_ref[1]
    width = send_ref.shape[1]
    begin = time_ref.shape[1] - width
    blocks = hold(contrasted_ref, held_ref, begin, width, Copies(sems))
    for f in range(0, width, BLOCK):
        blocks[f // BLOCK].wait()
        temporal_block(
            pix, full_ref, held_ref.at[f // BLOCK], gram_ref, time_ref, grad_ref, send_ref, keep_ref,
            begin + f, begin,
        )


def spatial_loads(part, full_ref, contrasted_ref, strip_ref, held_ref, copies):
    begin, width, _ = PARTS[part]
    return [
        copies.start(contrasted_ref.at[pl.ds(begin, width), :], held_ref.at[pl.ds(0, width), :]),
        copies.start(full_ref.at[:, pl.ds(begin, width)], strip_ref.at[:, pl.ds(0, width)]),
    ]


def spatial_blocks(
    part, place_ref, time_ref, gram_ref, send_ref, keep_ref, grad_ref, strip_ref, held_ref, loads
):
    _, width, order = PARTS[part]
    tm = place_ref[0]
    for load in loads:
        load.wait()
    for low in range(0, width, BLOCK):
        size = min(BLOCK, width - low)
        pixels = slice(low, low + size)
        grad_ref[:, :size] = nt(time_ref[...], held_ref[pixels, :]) - nn(gram_ref[...], strip_ref[:, pixels])
        for position in range(8):
            row = pl.multiple_of((tm ^ reach(order, position)) * 64, 64)
            piece = grad_ref[pl.ds(row, 64), :size]
            if position < 4:
                keep_ref[position * 64 : position * 64 + 64, pixels] = piece
            else:
                send_ref[position * 64 - 256 : position * 64 - 192, pixels] = piece.astype(BF16)


def spatial_part(
    part, place_ref, full_ref, contrasted_ref, time_ref, gram_ref,
    send_ref, keep_ref, grad_ref, strip_ref, held_ref, sems,
):
    loads = spatial_loads(part, full_ref, contrasted_ref, strip_ref, held_ref, Copies(sems))
    spatial_blocks(
        part, place_ref, time_ref, gram_ref, send_ref, keep_ref, grad_ref, strip_ref, held_ref, loads
    )


def spatial_first(
    place_ref, full_ref, contrasted_ref, mine_ref, other_ref,
    send_ref, keep_ref, time_ref, gram_ref, grad_ref, strip_ref, held_ref, sems,
):
    loads = spatial_loads(0, full_ref, contrasted_ref, strip_ref, held_ref, Copies(sems))
    place_temporal(FRAME_PARTS, place_ref[1], mine_ref, other_ref, time_ref)
    gram_ref[...] = (nt(time_ref[...], time_ref[...]) * (1.0 / math.sqrt(time_ref.shape[0]))).astype(BF16)
    spatial_blocks(
        0, place_ref, time_ref, gram_ref, send_ref, keep_ref, grad_ref, strip_ref, held_ref, loads
    )


def per_device(
    movie, offsets, spatial, temporal, step_spatial, step_temporal, thresh_spatial, thresh_temporal
):
    slab, strip = spatial.shape
    shard, span = temporal.shape
    rank = slab * lax.axis_size("tm")
    pixels = strip * lax.axis_size("pix")
    frames = span * lax.axis_size("tm")
    pix = lax.axis_index("pix")
    tm = lax.axis_index("tm")
    place = jnp.stack([tm, pix]).astype(jnp.int32)

    def own(a, index, rows):
        return lax.dynamic_slice_in_dim(a, index * rows, rows, 0)[:, None]

    def own_temporal(a, order):
        return jnp.concatenate([own(a, pix ^ reach(order, position), shard) for position in range(4)])

    def own_spatial(a, mask):
        return jnp.concatenate([own(a, tm, slab), own(a, tm ^ mask, slab)])

    all_temporal = step_temporal * (math.sqrt(rank) / pixels)
    coef_temporal = [own_temporal(all_temporal, order) for _, _, order in FRAME_PARTS]
    limit_temporal = [own_temporal(thresh_temporal, order) for _, _, order in FRAME_PARTS]
    all_spatial = step_spatial * (math.sqrt(rank) / frames)
    coef_spatial = [own_spatial(all_spatial, order[2]) for _, _, order in PARTS]
    limit_spatial = [own_spatial(thresh_spatial, order[2]) for _, _, order in PARTS]

    def second_gather(slabs):
        return [jnp.concatenate([s, hop(s, "tm", order[1])]) for s, (_, _, order) in zip(slabs, PARTS)]

    def first_gather(near):
        return [(a, hop(a, "tm", order[0])) for a, (_, _, order) in zip(near, PARTS)]

    shards = [spatial[:, begin : begin + width] for begin, width, _ in PARTS]
    size = lax.axis_size("pix")
    up = [(i, i + 1) for i in range(size - 1)]
    down = [(j, i) for i, j in up]
    before = lax.ppermute(movie[movie.shape[0] - EDGE :], "pix", up)
    after = lax.ppermute(movie[:EDGE], "pix", down)
    slabs = [jnp.concatenate([s, hop(s, "tm", order[2])]) for s, (_, _, order) in zip(shards, PARTS)]
    near = second_gather(slabs)
    near, before, after = lax.optimization_barrier((near, before, after))
    pieces = first_gather(near)
    contrasted = contrast(movie, before, after, offsets, slabs[1])
    mine = temporal
    start = START_PARTS[0][2]
    for mask in reversed(start):
        mine = jnp.concatenate([mine, hop(mine, "pix", mask)])
    other = hop(mine, "pix", 1)
    place_of = {reach(start, position): position for position in range(8)}
    quads = []
    for begin, width, order in FRAME_PARTS:
        rows = [place_of[reach(order, position)] * shard for position in range(4)]
        quads.append(jnp.concatenate([mine[row : row + shard, begin : begin + width] for row in rows]))

    half = rank // 2
    for turn in range(ROUNDS):
        wide = span // 2
        scratch = [
            pltpu.VMEM((rank, BLOCK), F32),
            pltpu.VMEM((wide // BLOCK, strip, BLOCK), BF16),
            COPIES,
        ]
        halves = [jax.ShapeDtypeStruct((half, wide), BF16), jax.ShapeDtypeStruct((half, wide), F32)]
        full, time, gram, stored, send, keep = pl.pallas_call(
            functools.partial(temporal_first, START_PARTS if turn == 0 else FRAME_PARTS),
            out_shape=[
                jax.ShapeDtypeStruct((rank, strip), BF16),
                jax.ShapeDtypeStruct((rank, span), BF16),
                jax.ShapeDtypeStruct((rank, rank), BF16),
                pltpu.HBM((rank, strip), BF16),
            ]
            + halves,
            in_specs=[SMEM] + [VMEM] * 6 + [HBM, VMEM, VMEM],
            out_specs=[VMEM, VMEM, VMEM, HBM, VMEM, VMEM],
            scratch_shapes=scratch,
            compiler_params=PARAMS,
        )(place, *[piece for both in pieces for piece in both], in_hbm(contrasted), mine, other)
        totals = [keep + hop(send, "pix", 1).astype(F32)]
        send, keep = pl.pallas_call(
            temporal_second,
            out_shape=halves,
            in_specs=[SMEM, VMEM, VMEM, VMEM, HBM],
            out_specs=[VMEM, VMEM],
            scratch_shapes=scratch,
            compiler_params=PARAMS,
        )(place, full, time, gram, in_hbm(contrasted))
        totals.append(keep + hop(send, "pix", 1).astype(F32))
        total = jnp.concatenate(totals, 1)
        totals = [total[:, begin : begin + width] for begin, width, _ in FRAME_PARTS]
        totals = [
            g[: half // 2] + hop(g[half // 2 :].astype(BF16), "pix", order[0]).astype(F32)
            for g, (_, _, order) in zip(totals, FRAME_PARTS)
        ]
        for stage, size in ((1, 2 * shard), (2, shard)):
            grads = [g.astype(BF16) for g in totals]
            totals = []
            for g, (_, _, order) in zip(grads, FRAME_PARTS):
                got = hop(g, "pix", order[stage])
                rows = [got[(i ^ 1) * size : (i ^ 1) * size + size] for i in range(4 * shard // size)]
                totals.append(g.astype(F32) + jnp.concatenate(rows).astype(F32))
        quads = [
            soften(q.astype(F32) + coef * g, limit).astype(BF16)
            for q, g, coef, limit in zip(quads, totals, coef_temporal, limit_temporal)
        ]
        mine = jnp.concatenate(
            [
                jnp.concatenate([q, hop(q, "pix", order[0])])
                for q, (_, _, order) in zip(quads, FRAME_PARTS)
            ],
            1,
        )
        other = hop(mine, "pix", 1)

        def part_shapes(part):
            width = PARTS[part][1]
            return [jax.ShapeDtypeStruct((half, width), BF16), jax.ShapeDtypeStruct((half, width), F32)]

        widest = max(width for _, width, _ in PARTS)
        scratch = [
            pltpu.VMEM((rank, BLOCK), F32),
            pltpu.VMEM((rank, widest), BF16),
            pltpu.VMEM((widest, span), BF16),
            COPIES,
        ]
        send, keep, time, gram = pl.pallas_call(
            spatial_first,
            out_shape=part_shapes(0)
            + [jax.ShapeDtypeStruct((rank, span), BF16), jax.ShapeDtypeStruct((rank, rank), BF16)],
            in_specs=[SMEM, HBM, HBM, VMEM, VMEM],
            out_specs=[VMEM] * 4,
            scratch_shapes=scratch,
            compiler_params=PARAMS,
        )(place, in_hbm(stored), in_hbm(contrasted), mine, other)
        grads = [(send, keep)]
        for part in (1, 2):
            grads.append(
                pl.pallas_call(
                    functools.partial(spatial_part, part),
                    out_shape=part_shapes(part),
                    in_specs=[SMEM, HBM, HBM, VMEM, VMEM],
                    out_specs=[VMEM] * 2,
                    scratch_shapes=scratch,
                    compiler_params=PARAMS,
                )(place, in_hbm(stored), in_hbm(contrasted), time, gram)
            )
        totals = [
            keep + hop(send, "tm", order[0]).astype(F32) for (send, keep), (_, _, order) in zip(grads, PARTS)
        ]
        totals = [
            total[: 2 * slab] + hop(total[2 * slab :].astype(BF16), "tm", order[1]).astype(F32)
            for total, (_, _, order) in zip(totals, PARTS)
        ]
        if turn < ROUNDS - 1:
            sums = []
            for total, (_, _, order) in zip(totals, PARTS):
                mine_sum = total.astype(BF16)
                got = hop(mine_sum, "tm", order[2])
                swapped = jnp.concatenate([got[slab:], got[:slab]])
                sums.append(mine_sum.astype(F32) + swapped.astype(F32))
            slabs = [
                soften(s.astype(F32) + coef * g, limit).astype(BF16)
                for s, g, coef, limit in zip(slabs, sums, coef_spatial, limit_spatial)
            ]
            pieces = first_gather(second_gather(slabs))
        else:
            sums = [
                total[:slab] + hop(total[slab:].astype(BF16), "tm", order[2]).astype(F32)
                for total, (_, _, order) in zip(totals, PARTS)
            ]
            shards = [
                soften(s[:slab].astype(F32) + coef[:slab] * g, limit[:slab]).astype(BF16)
                for s, g, coef, limit in zip(slabs, sums, coef_spatial, limit_spatial)
            ]
    temporal_out = jnp.concatenate([q[:shard] for q in quads], 1)
    return jnp.concatenate(shards, 1), temporal_out


def solution(mesh):
    placed = (P("pix", "tm"), P(), P("tm", "pix"), P("pix", "tm"), P(), P(), P(), P())
    return jax.shard_map(
        per_device,
        mesh=mesh,
        in_specs=placed,
        out_specs=(P("tm", "pix"), P("pix", "tm")),
        check_vma=False,
    )
```

```python
import functools
import math

import jax
import jax.numpy as jnp
from jax import lax
from jax.experimental import pallas as pl
from jax.experimental.pallas import tpu as pltpu
from jax.sharding import PartitionSpec as P

HALO = 129
EDGE = 144
BLOCK = 256
NBR = 8
ROUNDS = 2
BF16 = jnp.bfloat16
F32 = jnp.float32

PARTS = ((0, 640, (3, 4, 1)), (640, 768, (4, 1, 3)), (1408, 640, (1, 3, 4)))
FRAME_PARTS = ((0, 512, (4, 12, 2)), (512, 512, (12, 2, 4)))
START = (12, 4, 2)
VMEM = pl.BlockSpec(memory_space=pltpu.VMEM)
SMEM = pl.BlockSpec(memory_space=pltpu.SMEM)
HBM = pl.BlockSpec(memory_space=pltpu.HBM)
COPIES = pltpu.SemaphoreType.DMA((16,))
PARAMS = pltpu.CompilerParams(vmem_limit_bytes=12 * 1024 * 1024)


def hop(a, axis, mask):
    size = lax.axis_size(axis)
    return lax.ppermute(a, axis, [(i, i ^ mask) for i in range(size)])


def reach(order, position):
    first, second, third = order
    return first * (position // 4) ^ second * (position // 2 % 2) ^ third * (position % 2)


def soften(values, limit):
    return values - jnp.clip(values, -limit, limit)


def nn(a, b):
    return jnp.dot(a, b, preferred_element_type=F32)


def nt(a, b):
    return lax.dot_general(a, b, (((1,), (1,)), ((), ())), preferred_element_type=F32)


class Copies:
    def __init__(self, sems):
        self.sems = sems
        self.used = 0

    def start(self, source, target):
        copy = pltpu.make_async_copy(source, target, self.sems.at[self.used])
        self.used += 1
        copy.start()
        return copy


def stencil(offsets_ref, movie_ref, before_ref, after_ref, out_ref, held_ref, sems):
    rows = movie_ref.shape[0]
    blocks = rows // BLOCK
    copies = Copies(sems)

    def block(b):
        return pl.ds(b * BLOCK, BLOCK)

    loads = [copies.start(movie_ref.at[block(b), :], held_ref.at[block(b), :]) for b in range(blocks)]

    def band(columns, base):
        step = (
            lax.broadcasted_iota(jnp.int32, (BLOCK, columns), 1)
            - lax.broadcasted_iota(jnp.int32, (BLOCK, columns), 0)
            + base
        )
        weight = jnp.where(step == 0, 1.0, 0.0).astype(F32)
        for k in range(NBR):
            weight = weight - jnp.where(step == offsets_ref[k], 1.0 / NBR, 0.0).astype(F32)
        return weight.astype(BF16)

    main = band(3 * BLOCK, -BLOCK)
    loads[0].wait()
    for b in range(blocks):
        if b + 1 < blocks:
            loads[b + 1].wait()
        low = max(b - 1, 0) * BLOCK
        high = min(b + 2, blocks) * BLOCK
        first = low - (b - 1) * BLOCK
        total = nn(main[:, first : first + high - low], held_ref[low:high, :])
        if b == 0:
            total += nn(band(EDGE, -EDGE), before_ref[...])
        if b == blocks - 1:
            total += nn(band(EDGE, BLOCK), after_ref[...])
        out_ref[b * BLOCK : (b + 1) * BLOCK, :] = total.astype(BF16)


def contrast(movie, before, after, offsets):
    return pl.pallas_call(
        stencil,
        out_shape=pltpu.VMEM(movie.shape, BF16),
        in_specs=[SMEM, HBM, VMEM, VMEM],
        out_specs=VMEM,
        scratch_shapes=[pltpu.VMEM(movie.shape, BF16), COPIES],
        compiler_params=PARAMS,
    )(offsets, pltpu.with_memory_space_constraint(movie, pltpu.HBM), before, after)


def pin(a):
    return pltpu.with_memory_space_constraint(a, pltpu.VMEM)


def place_temporal(begin, order, pix, mine_ref, other_ref, time_ref):
    columns = slice(begin, begin + mine_ref.shape[1])
    for position in range(8):
        piece = slice(position * 32, position * 32 + 32)
        for from_ref, side in ((mine_ref, 0), (other_ref, 1)):
            row = pl.multiple_of((pix ^ side ^ reach(order, position)) * 32, 32)
            time_ref[pl.ds(row, 32), columns] = from_ref[piece, :]


def temporal_blocks(part, pix, full_ref, contrasted_ref, gram_ref, time_ref, send_ref, keep_ref, grad_ref):
    begin, width, order = FRAME_PARTS[part]
    for low in range(0, width, BLOCK):
        columns = slice(begin + low, begin + low + BLOCK)
        target = slice(low, low + BLOCK)
        grad_ref[...] = nn(full_ref[...], contrasted_ref[:, columns]) - nn(gram_ref[...], time_ref[:, columns])
        for position in range(8):
            piece = slice(position * 32, position * 32 + 32)
            row = pl.multiple_of((pix ^ reach(order, position)) * 32, 32)
            keep_ref[piece, target] = grad_ref[pl.ds(row, 32), :]
            row = pl.multiple_of((pix ^ 1 ^ reach(order, position)) * 32, 32)
            send_ref[piece, target] = grad_ref[pl.ds(row, 32), :].astype(BF16)


def make_full(tm, pieces, full_ref):
    for (begin, size, order), near, far in zip(PARTS, pieces[0::2], pieces[1::2]):
        for position in range(8):
            row = pl.multiple_of((tm ^ reach(order, position)) * 64, 64)
            piece = near if position < 4 else far
            full_ref[pl.ds(row, 64), begin : begin + size] = piece[pl.ds(position % 4 * 64, 64), :]


def make_gram(factor_ref, gram_ref):
    gram_ref[...] = (nt(factor_ref[...], factor_ref[...]) * (1.0 / math.sqrt(factor_ref.shape[0]))).astype(BF16)


def temporal_start(
    place_ref, a0, b0, a1, b1, a2, b2, contrasted_ref, mine_ref, other_ref, rows_ref,
    full_ref, gram_ref, send_ref, keep_ref, time_ref, quad0_ref, quad1_ref, table_ref, grad_ref,
):
    table_ref[...] = rows_ref[...].T
    tm, pix = place_ref[0], place_ref[1]
    make_full(tm, (a0, b0, a1, b1, a2, b2), full_ref)
    place_temporal(0, START, pix, mine_ref, other_ref, time_ref)
    make_gram(full_ref, gram_ref)
    temporal_blocks(0, pix, full_ref, contrasted_ref, gram_ref, time_ref, send_ref, keep_ref, grad_ref)
    for (begin, width, order), quad_ref in zip(FRAME_PARTS, (quad0_ref, quad1_ref)):
        for position in range(4):
            row = pl.multiple_of((pix ^ reach(order, position)) * 32, 32)
            quad_ref[position * 32 : position * 32 + 32, :] = time_ref[pl.ds(row, 32), begin : begin + width]


def temporal_first(
    place_ref, a0, b0, a1, b1, a2, b2, contrasted_ref, time_ref,
    full_ref, gram_ref, send_ref, keep_ref, grad_ref,
):
    make_full(place_ref[0], (a0, b0, a1, b1, a2, b2), full_ref)
    make_gram(full_ref, gram_ref)
    temporal_blocks(
        0, place_ref[1], full_ref, contrasted_ref, gram_ref, time_ref, send_ref, keep_ref, grad_ref
    )


def temporal_second(
    place_ref, full_ref, gram_ref, contrasted_ref, time_ref, send_ref, keep_ref, grad_ref
):
    temporal_blocks(
        1, place_ref[1], full_ref, contrasted_ref, gram_ref, time_ref, send_ref, keep_ref, grad_ref
    )


def temporal_update(part, place_ref, table_ref, quad_ref, sum_ref, got_ref, out_ref):
    order = FRAME_PARTS[part][2]
    for position in range(4):
        piece = slice(position * 32, position * 32 + 32)
        swapped = slice((position ^ 1) * 32, (position ^ 1) * 32 + 32)
        rows = pl.ds(pl.multiple_of((place_ref[1] ^ reach(order, position)) * 32, 32), 32)
        coef, limit = table_ref[rows, 0:1], table_ref[rows, 1:2]
        grad = sum_ref[piece, :].astype(F32) + got_ref[swapped, :].astype(F32)
        out_ref[piece, :] = soften(quad_ref[piece, :].astype(F32) + coef * grad, limit).astype(BF16)


def spatial_update(part, place_ref, table_ref, slab_ref, sum_ref, got_ref, out_ref):
    order = PARTS[part][2]
    for position in range(out_ref.shape[0] // 64):
        piece = slice(position * 64, position * 64 + 64)
        swapped = slice(0, 64) if got_ref.shape[0] == 64 else slice((position ^ 1) * 64, (position ^ 1) * 64 + 64)
        rows = pl.ds(pl.multiple_of((place_ref[0] ^ reach(order, position)) * 64, 64), 64)
        coef, limit = table_ref[rows, 2:3], table_ref[rows, 3:4]
        grad = sum_ref[piece, :].astype(F32) + got_ref[swapped, :].astype(F32)
        out_ref[piece, :] = soften(slab_ref[piece, :].astype(F32) + coef * grad, limit).astype(BF16)


def spatial_blocks(part, tm, full_ref, contrasted_ref, time_ref, gram_ref, send_ref, keep_ref, grad_ref):
    begin, width, order = PARTS[part]
    for low in range(0, width, BLOCK):
        size = min(BLOCK, width - low)
        pixels = slice(begin + low, begin + low + size)
        target = slice(low, low + size)
        grad_ref[:, :size] = nt(time_ref[...], contrasted_ref[pixels, :]) - nn(gram_ref[...], full_ref[:, pixels])
        for position in range(8):
            row = pl.multiple_of((tm ^ reach(order, position)) * 64, 64)
            piece = grad_ref[pl.ds(row, 64), :size]
            if position < 4:
                keep_ref[position * 64 : position * 64 + 64, target] = piece
            else:
                send_ref[position * 64 - 256 : position * 64 - 192, target] = piece.astype(BF16)


def spatial_first(
    place_ref, full_ref, contrasted_ref, mine0_ref, other0_ref, mine1_ref, other1_ref,
    time_ref, gram_ref, send_ref, keep_ref, grad_ref,
):
    tm, pix = place_ref[0], place_ref[1]
    for (begin, _, order), mine_ref, other_ref in zip(
        FRAME_PARTS, (mine0_ref, mine1_ref), (other0_ref, other1_ref)
    ):
        place_temporal(begin, order, pix, mine_ref, other_ref, time_ref)
    make_gram(time_ref, gram_ref)
    spatial_blocks(0, tm, full_ref, contrasted_ref, time_ref, gram_ref, send_ref, keep_ref, grad_ref)


def spatial_next(
    part, place_ref, full_ref, contrasted_ref, time_ref, gram_ref, send_ref, keep_ref, grad_ref
):
    spatial_blocks(
        part, place_ref[0], full_ref, contrasted_ref, time_ref, gram_ref, send_ref, keep_ref, grad_ref
    )


def call(kernel, place, operands, outs, scratch=()):
    return pl.pallas_call(
        kernel,
        out_shape=[pltpu.VMEM(shape, dtype) for shape, dtype in outs],
        in_specs=[SMEM] + [VMEM] * len(operands),
        out_specs=[VMEM] * len(outs),
        scratch_shapes=scratch,
        compiler_params=PARAMS,
    )(place, *[pin(operand) for operand in operands])


def per_device(
    movie, offsets, spatial, temporal, step_spatial, step_temporal, thresh_spatial, thresh_temporal
):
    slab, strip = spatial.shape
    shard, span = temporal.shape
    rank = slab * lax.axis_size("tm")
    pixels = strip * lax.axis_size("pix")
    frames = span * lax.axis_size("tm")
    pix = lax.axis_index("pix")
    tm = lax.axis_index("tm")
    place = jnp.stack([tm, pix]).astype(jnp.int32)

    table = jnp.stack(
        [
            step_temporal * (math.sqrt(rank) / pixels),
            thresh_temporal,
            step_spatial * (math.sqrt(rank) / frames),
            thresh_spatial,
        ]
        * 2
    )
    spatial, place, table = lax.optimization_barrier((spatial, place, table))

    def second_gather(slabs):
        return [jnp.concatenate([s, hop(s, "tm", order[1])]) for s, (_, _, order) in zip(slabs, PARTS)]

    def first_gather(near):
        return [(a, hop(a, "tm", order[0])) for a, (_, _, order) in zip(near, PARTS)]

    slabs = [spatial[:, begin : begin + width] for begin, width, _ in PARTS]
    slabs = [jnp.concatenate([s, hop(s, "tm", order[2])]) for s, (_, _, order) in zip(slabs, PARTS)]
    mine = jnp.concatenate([temporal, hop(temporal, "pix", START[2])])
    slabs, mine, low_edge, high_edge = lax.optimization_barrier(
        (slabs, mine, movie[:EDGE], movie[movie.shape[0] - EDGE :])
    )
    near = second_gather(slabs)
    size = lax.axis_size("pix")
    up = [(i, i + 1) for i in range(size - 1)]
    down = [(j, i) for i, j in up]
    before = lax.ppermute(high_edge, "pix", up)
    after = lax.ppermute(low_edge, "pix", down)
    for mask in (START[1], START[0]):
        mine = jnp.concatenate([mine, hop(mine, "pix", mask)])
    other = hop(mine, "pix", 1)
    near, before, after = lax.optimization_barrier((near, before, after))
    pieces = first_gather(near)
    contrasted = contrast(movie, before, after, offsets)

    half = rank // 2
    block = [pltpu.VMEM((rank, BLOCK), F32)]

    def both(width):
        return [((half, width), BF16), ((half, width), F32)]

    for turn in range(ROUNDS):
        flat = [piece for pair in pieces for piece in pair]
        outs = [((rank, strip), BF16), ((rank, rank), BF16)] + both(FRAME_PARTS[0][1])
        if turn == 0:
            outs += [((rank, span), BF16)] + [((half // 2, width), BF16) for _, width, _ in FRAME_PARTS]
            outs += [((rank, table.shape[0]), F32)]
            full, gram, send, keep, time, *quads, table = call(
                temporal_start, place, flat + [contrasted, mine, other, table], outs, block
            )
        else:
            full, gram, send, keep = call(temporal_first, place, flat + [contrasted, time], outs, block)
        grads = [(send, keep)]
        grads.append(
            call(temporal_second, place, [full, gram, contrasted, time], both(FRAME_PARTS[1][1]), block)
        )
        totals = [keep + hop(send, "pix", 1).astype(F32) for send, keep in grads]
        totals = [
            g[: half // 2] + hop(g[half // 2 :].astype(BF16), "pix", order[0]).astype(F32)
            for g, (_, _, order) in zip(totals, FRAME_PARTS)
        ]
        sums = []
        for g, (_, _, order) in zip(totals, FRAME_PARTS):
            g = g.astype(BF16)
            got = hop(g, "pix", order[1])
            got = jnp.concatenate([got[2 * shard :], got[: 2 * shard]])
            sums.append((g.astype(F32) + got.astype(F32)).astype(BF16))
        gots = [hop(g, "pix", order[2]) for g, (_, _, order) in zip(sums, FRAME_PARTS)]
        quads = [
            call(functools.partial(temporal_update, part), place, [table, q, g, got], [(q.shape, BF16)])[0]
            for part, (q, g, got) in enumerate(zip(quads, sums, gots))
        ]
        ends = []
        for q, (_, _, order) in zip(quads, FRAME_PARTS):
            mine = jnp.concatenate([q, hop(q, "pix", order[0])])
            ends += [mine, hop(mine, "pix", 1)]
        time, gram, send, keep = call(
            spatial_first,
            place,
            [full, contrasted] + ends,
            [((rank, span), BF16), ((rank, rank), BF16)] + both(PARTS[0][1]),
            block,
        )
        grads = [(send, keep)]
        for part in (1, 2):
            grads.append(
                call(
                    functools.partial(spatial_next, part),
                    place,
                    [full, contrasted, time, gram],
                    both(PARTS[part][1]),
                    block,
                )
            )
        totals = [
            keep + hop(send, "tm", order[0]).astype(F32) for (send, keep), (_, _, order) in zip(grads, PARTS)
        ]
        totals = [
            total[: 2 * slab] + hop(total[2 * slab :].astype(BF16), "tm", order[1]).astype(F32)
            for total, (_, _, order) in zip(totals, PARTS)
        ]
        last = turn == ROUNDS - 1
        if last:
            sums = [total[:slab] for total in totals]
            gots = [
                hop(total[slab:].astype(BF16), "tm", order[2]) for total, (_, _, order) in zip(totals, PARTS)
            ]
        else:
            sums = [total.astype(BF16) for total in totals]
            gots = [hop(total, "tm", order[2]) for total, (_, _, order) in zip(sums, PARTS)]
        slabs = [
            call(functools.partial(spatial_update, part), place, [table, s, g, got], [(g.shape, BF16)])[0]
            for part, (s, g, got) in enumerate(zip(slabs, sums, gots))
        ]
        if not last:
            pieces = first_gather(second_gather(slabs))
    return jnp.concatenate(slabs, 1), jnp.concatenate([q[:shard] for q in quads], 1)


def solution(mesh):
    placed = (P("pix", "tm"), P(), P("tm", "pix"), P("pix", "tm"), P(), P(), P(), P())
    return jax.shard_map(
        per_device,
        mesh=mesh,
        in_specs=placed,
        out_specs=(P("tm", "pix"), P("pix", "tm")),
        check_vma=False,
    )
```

```python
import functools
import math

import jax
import jax.numpy as jnp
from jax import lax
from jax.experimental import pallas as pl
from jax.experimental.pallas import tpu as pltpu
from jax.sharding import PartitionSpec as P

HALO = 129
EDGE = 144
BLOCK = 256
NBR = 8
ROUNDS = 2
BF16 = jnp.bfloat16
F32 = jnp.float32

PARTS = ((0, 768, (3, 4, 1)), (768, 640, (4, 1, 3)), (1408, 640, (1, 3, 4)))
FRAME_PARTS = ((0, 512, (4, 12, 2)), (512, 512, (12, 2, 4)))
START = (12, 4, 2)
LANES = 128
VMEM = pl.BlockSpec(memory_space=pltpu.VMEM)
SMEM = pl.BlockSpec(memory_space=pltpu.SMEM)
HBM = pl.BlockSpec(memory_space=pltpu.HBM)
COPIES = pltpu.SemaphoreType.DMA((16,))
PARAMS = pltpu.CompilerParams(vmem_limit_bytes=12 * 1024 * 1024)


def hop(a, axis, mask):
    size = lax.axis_size(axis)
    return lax.ppermute(a, axis, [(i, i ^ mask) for i in range(size)])


def reach(order, position):
    first, second, third = order
    return first * (position // 4) ^ second * (position // 2 % 2) ^ third * (position % 2)


def soften(values, limit):
    return values - jnp.clip(values, -limit, limit)


def nn(a, b):
    return jnp.dot(a, b, preferred_element_type=F32)


def nt(a, b):
    return lax.dot_general(a, b, (((1,), (1,)), ((), ())), preferred_element_type=F32)


class Copies:
    def __init__(self, sems):
        self.sems = sems
        self.used = 0

    def start(self, source, target):
        copy = pltpu.make_async_copy(source, target, self.sems.at[self.used])
        self.used += 1
        copy.start()
        return copy


def band(offsets_ref, columns, base, inside=None):
    step = (
        lax.broadcasted_iota(jnp.int32, (BLOCK, columns), 1)
        - lax.broadcasted_iota(jnp.int32, (BLOCK, columns), 0)
        + base
    )
    weight = jnp.where(step == 0, 1.0, 0.0).astype(F32)
    for k in range(NBR):
        weight = weight - jnp.where(step == offsets_ref[k], 1.0 / NBR, 0.0).astype(F32)
    if inside is not None:
        weight = jnp.where(inside, weight, 0.0)
    return weight.astype(BF16)


def stencil_blocks(offsets_ref, movie_ref, edge_ref, out_ref, held_ref, sems, lower, inside):
    half = movie_ref.shape[0] // 2
    count = half // BLOCK
    start = 0 if lower else half - BLOCK
    copies = Copies(sems)
    loads = [
        copies.start(
            movie_ref.at[pl.ds(start + b * BLOCK, BLOCK), :], held_ref.at[pl.ds(b * BLOCK, BLOCK), :]
        )
        for b in range(count + 1)
    ]
    main = band(offsets_ref, 3 * BLOCK, -BLOCK)
    loads[0].wait()
    loads[1].wait()
    for b in range(count):
        middle = b if lower else b + 1
        if 1 < middle + 1 <= count:
            loads[middle + 1].wait()
        low = max(middle - 1, 0)
        high = min(middle + 2, count + 1)
        first = (low - middle + 1) * BLOCK
        total = nn(main[:, first : first + (high - low) * BLOCK], held_ref[low * BLOCK : high * BLOCK, :])
        if lower and b == 0:
            total += nn(band(offsets_ref, EDGE, -EDGE, inside), edge_ref[...])
        if not lower and b == count - 1:
            total += nn(band(offsets_ref, EDGE, BLOCK, inside), edge_ref[...])
        row = (0 if lower else half) + b * BLOCK
        out_ref[row : row + BLOCK, :] = total.astype(BF16)


def stencil_lower(place_ref, offsets_ref, movie_ref, edge_ref, out_ref, held_ref, sems):
    stencil_blocks(offsets_ref, movie_ref, edge_ref, out_ref, held_ref, sems, True, place_ref[1] > 0)


def stencil_upper(strips, place_ref, offsets_ref, movie_ref, edge_ref, made_ref, out_ref, held_ref, sems):
    del made_ref
    stencil_blocks(
        offsets_ref, movie_ref, edge_ref, out_ref, held_ref, sems, False, place_ref[1] < strips - 1
    )


def contrast(kernel, place, offsets, movie, edge, made=()):
    rows, span = movie.shape
    return pl.pallas_call(
        kernel,
        out_shape=pltpu.VMEM(movie.shape, BF16),
        in_specs=[SMEM, SMEM, HBM] + [VMEM] * (1 + len(made)),
        out_specs=VMEM,
        scratch_shapes=[pltpu.VMEM((rows // 2 + BLOCK, span), BF16), COPIES],
        input_output_aliases={4: 0} if made else {},
        compiler_params=PARAMS,
    )(place, offsets, pltpu.with_memory_space_constraint(movie, pltpu.HBM), pin(edge), *[pin(m) for m in made])


def pin(a):
    return pltpu.with_memory_space_constraint(a, pltpu.VMEM)


def place_temporal(begin, order, pix, mine_ref, other_ref, time_ref):
    columns = slice(begin, begin + mine_ref.shape[1])
    for position in range(8):
        piece = slice(position * 32, position * 32 + 32)
        for from_ref, side in ((mine_ref, 0), (other_ref, 1)):
            row = pl.multiple_of((pix ^ side ^ reach(order, position)) * 32, 32)
            time_ref[pl.ds(row, 32), columns] = from_ref[piece, :]


def temporal_blocks(part, pix, full_ref, contrasted_ref, gram_ref, time_ref, send_ref, keep_ref, grad_ref):
    begin, width, order = FRAME_PARTS[part]
    for low in range(0, width, BLOCK):
        columns = slice(begin + low, begin + low + BLOCK)
        target = slice(low, low + BLOCK)
        grad_ref[...] = nn(full_ref[...], contrasted_ref[:, columns]) - nn(gram_ref[...], time_ref[:, columns])
        for position in range(8):
            piece = slice(position * 32, position * 32 + 32)
            row = pl.multiple_of((pix ^ reach(order, position)) * 32, 32)
            keep_ref[piece, target] = grad_ref[pl.ds(row, 32), :]
            row = pl.multiple_of((pix ^ 1 ^ reach(order, position)) * 32, 32)
            send_ref[piece, target] = grad_ref[pl.ds(row, 32), :].astype(BF16)


def make_full(tm, pieces, full_ref):
    for (begin, size, order), near, far in zip(PARTS, pieces[0::2], pieces[1::2]):
        for position in range(8):
            row = pl.multiple_of((tm ^ reach(order, position)) * 64, 64)
            piece = near if position < 4 else far
            full_ref[pl.ds(row, 64), begin : begin + size] = piece[pl.ds(position % 4 * 64, 64), :]


def make_gram(factor_ref, gram_ref):
    gram_ref[...] = (nt(factor_ref[...], factor_ref[...]) * (1.0 / math.sqrt(factor_ref.shape[0]))).astype(BF16)


def temporal_start(
    factors, place_ref, a0, b0, a1, b1, a2, b2, contrasted_ref, mine_ref, other_ref, r0, r1, r2, r3,
    full_ref, gram_ref, send_ref, keep_ref, time_ref, quad0_ref, quad1_ref, table_ref, grad_ref,
):
    for i in range(8):
        grad_ref[i : i + 1, :] = jnp.zeros((1, grad_ref.shape[1]), F32)
    for low in range(0, table_ref.shape[0], LANES):
        for i, (row_ref, factor) in enumerate(zip((r0, r1, r2, r3), factors)):
            grad_ref[i : i + 1, :LANES] = row_ref[:, low : low + LANES] * factor
        table_ref[low : low + LANES, :] = grad_ref[0:8, :LANES].T
    tm, pix = place_ref[0], place_ref[1]
    make_full(tm, (a0, b0, a1, b1, a2, b2), full_ref)
    place_temporal(0, START, pix, mine_ref, other_ref, time_ref)
    make_gram(full_ref, gram_ref)
    temporal_blocks(0, pix, full_ref, contrasted_ref, gram_ref, time_ref, send_ref, keep_ref, grad_ref)
    for (begin, width, order), quad_ref in zip(FRAME_PARTS, (quad0_ref, quad1_ref)):
        for position in range(4):
            row = pl.multiple_of((pix ^ reach(order, position)) * 32, 32)
            quad_ref[position * 32 : position * 32 + 32, :] = time_ref[pl.ds(row, 32), begin : begin + width]


def temporal_first(
    place_ref, a0, b0, a1, b1, a2, b2, contrasted_ref, time_ref,
    full_ref, gram_ref, send_ref, keep_ref, grad_ref,
):
    make_full(place_ref[0], (a0, b0, a1, b1, a2, b2), full_ref)
    make_gram(full_ref, gram_ref)
    temporal_blocks(
        0, place_ref[1], full_ref, contrasted_ref, gram_ref, time_ref, send_ref, keep_ref, grad_ref
    )


def temporal_second(
    place_ref, full_ref, gram_ref, contrasted_ref, time_ref, send_ref, keep_ref, grad_ref
):
    temporal_blocks(
        1, place_ref[1], full_ref, contrasted_ref, gram_ref, time_ref, send_ref, keep_ref, grad_ref
    )


def temporal_update(part, place_ref, table_ref, quad_ref, sum_ref, got_ref, out_ref):
    order = FRAME_PARTS[part][2]
    for position in range(4):
        piece = slice(position * 32, position * 32 + 32)
        swapped = slice((position ^ 1) * 32, (position ^ 1) * 32 + 32)
        rows = pl.ds(pl.multiple_of((place_ref[1] ^ reach(order, position)) * 32, 32), 32)
        coef, limit = table_ref[rows, 0:1], table_ref[rows, 1:2]
        grad = sum_ref[piece, :].astype(F32) + got_ref[swapped, :].astype(F32)
        out_ref[piece, :] = soften(quad_ref[piece, :].astype(F32) + coef * grad, limit).astype(BF16)


def spatial_update(part, place_ref, table_ref, slab_ref, sum_ref, got_ref, out_ref):
    order = PARTS[part][2]
    for position in range(out_ref.shape[0] // 64):
        piece = slice(position * 64, position * 64 + 64)
        swapped = slice(0, 64) if got_ref.shape[0] == 64 else slice((position ^ 1) * 64, (position ^ 1) * 64 + 64)
        rows = pl.ds(pl.multiple_of((place_ref[0] ^ reach(order, position)) * 64, 64), 64)
        coef, limit = table_ref[rows, 2:3], table_ref[rows, 3:4]
        grad = sum_ref[piece, :].astype(F32) + got_ref[swapped, :].astype(F32)
        out_ref[piece, :] = soften(slab_ref[piece, :].astype(F32) + coef * grad, limit).astype(BF16)


def spatial_blocks(part, tm, full_ref, contrasted_ref, time_ref, gram_ref, send_ref, keep_ref, grad_ref):
    begin, width, order = PARTS[part]
    for low in range(0, width, BLOCK):
        size = min(BLOCK, width - low)
        pixels = slice(begin + low, begin + low + size)
        target = slice(low, low + size)
        grad_ref[:, :size] = nt(time_ref[...], contrasted_ref[pixels, :]) - nn(gram_ref[...], full_ref[:, pixels])
        for position in range(8):
            row = pl.multiple_of((tm ^ reach(order, position)) * 64, 64)
            piece = grad_ref[pl.ds(row, 64), :size]
            if position < 4:
                keep_ref[position * 64 : position * 64 + 64, target] = piece
            else:
                send_ref[position * 64 - 256 : position * 64 - 192, target] = piece.astype(BF16)


def spatial_first(
    place_ref, full_ref, contrasted_ref, mine0_ref, other0_ref, mine1_ref, other1_ref,
    time_ref, gram_ref, send_ref, keep_ref, grad_ref,
):
    tm, pix = place_ref[0], place_ref[1]
    for (begin, _, order), mine_ref, other_ref in zip(
        FRAME_PARTS, (mine0_ref, mine1_ref), (other0_ref, other1_ref)
    ):
        place_temporal(begin, order, pix, mine_ref, other_ref, time_ref)
    make_gram(time_ref, gram_ref)
    spatial_blocks(0, tm, full_ref, contrasted_ref, time_ref, gram_ref, send_ref, keep_ref, grad_ref)


def spatial_next(
    part, place_ref, full_ref, contrasted_ref, time_ref, gram_ref, send_ref, keep_ref, grad_ref
):
    spatial_blocks(
        part, place_ref[0], full_ref, contrasted_ref, time_ref, gram_ref, send_ref, keep_ref, grad_ref
    )


def call(kernel, place, operands, outs, scratch=()):
    return pl.pallas_call(
        kernel,
        out_shape=[pltpu.VMEM(shape, dtype) for shape, dtype in outs],
        in_specs=[SMEM] + [VMEM] * len(operands),
        out_specs=[VMEM] * len(outs),
        scratch_shapes=scratch,
        compiler_params=PARAMS,
    )(place, *[pin(operand) for operand in operands])


def per_device(
    movie, offsets, spatial, temporal, step_spatial, step_temporal, thresh_spatial, thresh_temporal
):
    slab, strip = spatial.shape
    shard, span = temporal.shape
    rank = slab * lax.axis_size("tm")
    pixels = strip * lax.axis_size("pix")
    frames = span * lax.axis_size("tm")
    pix = lax.axis_index("pix")
    tm = lax.axis_index("tm")
    place = jnp.stack([tm, pix]).astype(jnp.int32)

    spatial, place = lax.optimization_barrier((spatial, place))

    def second_gather(slabs):
        return [jnp.concatenate([s, hop(s, "tm", order[1])]) for s, (_, _, order) in zip(slabs, PARTS)]

    def first_gather(near):
        return [(a, hop(a, "tm", order[0])) for a, (_, _, order) in zip(near, PARTS)]

    slabs = [spatial[:, begin : begin + width] for begin, width, _ in PARTS]
    slabs = [jnp.concatenate([s, hop(s, "tm", order[2])]) for s, (_, _, order) in zip(slabs, PARTS)]
    mine = jnp.concatenate([temporal, hop(temporal, "pix", START[2])])
    mine = jnp.concatenate([mine, hop(mine, "pix", START[1])])
    size = lax.axis_size("pix")
    up = [(i, (i + 1) % size) for i in range(size)]
    down = [(j, i) for i, j in up]
    before = lax.ppermute(movie[movie.shape[0] - EDGE :], "pix", up)
    after = lax.ppermute(movie[:EDGE], "pix", down)
    slabs, mine, before, after = lax.optimization_barrier((slabs, mine, before, after))
    near = second_gather(slabs)
    mine = jnp.concatenate([mine, hop(mine, "pix", START[0])])
    contrasted = contrast(stencil_lower, place, offsets, movie, before)
    near, mine, contrasted = lax.optimization_barrier((near, mine, contrasted))
    pieces = first_gather(near)
    contrasted = contrast(
        functools.partial(stencil_upper, size), place, offsets, movie, after, (contrasted,)
    )
    other = hop(mine, "pix", 1)
    factors = (math.sqrt(rank) / pixels, 1.0, math.sqrt(rank) / frames, 1.0)
    steps = [a.reshape(1, rank) for a in (step_temporal, thresh_temporal, step_spatial, thresh_spatial)]

    half = rank // 2
    block = [pltpu.VMEM((rank, BLOCK), F32)]

    def both(width):
        return [((half, width), BF16), ((half, width), F32)]

    for turn in range(ROUNDS):
        flat = [piece for pair in pieces for piece in pair]
        outs = [((rank, strip), BF16), ((rank, rank), BF16)] + both(FRAME_PARTS[0][1])
        if turn == 0:
            outs += [((rank, span), BF16)] + [((half // 2, width), BF16) for _, width, _ in FRAME_PARTS]
            outs += [((rank, 8), F32)]
            full, gram, send, keep, time, *quads, table = call(
                functools.partial(temporal_start, factors),
                place,
                flat + [contrasted, mine, other] + steps,
                outs,
                block,
            )
        else:
            full, gram, send, keep = call(temporal_first, place, flat + [contrasted, time], outs, block)
        grads = [(send, keep)]
        grads.append(
            call(temporal_second, place, [full, gram, contrasted, time], both(FRAME_PARTS[1][1]), block)
        )
        totals = [keep + hop(send, "pix", 1).astype(F32) for send, keep in grads]
        totals = [
            g[: half // 2] + hop(g[half // 2 :].astype(BF16), "pix", order[0]).astype(F32)
            for g, (_, _, order) in zip(totals, FRAME_PARTS)
        ]
        sums = []
        for g, (_, _, order) in zip(totals, FRAME_PARTS):
            g = g.astype(BF16)
            got = hop(g, "pix", order[1])
            got = jnp.concatenate([got[2 * shard :], got[: 2 * shard]])
            sums.append((g.astype(F32) + got.astype(F32)).astype(BF16))
        gots = [hop(g, "pix", order[2]) for g, (_, _, order) in zip(sums, FRAME_PARTS)]
        quads = [
            call(functools.partial(temporal_update, part), place, [table, q, g, got], [(q.shape, BF16)])[0]
            for part, (q, g, got) in enumerate(zip(quads, sums, gots))
        ]
        ends = []
        for q, (_, _, order) in zip(quads, FRAME_PARTS):
            mine = jnp.concatenate([q, hop(q, "pix", order[0])])
            ends += [mine, hop(mine, "pix", 1)]
        time, gram, send, keep = call(
            spatial_first,
            place,
            [full, contrasted] + ends,
            [((rank, span), BF16), ((rank, rank), BF16)] + both(PARTS[0][1]),
            block,
        )
        grads = [(send, keep)]
        for part in (1, 2):
            grads.append(
                call(
                    functools.partial(spatial_next, part),
                    place,
                    [full, contrasted, time, gram],
                    both(PARTS[part][1]),
                    block,
                )
            )
        totals = [
            keep + hop(send, "tm", order[0]).astype(F32) for (send, keep), (_, _, order) in zip(grads, PARTS)
        ]
        totals = [
            total[: 2 * slab] + hop(total[2 * slab :].astype(BF16), "tm", order[1]).astype(F32)
            for total, (_, _, order) in zip(totals, PARTS)
        ]
        last = turn == ROUNDS - 1
        if last:
            sums = [total[:slab] for total in totals]
            gots = [
                hop(total[slab:].astype(BF16), "tm", order[2]) for total, (_, _, order) in zip(totals, PARTS)
            ]
        else:
            sums = [total.astype(BF16) for total in totals]
            gots = [hop(total, "tm", order[2]) for total, (_, _, order) in zip(sums, PARTS)]
        slabs = [
            call(functools.partial(spatial_update, part), place, [table, s, g, got], [(g.shape, BF16)])[0]
            for part, (s, g, got) in enumerate(zip(slabs, sums, gots))
        ]
        if not last:
            pieces = first_gather(second_gather(slabs))
    return jnp.concatenate(slabs, 1), jnp.concatenate([q[:shard] for q in quads], 1)


def solution(mesh):
    placed = (P("pix", "tm"), P(), P("tm", "pix"), P("pix", "tm"), P(), P(), P(), P())
    return jax.shard_map(
        per_device,
        mesh=mesh,
        in_specs=placed,
        out_specs=(P("tm", "pix"), P("pix", "tm")),
        check_vma=False,
    )
```

```python
import functools
import math

import jax
import jax.numpy as jnp
from jax import lax
from jax.experimental import pallas as pl
from jax.experimental.pallas import tpu as pltpu
from jax.sharding import PartitionSpec as P

HALO = 129
EDGE = 144
BLOCK = 256
NBR = 8
ROUNDS = 2
BF16 = jnp.bfloat16
F32 = jnp.float32

PARTS = ((0, 768, (3, 4, 1)), (768, 640, (4, 1, 3)), (1408, 640, (1, 3, 4)))
FRAME_PARTS = ((0, 512, (4, 12, 2)), (512, 512, (12, 2, 4)))
START = (12, 4, 2)
LANES = 128
VMEM = pl.BlockSpec(memory_space=pltpu.VMEM)
SMEM = pl.BlockSpec(memory_space=pltpu.SMEM)
HBM = pl.BlockSpec(memory_space=pltpu.HBM)
COPIES = pltpu.SemaphoreType.DMA((16,))
PARAMS = pltpu.CompilerParams(vmem_limit_bytes=12 * 1024 * 1024)


def hop(a, axis, mask):
    size = lax.axis_size(axis)
    return lax.ppermute(a, axis, [(i, i ^ mask) for i in range(size)])


def reach(order, position):
    first, second, third = order
    return first * (position // 4) ^ second * (position // 2 % 2) ^ third * (position % 2)


def soften(values, limit):
    return values - jnp.clip(values, -limit, limit)


def nn(a, b):
    return jnp.dot(a, b, preferred_element_type=F32)


def nt(a, b):
    return lax.dot_general(a, b, (((1,), (1,)), ((), ())), preferred_element_type=F32)


class Copies:
    def __init__(self, sems):
        self.sems = sems
        self.used = 0

    def start(self, source, target):
        copy = pltpu.make_async_copy(source, target, self.sems.at[self.used])
        self.used += 1
        copy.start()
        return copy


def band(offsets_ref, columns, base, inside=None):
    step = (
        lax.broadcasted_iota(jnp.int32, (BLOCK, columns), 1)
        - lax.broadcasted_iota(jnp.int32, (BLOCK, columns), 0)
        + base
    )
    weight = jnp.where(step == 0, 1.0, 0.0).astype(F32)
    for k in range(NBR):
        weight = weight - jnp.where(step == offsets_ref[k], 1.0 / NBR, 0.0).astype(F32)
    if inside is not None:
        weight = jnp.where(inside, weight, 0.0)
    return weight.astype(BF16)


def stencil_blocks(offsets_ref, movie_ref, edge_ref, out_ref, held_ref, sems, lower, inside):
    half = movie_ref.shape[0] // 2
    count = half // BLOCK
    start = 0 if lower else half - BLOCK
    copies = Copies(sems)
    loads = [
        copies.start(
            movie_ref.at[pl.ds(start + b * BLOCK, BLOCK), :], held_ref.at[pl.ds(b * BLOCK, BLOCK), :]
        )
        for b in range(count + 1)
    ]
    main = band(offsets_ref, 3 * BLOCK, -BLOCK)
    loads[0].wait()
    loads[1].wait()
    for b in range(count):
        middle = b if lower else b + 1
        if 1 < middle + 1 <= count:
            loads[middle + 1].wait()
        low = max(middle - 1, 0)
        high = min(middle + 2, count + 1)
        first = (low - middle + 1) * BLOCK
        total = nn(main[:, first : first + (high - low) * BLOCK], held_ref[low * BLOCK : high * BLOCK, :])
        if lower and b == 0:
            total += nn(band(offsets_ref, EDGE, -EDGE, inside), edge_ref[...])
        if not lower and b == count - 1:
            total += nn(band(offsets_ref, EDGE, BLOCK, inside), edge_ref[...])
        row = (0 if lower else half) + b * BLOCK
        out_ref[row : row + BLOCK, :] = total.astype(BF16)


def stencil_lower(place_ref, offsets_ref, movie_ref, edge_ref, out_ref, held_ref, sems):
    stencil_blocks(offsets_ref, movie_ref, edge_ref, out_ref, held_ref, sems, True, place_ref[1] > 0)


def stencil_upper(strips, place_ref, offsets_ref, movie_ref, edge_ref, made_ref, out_ref, held_ref, sems):
    del made_ref
    stencil_blocks(
        offsets_ref, movie_ref, edge_ref, out_ref, held_ref, sems, False, place_ref[1] < strips - 1
    )


def contrast(kernel, place, offsets, movie, edge, made=()):
    rows, span = movie.shape
    return pl.pallas_call(
        kernel,
        out_shape=pltpu.VMEM(movie.shape, BF16),
        in_specs=[SMEM, SMEM, HBM] + [VMEM] * (1 + len(made)),
        out_specs=VMEM,
        scratch_shapes=[pltpu.VMEM((rows // 2 + BLOCK, span), BF16), COPIES],
        input_output_aliases={4: 0} if made else {},
        compiler_params=PARAMS,
    )(place, offsets, pltpu.with_memory_space_constraint(movie, pltpu.HBM), pin(edge), *[pin(m) for m in made])


def pin(a):
    return pltpu.with_memory_space_constraint(a, pltpu.VMEM)


def place_temporal(begin, order, pix, mine_ref, other_ref, time_ref):
    columns = slice(begin, begin + mine_ref.shape[1])
    for position in range(8):
        piece = slice(position * 32, position * 32 + 32)
        for from_ref, side in ((mine_ref, 0), (other_ref, 1)):
            row = pl.multiple_of((pix ^ side ^ reach(order, position)) * 32, 32)
            time_ref[pl.ds(row, 32), columns] = from_ref[piece, :]


def temporal_blocks(part, pix, full_ref, contrasted_ref, gram_ref, time_ref, send_ref, keep_ref, grad_ref):
    begin, width, order = FRAME_PARTS[part]
    for low in range(0, width, BLOCK):
        columns = slice(begin + low, begin + low + BLOCK)
        target = slice(low, low + BLOCK)
        grad_ref[...] = nn(full_ref[...], contrasted_ref[:, columns]) - nn(gram_ref[...], time_ref[:, columns])
        for position in range(8):
            piece = slice(position * 32, position * 32 + 32)
            row = pl.multiple_of((pix ^ reach(order, position)) * 32, 32)
            keep_ref[piece, target] = grad_ref[pl.ds(row, 32), :]
            row = pl.multiple_of((pix ^ 1 ^ reach(order, position)) * 32, 32)
            send_ref[piece, target] = grad_ref[pl.ds(row, 32), :].astype(BF16)


def make_full(tm, pieces, full_ref):
    for (begin, size, order), near, far in zip(PARTS, pieces[0::2], pieces[1::2]):
        for position in range(8):
            row = pl.multiple_of((tm ^ reach(order, position)) * 64, 64)
            piece = near if position < 4 else far
            full_ref[pl.ds(row, 64), begin : begin + size] = piece[pl.ds(position % 4 * 64, 64), :]


def make_gram(factor_ref, gram_ref):
    gram_ref[...] = (nt(factor_ref[...], factor_ref[...]) * (1.0 / math.sqrt(factor_ref.shape[0]))).astype(BF16)


def temporal_start(
    factors, place_ref, a0, b0, a1, b1, a2, b2, contrasted_ref, mine_ref, other_ref, r0, r1, r2, r3,
    full_ref, s0, k0, s1, k1, time_ref, quad0_ref, quad1_ref, table_ref, gram_ref, grad_ref,
):
    for i in range(8):
        grad_ref[i : i + 1, :] = jnp.zeros((1, grad_ref.shape[1]), F32)
    for low in range(0, table_ref.shape[0], LANES):
        for i, (row_ref, factor) in enumerate(zip((r0, r1, r2, r3), factors)):
            grad_ref[i : i + 1, :LANES] = row_ref[:, low : low + LANES] * factor
        table_ref[low : low + LANES, :] = grad_ref[0:8, :LANES].T
    pix = place_ref[1]
    place_temporal(0, START, pix, mine_ref, other_ref, time_ref)
    temporal_step(
        place_ref, a0, b0, a1, b1, a2, b2, contrasted_ref, time_ref, full_ref, s0, k0, s1, k1, gram_ref, grad_ref
    )
    for (begin, width, order), quad_ref in zip(FRAME_PARTS, (quad0_ref, quad1_ref)):
        for position in range(4):
            row = pl.multiple_of((pix ^ reach(order, position)) * 32, 32)
            quad_ref[position * 32 : position * 32 + 32, :] = time_ref[pl.ds(row, 32), begin : begin + width]


def temporal_step(
    place_ref, a0, b0, a1, b1, a2, b2, contrasted_ref, time_ref,
    full_ref, s0, k0, s1, k1, gram_ref, grad_ref,
):
    make_full(place_ref[0], (a0, b0, a1, b1, a2, b2), full_ref)
    make_gram(full_ref, gram_ref)
    for part, (send_ref, keep_ref) in enumerate(((s0, k0), (s1, k1))):
        temporal_blocks(
            part, place_ref[1], full_ref, contrasted_ref, gram_ref, time_ref, send_ref, keep_ref, grad_ref
        )


def temporal_update(part, place_ref, table_ref, quad_ref, sum_ref, got_ref, out_ref):
    order = FRAME_PARTS[part][2]
    for position in range(4):
        piece = slice(position * 32, position * 32 + 32)
        swapped = slice((position ^ 1) * 32, (position ^ 1) * 32 + 32)
        rows = pl.ds(pl.multiple_of((place_ref[1] ^ reach(order, position)) * 32, 32), 32)
        coef, limit = table_ref[rows, 0:1], table_ref[rows, 1:2]
        grad = sum_ref[piece, :].astype(F32) + got_ref[swapped, :].astype(F32)
        out_ref[piece, :] = soften(quad_ref[piece, :].astype(F32) + coef * grad, limit).astype(BF16)


def spatial_update(part, place_ref, table_ref, slab_ref, sum_ref, got_ref, out_ref):
    order = PARTS[part][2]
    for position in range(out_ref.shape[0] // 64):
        piece = slice(position * 64, position * 64 + 64)
        swapped = slice(0, 64) if got_ref.shape[0] == 64 else slice((position ^ 1) * 64, (position ^ 1) * 64 + 64)
        rows = pl.ds(pl.multiple_of((place_ref[0] ^ reach(order, position)) * 64, 64), 64)
        coef, limit = table_ref[rows, 2:3], table_ref[rows, 3:4]
        grad = sum_ref[piece, :].astype(F32) + got_ref[swapped, :].astype(F32)
        out_ref[piece, :] = soften(slab_ref[piece, :].astype(F32) + coef * grad, limit).astype(BF16)


def spatial_blocks(part, tm, full_ref, contrasted_ref, time_ref, gram_ref, send_ref, keep_ref, grad_ref):
    begin, width, order = PARTS[part]
    for low in range(0, width, BLOCK):
        size = min(BLOCK, width - low)
        pixels = slice(begin + low, begin + low + size)
        target = slice(low, low + size)
        grad_ref[:, :size] = nt(time_ref[...], contrasted_ref[pixels, :]) - nn(gram_ref[...], full_ref[:, pixels])
        for position in range(8):
            row = pl.multiple_of((tm ^ reach(order, position)) * 64, 64)
            piece = grad_ref[pl.ds(row, 64), :size]
            if position < 4:
                keep_ref[position * 64 : position * 64 + 64, target] = piece
            else:
                send_ref[position * 64 - 256 : position * 64 - 192, target] = piece.astype(BF16)


def spatial_step(
    place_ref, full_ref, contrasted_ref, mine0_ref, other0_ref, mine1_ref, other1_ref,
    time_ref, s0, k0, s1, k1, s2, k2, gram_ref, grad_ref,
):
    tm, pix = place_ref[0], place_ref[1]
    for (begin, _, order), mine_ref, other_ref in zip(
        FRAME_PARTS, (mine0_ref, mine1_ref), (other0_ref, other1_ref)
    ):
        place_temporal(begin, order, pix, mine_ref, other_ref, time_ref)
    make_gram(time_ref, gram_ref)
    for part, (send_ref, keep_ref) in enumerate(((s0, k0), (s1, k1), (s2, k2))):
        spatial_blocks(
            part, tm, full_ref, contrasted_ref, time_ref, gram_ref, send_ref, keep_ref, grad_ref
        )


def call(kernel, place, operands, outs, scratch=()):
    return pl.pallas_call(
        kernel,
        out_shape=[pltpu.VMEM(shape, dtype) for shape, dtype in outs],
        in_specs=[SMEM] + [VMEM] * len(operands),
        out_specs=[VMEM] * len(outs),
        scratch_shapes=scratch,
        compiler_params=PARAMS,
    )(place, *[pin(operand) for operand in operands])


def per_device(
    movie, offsets, spatial, temporal, step_spatial, step_temporal, thresh_spatial, thresh_temporal
):
    slab, strip = spatial.shape
    shard, span = temporal.shape
    rank = slab * lax.axis_size("tm")
    pixels = strip * lax.axis_size("pix")
    frames = span * lax.axis_size("tm")
    pix = lax.axis_index("pix")
    tm = lax.axis_index("tm")
    place = jnp.stack([tm, pix]).astype(jnp.int32)

    spatial, place = lax.optimization_barrier((spatial, place))

    def second_gather(slabs):
        return [jnp.concatenate([s, hop(s, "tm", order[1])]) for s, (_, _, order) in zip(slabs, PARTS)]

    def first_gather(near):
        return [(a, hop(a, "tm", order[0])) for a, (_, _, order) in zip(near, PARTS)]

    slabs = [spatial[:, begin : begin + width] for begin, width, _ in PARTS]
    slabs = [jnp.concatenate([s, hop(s, "tm", order[2])]) for s, (_, _, order) in zip(slabs, PARTS)]
    mine = jnp.concatenate([temporal, hop(temporal, "pix", START[2])])
    size = lax.axis_size("pix")
    up = [(i, (i + 1) % size) for i in range(size)]
    down = [(j, i) for i, j in up]
    before = lax.ppermute(movie[movie.shape[0] - EDGE :], "pix", up)
    after = lax.ppermute(movie[:EDGE], "pix", down)
    slabs, mine, before, after = lax.optimization_barrier((slabs, mine, before, after))
    near = second_gather(slabs)
    mine = jnp.concatenate([mine, hop(mine, "pix", START[1])])
    contrasted = contrast(stencil_lower, place, offsets, movie, before)
    near, mine, contrasted = lax.optimization_barrier((near, mine, contrasted))
    pieces = first_gather(near)
    mine = jnp.concatenate([mine, hop(mine, "pix", START[0])])
    contrasted = contrast(
        functools.partial(stencil_upper, size), place, offsets, movie, after, (contrasted,)
    )
    pieces, mine, contrasted = lax.optimization_barrier((pieces, mine, contrasted))
    other = hop(mine, "pix", 1)
    factors = (math.sqrt(rank) / pixels, 1.0, math.sqrt(rank) / frames, 1.0)
    steps = [a.reshape(1, rank) for a in (step_temporal, thresh_temporal, step_spatial, thresh_spatial)]

    half = rank // 2
    scratch = [pltpu.VMEM((rank, rank), BF16), pltpu.VMEM((rank, BLOCK), F32)]

    def both(parts):
        return [((half, width), dtype) for _, width, _ in parts for dtype in (BF16, F32)]

    for turn in range(ROUNDS):
        flat = [piece for pair in pieces for piece in pair]
        outs = [((rank, strip), BF16)] + both(FRAME_PARTS)
        if turn == 0:
            outs += [((rank, span), BF16)] + [((half // 2, width), BF16) for _, width, _ in FRAME_PARTS]
            outs += [((rank, 8), F32)]
            full, s0, k0, s1, k1, time, *quads, table = call(
                functools.partial(temporal_start, factors),
                place,
                flat + [contrasted, mine, other] + steps,
                outs,
                scratch,
            )
        else:
            full, s0, k0, s1, k1 = call(temporal_step, place, flat + [contrasted, time], outs, scratch)
        grads = [(s0, k0), (s1, k1)]
        totals = [keep + hop(send, "pix", 1).astype(F32) for send, keep in grads]
        totals = [
            g[: half // 2] + hop(g[half // 2 :].astype(BF16), "pix", order[0]).astype(F32)
            for g, (_, _, order) in zip(totals, FRAME_PARTS)
        ]
        sums = []
        for g, (_, _, order) in zip(totals, FRAME_PARTS):
            g = g.astype(BF16)
            got = hop(g, "pix", order[1])
            got = jnp.concatenate([got[2 * shard :], got[: 2 * shard]])
            sums.append((g.astype(F32) + got.astype(F32)).astype(BF16))
        gots = [hop(g, "pix", order[2]) for g, (_, _, order) in zip(sums, FRAME_PARTS)]
        quads = [
            call(functools.partial(temporal_update, part), place, [table, q, g, got], [(q.shape, BF16)])[0]
            for part, (q, g, got) in enumerate(zip(quads, sums, gots))
        ]
        ends = []
        for q, (_, _, order) in zip(quads, FRAME_PARTS):
            mine = jnp.concatenate([q, hop(q, "pix", order[0])])
            ends += [mine, hop(mine, "pix", 1)]
        time, *grads = call(
            spatial_step, place, [full, contrasted] + ends, [((rank, span), BF16)] + both(PARTS), scratch
        )
        grads = list(zip(grads[0::2], grads[1::2]))
        totals = [
            keep + hop(send, "tm", order[0]).astype(F32) for (send, keep), (_, _, order) in zip(grads, PARTS)
        ]
        totals = [
            total[: 2 * slab] + hop(total[2 * slab :].astype(BF16), "tm", order[1]).astype(F32)
            for total, (_, _, order) in zip(totals, PARTS)
        ]
        last = turn == ROUNDS - 1
        if last:
            sums = [total[:slab] for total in totals]
            gots = [
                hop(total[slab:].astype(BF16), "tm", order[2]) for total, (_, _, order) in zip(totals, PARTS)
            ]
        else:
            sums = [total.astype(BF16) for total in totals]
            gots = [hop(total, "tm", order[2]) for total, (_, _, order) in zip(sums, PARTS)]
        slabs = [
            call(functools.partial(spatial_update, part), place, [table, s, g, got], [(g.shape, BF16)])[0]
            for part, (s, g, got) in enumerate(zip(slabs, sums, gots))
        ]
        if not last:
            pieces = first_gather(second_gather(slabs))
    return jnp.concatenate(slabs, 1), jnp.concatenate([q[:shard] for q in quads], 1)


def solution(mesh):
    placed = (P("pix", "tm"), P(), P("tm", "pix"), P("pix", "tm"), P(), P(), P(), P())
    return jax.shard_map(
        per_device,
        mesh=mesh,
        in_specs=placed,
        out_specs=(P("tm", "pix"), P("pix", "tm")),
        check_vma=False,
    )
```

```python
import functools
import math

import jax
import jax.numpy as jnp
from jax import lax
from jax.experimental import pallas as pl
from jax.experimental.pallas import tpu as pltpu
from jax.sharding import PartitionSpec as P

HALO = 129
EDGE = 144
BLOCK = 256
NBR = 8
ROUNDS = 2
BF16 = jnp.bfloat16
F32 = jnp.float32

PARTS = ((0, 768, (3, 4, 1)), (768, 640, (4, 1, 3)), (1408, 640, (1, 3, 4)))
FRAME_PARTS = ((0, 512, (4, 12, 2)), (512, 512, (12, 2, 4)))
START = (12, 4, 2)
LANES = 128
VMEM = pl.BlockSpec(memory_space=pltpu.VMEM)
SMEM = pl.BlockSpec(memory_space=pltpu.SMEM)
HBM = pl.BlockSpec(memory_space=pltpu.HBM)
COPIES = pltpu.SemaphoreType.DMA((16,))
PARAMS = pltpu.CompilerParams(vmem_limit_bytes=12 * 1024 * 1024)


def hop(a, axis, mask):
    size = lax.axis_size(axis)
    return lax.ppermute(a, axis, [(i, i ^ mask) for i in range(size)])


def reach(order, position):
    first, second, third = order
    return first * (position // 4) ^ second * (position // 2 % 2) ^ third * (position % 2)


def soften(values, limit):
    return values - jnp.clip(values, -limit, limit)


def nn(a, b):
    return jnp.dot(a, b, preferred_element_type=F32)


def nt(a, b):
    return lax.dot_general(a, b, (((1,), (1,)), ((), ())), preferred_element_type=F32)


class Copies:
    def __init__(self, sems):
        self.sems = sems
        self.used = 0

    def start(self, source, target):
        copy = pltpu.make_async_copy(source, target, self.sems.at[self.used])
        self.used += 1
        copy.start()
        return copy


def band(offsets_ref, columns, base, inside=None):
    step = (
        lax.broadcasted_iota(jnp.int32, (BLOCK, columns), 1)
        - lax.broadcasted_iota(jnp.int32, (BLOCK, columns), 0)
        + base
    )
    weight = jnp.where(step == 0, 1.0, 0.0).astype(F32)
    for k in range(NBR):
        weight = weight - jnp.where(step == offsets_ref[k], 1.0 / NBR, 0.0).astype(F32)
    if inside is not None:
        weight = jnp.where(inside, weight, 0.0)
    return weight.astype(BF16)


def stencil_blocks(which, place_ref, offsets_ref, movie_ref, edges, out_ref, held_ref, sems):
    count = movie_ref.shape[0] // BLOCK
    copies = Copies(sems)
    loads = {}
    for b in which:
        for n in range(max(b - 1, 0), min(b + 2, count)):
            if n not in loads:
                rows = pl.ds(n * BLOCK, BLOCK)
                loads[n] = copies.start(movie_ref.at[rows, :], held_ref.at[rows, :])
    main = band(offsets_ref, 3 * BLOCK, -BLOCK)
    for b in which:
        low = max(b - 1, 0)
        high = min(b + 2, count)
        for n in range(low, high):
            if n in loads:
                loads.pop(n).wait()
        first = (low - b + 1) * BLOCK
        total = nn(main[:, first : first + (high - low) * BLOCK], held_ref[low * BLOCK : high * BLOCK, :])
        if b == 0:
            total += nn(band(offsets_ref, EDGE, -EDGE, place_ref[1] > 0), edges[0][...])
        if b == count - 1:
            total += nn(band(offsets_ref, EDGE, BLOCK, place_ref[1] < edges[2] - 1), edges[1][...])
        out_ref[b * BLOCK : (b + 1) * BLOCK, :] = total.astype(BF16)


def stencil_inner(which, place_ref, offsets_ref, movie_ref, out_ref, held_ref, sems):
    stencil_blocks(which, place_ref, offsets_ref, movie_ref, None, out_ref, held_ref, sems)


def stencil_outer(
    which, strips, place_ref, offsets_ref, movie_ref, made_ref, before_ref, after_ref, out_ref, held_ref, sems
):
    del made_ref
    stencil_blocks(
        which, place_ref, offsets_ref, movie_ref, (before_ref, after_ref, strips), out_ref, held_ref, sems
    )


def contrast(kernel, place, offsets, movie, made=()):
    return pl.pallas_call(
        kernel,
        out_shape=pltpu.VMEM(movie.shape, BF16),
        in_specs=[SMEM, SMEM, HBM] + [VMEM] * len(made),
        out_specs=VMEM,
        scratch_shapes=[pltpu.VMEM(movie.shape, BF16), COPIES],
        input_output_aliases={3: 0} if made else {},
        compiler_params=PARAMS,
    )(place, offsets, pltpu.with_memory_space_constraint(movie, pltpu.HBM), *[pin(m) for m in made])


def pin(a):
    return pltpu.with_memory_space_constraint(a, pltpu.VMEM)


def place_temporal(begin, order, pix, mine_ref, other_ref, time_ref):
    columns = slice(begin, begin + mine_ref.shape[1])
    for position in range(8):
        piece = slice(position * 32, position * 32 + 32)
        for from_ref, side in ((mine_ref, 0), (other_ref, 1)):
            row = pl.multiple_of((pix ^ side ^ reach(order, position)) * 32, 32)
            time_ref[pl.ds(row, 32), columns] = from_ref[piece, :]


def temporal_blocks(part, pix, full_ref, contrasted_ref, gram_ref, time_ref, send_ref, keep_ref, grad_ref):
    begin, width, order = FRAME_PARTS[part]
    for low in range(0, width, BLOCK):
        columns = slice(begin + low, begin + low + BLOCK)
        target = slice(low, low + BLOCK)
        grad_ref[...] = nn(full_ref[...], contrasted_ref[:, columns]) - nn(gram_ref[...], time_ref[:, columns])
        for position in range(8):
            piece = slice(position * 32, position * 32 + 32)
            row = pl.multiple_of((pix ^ reach(order, position)) * 32, 32)
            keep_ref[piece, target] = grad_ref[pl.ds(row, 32), :]
            row = pl.multiple_of((pix ^ 1 ^ reach(order, position)) * 32, 32)
            send_ref[piece, target] = grad_ref[pl.ds(row, 32), :].astype(BF16)


def make_full(tm, pieces, full_ref):
    for (begin, size, order), near, far in zip(PARTS, pieces[0::2], pieces[1::2]):
        for position in range(8):
            row = pl.multiple_of((tm ^ reach(order, position)) * 64, 64)
            piece = near if position < 4 else far
            full_ref[pl.ds(row, 64), begin : begin + size] = piece[pl.ds(position % 4 * 64, 64), :]


def make_gram(factor_ref, gram_ref):
    gram_ref[...] = (nt(factor_ref[...], factor_ref[...]) * (1.0 / math.sqrt(factor_ref.shape[0]))).astype(BF16)


def temporal_start(
    factors, place_ref, a0, b0, a1, b1, a2, b2, contrasted_ref, mine_ref, other_ref, r0, r1, r2, r3,
    full_ref, s0, k0, s1, k1, time_ref, quad0_ref, quad1_ref,
    tc0, tl0, tc1, tl1, sc0, sl0, sc1, sl1, sc2, sl2, gram_ref, grad_ref, table_ref,
):
    for i in range(8):
        grad_ref[i : i + 1, :] = jnp.zeros((1, grad_ref.shape[1]), F32)
    for low in range(0, table_ref.shape[0], LANES):
        for i, (row_ref, factor) in enumerate(zip((r0, r1, r2, r3), factors)):
            grad_ref[i : i + 1, :LANES] = row_ref[:, low : low + LANES] * factor
        table_ref[low : low + LANES, :] = grad_ref[0:8, :LANES].T
    pix = place_ref[1]
    place_temporal(0, START, pix, mine_ref, other_ref, time_ref)
    temporal_step(
        place_ref, a0, b0, a1, b1, a2, b2, contrasted_ref, time_ref, full_ref, s0, k0, s1, k1, gram_ref, grad_ref
    )
    for (begin, width, order), quad_ref in zip(FRAME_PARTS, (quad0_ref, quad1_ref)):
        for position in range(4):
            row = pl.multiple_of((pix ^ reach(order, position)) * 32, 32)
            quad_ref[position * 32 : position * 32 + 32, :] = time_ref[pl.ds(row, 32), begin : begin + width]
    lay_out(FRAME_PARTS, pix, 32, table_ref, 0, ((tc0, tl0), (tc1, tl1)))
    lay_out(PARTS, place_ref[0], 64, table_ref, 2, ((sc0, sl0), (sc1, sl1), (sc2, sl2)))


def lay_out(parts, here, size, table_ref, column, targets):
    for (_, width, order), pair in zip(parts, targets):
        for position in range(pair[0].shape[0] // size):
            row = pl.multiple_of((here ^ reach(order, position)) * size, size)
            piece = slice(position * size, position * size + size)
            for i, target in enumerate(pair):
                value = table_ref[pl.ds(row, size), column + i : column + i + 1]
                target[piece, :] = jnp.broadcast_to(value, (size, width))


def temporal_step(
    place_ref, a0, b0, a1, b1, a2, b2, contrasted_ref, time_ref,
    full_ref, s0, k0, s1, k1, gram_ref, grad_ref,
):
    make_full(place_ref[0], (a0, b0, a1, b1, a2, b2), full_ref)
    make_gram(full_ref, gram_ref)
    for part, (send_ref, keep_ref) in enumerate(((s0, k0), (s1, k1))):
        temporal_blocks(
            part, place_ref[1], full_ref, contrasted_ref, gram_ref, time_ref, send_ref, keep_ref, grad_ref
        )


def spatial_blocks(part, tm, full_ref, contrasted_ref, time_ref, gram_ref, send_ref, keep_ref, grad_ref):
    begin, width, order = PARTS[part]
    for low in range(0, width, BLOCK):
        size = min(BLOCK, width - low)
        pixels = slice(begin + low, begin + low + size)
        target = slice(low, low + size)
        grad_ref[:, :size] = nt(time_ref[...], contrasted_ref[pixels, :]) - nn(gram_ref[...], full_ref[:, pixels])
        for position in range(8):
            row = pl.multiple_of((tm ^ reach(order, position)) * 64, 64)
            piece = grad_ref[pl.ds(row, 64), :size]
            if position < 4:
                keep_ref[position * 64 : position * 64 + 64, target] = piece
            else:
                send_ref[position * 64 - 256 : position * 64 - 192, target] = piece.astype(BF16)


def spatial_step(
    place_ref, full_ref, contrasted_ref, mine0_ref, other0_ref, mine1_ref, other1_ref,
    time_ref, s0, k0, s1, k1, s2, k2, gram_ref, grad_ref,
):
    tm, pix = place_ref[0], place_ref[1]
    for (begin, _, order), mine_ref, other_ref in zip(
        FRAME_PARTS, (mine0_ref, mine1_ref), (other0_ref, other1_ref)
    ):
        place_temporal(begin, order, pix, mine_ref, other_ref, time_ref)
    make_gram(time_ref, gram_ref)
    for part, (send_ref, keep_ref) in enumerate(((s0, k0), (s1, k1), (s2, k2))):
        spatial_blocks(
            part, tm, full_ref, contrasted_ref, time_ref, gram_ref, send_ref, keep_ref, grad_ref
        )


def update(values, sums, got, rule, size):
    rows = sums.shape[0]
    if rows > size:
        got = jnp.concatenate([got[(i ^ 1) * size : (i ^ 1) * size + size] for i in range(rows // size)])
    coef, limit = (a[:rows] for a in rule)
    grad = sums.astype(F32) + got.astype(F32)
    return soften(values[:rows].astype(F32) + coef * grad, limit).astype(BF16)


def call(kernel, place, operands, outs, scratch=()):
    return pl.pallas_call(
        kernel,
        out_shape=[pltpu.VMEM(shape, dtype) for shape, dtype in outs],
        in_specs=[SMEM] + [VMEM] * len(operands),
        out_specs=[VMEM] * len(outs),
        scratch_shapes=scratch,
        compiler_params=PARAMS,
    )(place, *[pin(operand) for operand in operands])


def per_device(
    movie, offsets, spatial, temporal, step_spatial, step_temporal, thresh_spatial, thresh_temporal
):
    slab, strip = spatial.shape
    shard, span = temporal.shape
    rank = slab * lax.axis_size("tm")
    pixels = strip * lax.axis_size("pix")
    frames = span * lax.axis_size("tm")
    pix = lax.axis_index("pix")
    tm = lax.axis_index("tm")
    place = jnp.stack([tm, pix]).astype(jnp.int32)

    spatial, place = lax.optimization_barrier((spatial, place))

    def second_gather(slabs):
        return [jnp.concatenate([s, hop(s, "tm", order[1])]) for s, (_, _, order) in zip(slabs, PARTS)]

    def first_gather(near):
        return [(a, hop(a, "tm", order[0])) for a, (_, _, order) in zip(near, PARTS)]

    slabs = [spatial[:, begin : begin + width] for begin, width, _ in PARTS]
    slabs = [jnp.concatenate([s, hop(s, "tm", order[2])]) for s, (_, _, order) in zip(slabs, PARTS)]
    mine = jnp.concatenate([temporal, hop(temporal, "pix", START[2])])
    size = lax.axis_size("pix")
    up = [(i, (i + 1) % size) for i in range(size)]
    down = [(j, i) for i, j in up]
    before = lax.ppermute(movie[movie.shape[0] - EDGE :], "pix", up)
    after = lax.ppermute(movie[:EDGE], "pix", down)
    slabs, mine, place, before = lax.optimization_barrier((slabs, mine, place, before))
    near = second_gather(slabs)
    mine = jnp.concatenate([mine, hop(mine, "pix", START[1])])
    blocks = range(strip // BLOCK)
    inner = blocks[1 : 1 + len(blocks) // 2]
    outer = [b for b in blocks if b not in inner]
    contrasted = contrast(functools.partial(stencil_inner, inner), place, offsets, movie)
    near, mine, contrasted, after = lax.optimization_barrier((near, mine, contrasted, after))
    pieces = first_gather(near)
    mine = jnp.concatenate([mine, hop(mine, "pix", START[0])])
    contrasted = contrast(
        functools.partial(stencil_outer, outer, size), place, offsets, movie, (contrasted, before, after)
    )
    pieces, mine, contrasted = lax.optimization_barrier((pieces, mine, contrasted))
    other = hop(mine, "pix", 1)
    factors = (math.sqrt(rank) / pixels, 1.0, math.sqrt(rank) / frames, 1.0)
    steps = [a.reshape(1, rank) for a in (step_temporal, thresh_temporal, step_spatial, thresh_spatial)]

    half = rank // 2
    scratch = [pltpu.VMEM((rank, rank), BF16), pltpu.VMEM((rank, BLOCK), F32)]

    def both(parts):
        return [((half, width), dtype) for _, width, _ in parts for dtype in (BF16, F32)]

    for turn in range(ROUNDS):
        flat = [piece for pair in pieces for piece in pair]
        outs = [((rank, strip), BF16)] + both(FRAME_PARTS)
        if turn == 0:
            outs += [((rank, span), BF16)] + [((half // 2, width), BF16) for _, width, _ in FRAME_PARTS]
            outs += [((half // 2, width), F32) for _, width, _ in FRAME_PARTS + PARTS for _ in range(2)]
            full, s0, k0, s1, k1, time, *rest = call(
                functools.partial(temporal_start, factors),
                place,
                flat + [contrasted, mine, other] + steps,
                outs,
                scratch + [pltpu.VMEM((rank, 8), F32)],
            )
            count = len(FRAME_PARTS)
            quads = rest[:count]
            rules = list(zip(rest[count::2], rest[count + 1 :: 2]))
        else:
            full, s0, k0, s1, k1 = call(temporal_step, place, flat + [contrasted, time], outs, scratch)
        grads = [(s0, k0), (s1, k1)]
        totals = [keep + hop(send, "pix", 1).astype(F32) for send, keep in grads]
        totals = [
            g[: half // 2] + hop(g[half // 2 :].astype(BF16), "pix", order[0]).astype(F32)
            for g, (_, _, order) in zip(totals, FRAME_PARTS)
        ]
        sums = []
        for g, (_, _, order) in zip(totals, FRAME_PARTS):
            g = g.astype(BF16)
            got = hop(g, "pix", order[1])
            got = jnp.concatenate([got[2 * shard :], got[: 2 * shard]])
            sums.append((g.astype(F32) + got.astype(F32)).astype(BF16))
        gots = [hop(g, "pix", order[2]) for g, (_, _, order) in zip(sums, FRAME_PARTS)]
        quads = [update(*each, shard) for each in zip(quads, sums, gots, rules[:count])]
        ends = []
        for q, (_, _, order) in zip(quads, FRAME_PARTS):
            mine = jnp.concatenate([q, hop(q, "pix", order[0])])
            ends += [mine, hop(mine, "pix", 1)]
        time, *grads = call(
            spatial_step, place, [full, contrasted] + ends, [((rank, span), BF16)] + both(PARTS), scratch
        )
        grads = list(zip(grads[0::2], grads[1::2]))
        totals = [
            keep + hop(send, "tm", order[0]).astype(F32) for (send, keep), (_, _, order) in zip(grads, PARTS)
        ]
        totals = [
            total[: 2 * slab] + hop(total[2 * slab :].astype(BF16), "tm", order[1]).astype(F32)
            for total, (_, _, order) in zip(totals, PARTS)
        ]
        last = turn == ROUNDS - 1
        if last:
            sums = [total[:slab] for total in totals]
            gots = [
                hop(total[slab:].astype(BF16), "tm", order[2]) for total, (_, _, order) in zip(totals, PARTS)
            ]
        else:
            sums = [total.astype(BF16) for total in totals]
            gots = [hop(total, "tm", order[2]) for total, (_, _, order) in zip(sums, PARTS)]
        slabs = [update(*each, slab) for each in zip(slabs, sums, gots, rules[count:])]
        if not last:
            pieces = first_gather(second_gather(slabs))
    return jnp.concatenate(slabs, 1), jnp.concatenate([q[:shard] for q in quads], 1)


def solution(mesh):
    placed = (P("pix", "tm"), P(), P("tm", "pix"), P("pix", "tm"), P(), P(), P(), P())
    return jax.shard_map(
        per_device,
        mesh=mesh,
        in_specs=placed,
        out_specs=(P("tm", "pix"), P("pix", "tm")),
        check_vma=False,
    )
```

```python
import functools
import math

import jax
import jax.numpy as jnp
from jax import lax
from jax.experimental import pallas as pl
from jax.experimental.pallas import tpu as pltpu
from jax.sharding import PartitionSpec as P

HALO = 129
EDGE = 144
BLOCK = 256
NBR = 8
ROUNDS = 2
BF16 = jnp.bfloat16
F32 = jnp.float32

PARTS = ((0, 768, (3, 4, 1)), (768, 640, (4, 1, 3)), (1408, 640, (1, 3, 4)))
FRAME_PARTS = ((0, 512, (4, 12, 2)), (512, 512, (12, 2, 4)))
START_PARTS = ((0, 1024, (1, 3, 4)), (1024, 1024, (3, 1, 4)))
LANES = 128
VMEM = pl.BlockSpec(memory_space=pltpu.VMEM)
SMEM = pl.BlockSpec(memory_space=pltpu.SMEM)
HBM = pl.BlockSpec(memory_space=pltpu.HBM)
COPIES = pltpu.SemaphoreType.DMA((16,))
PARAMS = pltpu.CompilerParams(vmem_limit_bytes=12 * 1024 * 1024)


def hop(a, axis, mask):
    size = lax.axis_size(axis)
    return lax.ppermute(a, axis, [(i, i ^ mask) for i in range(size)])


def reach(order, position):
    first, second, third = order
    return first * (position // 4) ^ second * (position // 2 % 2) ^ third * (position % 2)


def soften(values, limit):
    return values - jnp.clip(values, -limit, limit)


def nn(a, b):
    return jnp.dot(a, b, preferred_element_type=F32)


def nt(a, b):
    return lax.dot_general(a, b, (((1,), (1,)), ((), ())), preferred_element_type=F32)


class Copies:
    def __init__(self, sems):
        self.sems = sems
        self.used = 0

    def start(self, source, target):
        copy = pltpu.make_async_copy(source, target, self.sems.at[self.used])
        self.used += 1
        copy.start()
        return copy


def band(offsets_ref, columns, base, inside=None):
    step = (
        lax.broadcasted_iota(jnp.int32, (BLOCK, columns), 1)
        - lax.broadcasted_iota(jnp.int32, (BLOCK, columns), 0)
        + base
    )
    weight = jnp.where(step == 0, 1.0, 0.0).astype(F32)
    for k in range(NBR):
        weight = weight - jnp.where(step == offsets_ref[k], 1.0 / NBR, 0.0).astype(F32)
    if inside is not None:
        weight = jnp.where(inside, weight, 0.0)
    return weight.astype(BF16)


def stencil_blocks(which, place_ref, offsets_ref, movie_ref, edges, out_ref, held_ref, sems):
    count = movie_ref.shape[0] // BLOCK
    copies = Copies(sems)
    loads = {}
    for b in which:
        for n in range(max(b - 1, 0), min(b + 2, count)):
            if n not in loads:
                rows = pl.ds(n * BLOCK, BLOCK)
                loads[n] = copies.start(movie_ref.at[rows, :], held_ref.at[rows, :])
    main = band(offsets_ref, 3 * BLOCK, -BLOCK)
    for b in which:
        low = max(b - 1, 0)
        high = min(b + 2, count)
        for n in range(low, high):
            if n in loads:
                loads.pop(n).wait()
        first = (low - b + 1) * BLOCK
        total = nn(main[:, first : first + (high - low) * BLOCK], held_ref[low * BLOCK : high * BLOCK, :])
        if b == 0:
            total += nn(band(offsets_ref, EDGE, -EDGE, place_ref[1] > 0), edges[0][...])
        if b == count - 1:
            total += nn(band(offsets_ref, EDGE, BLOCK, place_ref[1] < edges[2] - 1), edges[1][...])
        out_ref[b * BLOCK : (b + 1) * BLOCK, :] = total.astype(BF16)


def stencil_inner(which, place_ref, offsets_ref, movie_ref, out_ref, held_ref, sems):
    stencil_blocks(which, place_ref, offsets_ref, movie_ref, None, out_ref, held_ref, sems)


def stencil_outer(
    which, strips, place_ref, offsets_ref, movie_ref, made_ref, before_ref, after_ref, out_ref, held_ref, sems
):
    del made_ref
    stencil_blocks(
        which, place_ref, offsets_ref, movie_ref, (before_ref, after_ref, strips), out_ref, held_ref, sems
    )


def contrast(kernel, place, offsets, movie, made=()):
    return pl.pallas_call(
        kernel,
        out_shape=pltpu.VMEM(movie.shape, BF16),
        in_specs=[SMEM, SMEM, HBM] + [VMEM] * len(made),
        out_specs=VMEM,
        scratch_shapes=[pltpu.VMEM(movie.shape, BF16), COPIES],
        input_output_aliases={3: 0} if made else {},
        compiler_params=PARAMS,
    )(place, offsets, pltpu.with_memory_space_constraint(movie, pltpu.HBM), *[pin(m) for m in made])


def pin(a):
    return pltpu.with_memory_space_constraint(a, pltpu.VMEM)


def place_temporal(begin, order, pix, mine_ref, other_ref, time_ref):
    columns = slice(begin, begin + mine_ref.shape[1])
    for position in range(8):
        piece = slice(position * 32, position * 32 + 32)
        for from_ref, side in ((mine_ref, 0), (other_ref, 1)):
            row = pl.multiple_of((pix ^ side ^ reach(order, position)) * 32, 32)
            time_ref[pl.ds(row, 32), columns] = from_ref[piece, :]


def temporal_blocks(part, pix, full_ref, contrasted_ref, gram_ref, time_ref, send_ref, keep_ref, grad_ref):
    begin, width, order = FRAME_PARTS[part]
    for low in range(0, width, BLOCK):
        columns = slice(begin + low, begin + low + BLOCK)
        target = slice(low, low + BLOCK)
        grad_ref[...] = nn(full_ref[...], contrasted_ref[:, columns]) - nn(gram_ref[...], time_ref[:, columns])
        for position in range(8):
            piece = slice(position * 32, position * 32 + 32)
            row = pl.multiple_of((pix ^ reach(order, position)) * 32, 32)
            keep_ref[piece, target] = grad_ref[pl.ds(row, 32), :]
            row = pl.multiple_of((pix ^ 1 ^ reach(order, position)) * 32, 32)
            send_ref[piece, target] = grad_ref[pl.ds(row, 32), :].astype(BF16)


def make_full(parts, tm, pieces, full_ref):
    for (begin, size, order), near, far in zip(parts, pieces[0::2], pieces[1::2]):
        for position in range(8):
            row = pl.multiple_of((tm ^ reach(order, position)) * 64, 64)
            piece = near if position < 4 else far
            full_ref[pl.ds(row, 64), begin : begin + size] = piece[pl.ds(position % 4 * 64, 64), :]


def make_gram(factor_ref, gram_ref):
    gram_ref[...] = (nt(factor_ref[...], factor_ref[...]) * (1.0 / math.sqrt(factor_ref.shape[0]))).astype(BF16)


def temporal_start(
    factors, place_ref, a0, b0, a1, b1, contrasted_ref, near_ref, far_ref, r0, r1, r2, r3,
    full_ref, s0, k0, s1, k1, time_ref, quad0_ref, quad1_ref, slab0_ref, slab1_ref, slab2_ref,
    tc0, tl0, tc1, tl1, sc0, sl0, sc1, sl1, sc2, sl2, gram_ref, grad_ref, table_ref,
):
    for i in range(8):
        grad_ref[i : i + 1, :] = jnp.zeros((1, grad_ref.shape[1]), F32)
    for low in range(0, table_ref.shape[0], LANES):
        for i, (row_ref, factor) in enumerate(zip((r0, r1, r2, r3), factors)):
            grad_ref[i : i + 1, :LANES] = row_ref[:, low : low + LANES] * factor
        table_ref[low : low + LANES, :] = grad_ref[0:8, :LANES].T
    tm, pix = place_ref[0], place_ref[1]
    for side, from_ref in ((0, near_ref), (12, far_ref)):
        for position in range(8):
            row = pl.multiple_of((pix ^ side ^ reach((4, 2, 1), position)) * 32, 32)
            time_ref[pl.ds(row, 32), :] = from_ref[position * 32 : position * 32 + 32, :]
    make_full(START_PARTS, tm, (a0, b0, a1, b1), full_ref)
    temporal_products(
        place_ref, contrasted_ref, time_ref, full_ref, ((s0, k0), (s1, k1)), gram_ref, grad_ref
    )
    for (begin, width, order), slab_ref in zip(PARTS, (slab0_ref, slab1_ref, slab2_ref)):
        for position in range(2):
            row = pl.multiple_of((tm ^ reach(order, position)) * 64, 64)
            slab_ref[position * 64 : position * 64 + 64, :] = full_ref[pl.ds(row, 64), begin : begin + width]
    for (begin, width, order), quad_ref in zip(FRAME_PARTS, (quad0_ref, quad1_ref)):
        for position in range(4):
            row = pl.multiple_of((pix ^ reach(order, position)) * 32, 32)
            quad_ref[position * 32 : position * 32 + 32, :] = time_ref[pl.ds(row, 32), begin : begin + width]
    lay_out(FRAME_PARTS, pix, 32, table_ref, 0, ((tc0, tl0), (tc1, tl1)))
    lay_out(PARTS, place_ref[0], 64, table_ref, 2, ((sc0, sl0), (sc1, sl1), (sc2, sl2)))


def lay_out(parts, here, size, table_ref, column, targets):
    for (_, width, order), pair in zip(parts, targets):
        for position in range(pair[0].shape[0] // size):
            row = pl.multiple_of((here ^ reach(order, position)) * size, size)
            piece = slice(position * size, position * size + size)
            for i, target in enumerate(pair):
                value = table_ref[pl.ds(row, size), column + i : column + i + 1]
                target[piece, :] = jnp.broadcast_to(value, (size, width))


def temporal_step(
    place_ref, a0, b0, a1, b1, a2, b2, contrasted_ref, time_ref,
    full_ref, s0, k0, s1, k1, gram_ref, grad_ref,
):
    make_full(PARTS, place_ref[0], (a0, b0, a1, b1, a2, b2), full_ref)
    temporal_products(
        place_ref, contrasted_ref, time_ref, full_ref, ((s0, k0), (s1, k1)), gram_ref, grad_ref
    )


def temporal_products(place_ref, contrasted_ref, time_ref, full_ref, targets, gram_ref, grad_ref):
    make_gram(full_ref, gram_ref)
    for part, (send_ref, keep_ref) in enumerate(targets):
        temporal_blocks(
            part, place_ref[1], full_ref, contrasted_ref, gram_ref, time_ref, send_ref, keep_ref, grad_ref
        )


def spatial_blocks(part, tm, full_ref, contrasted_ref, time_ref, gram_ref, send_ref, keep_ref, grad_ref):
    begin, width, order = PARTS[part]
    for low in range(0, width, BLOCK):
        size = min(BLOCK, width - low)
        pixels = slice(begin + low, begin + low + size)
        target = slice(low, low + size)
        grad_ref[:, :size] = nt(time_ref[...], contrasted_ref[pixels, :]) - nn(gram_ref[...], full_ref[:, pixels])
        for position in range(8):
            row = pl.multiple_of((tm ^ reach(order, position)) * 64, 64)
            piece = grad_ref[pl.ds(row, 64), :size]
            if position < 4:
                keep_ref[position * 64 : position * 64 + 64, target] = piece
            else:
                send_ref[position * 64 - 256 : position * 64 - 192, target] = piece.astype(BF16)


def spatial_step(
    place_ref, full_ref, contrasted_ref, mine0_ref, other0_ref, mine1_ref, other1_ref,
    time_ref, s0, k0, s1, k1, s2, k2, gram_ref, grad_ref,
):
    tm, pix = place_ref[0], place_ref[1]
    for (begin, _, order), mine_ref, other_ref in zip(
        FRAME_PARTS, (mine0_ref, mine1_ref), (other0_ref, other1_ref)
    ):
        place_temporal(begin, order, pix, mine_ref, other_ref, time_ref)
    make_gram(time_ref, gram_ref)
    for part, (send_ref, keep_ref) in enumerate(((s0, k0), (s1, k1), (s2, k2))):
        spatial_blocks(
            part, tm, full_ref, contrasted_ref, time_ref, gram_ref, send_ref, keep_ref, grad_ref
        )


def update(values, sums, got, rule, size):
    rows = sums.shape[0]
    if rows > size:
        got = jnp.concatenate([got[(i ^ 1) * size : (i ^ 1) * size + size] for i in range(rows // size)])
    coef, limit = (a[:rows] for a in rule)
    grad = sums.astype(F32) + got.astype(F32)
    return soften(values[:rows].astype(F32) + coef * grad, limit).astype(BF16)


def call(kernel, place, operands, outs, scratch=()):
    return pl.pallas_call(
        kernel,
        out_shape=[pltpu.VMEM(shape, dtype) for shape, dtype in outs],
        in_specs=[SMEM] + [VMEM] * len(operands),
        out_specs=[VMEM] * len(outs),
        scratch_shapes=scratch,
        compiler_params=PARAMS,
    )(place, *[pin(operand) for operand in operands])


def per_device(
    movie, offsets, spatial, temporal, step_spatial, step_temporal, thresh_spatial, thresh_temporal
):
    slab, strip = spatial.shape
    shard, span = temporal.shape
    rank = slab * lax.axis_size("tm")
    pixels = strip * lax.axis_size("pix")
    frames = span * lax.axis_size("tm")
    pix = lax.axis_index("pix")
    tm = lax.axis_index("tm")
    place = jnp.stack([tm, pix]).astype(jnp.int32)

    spatial, place = lax.optimization_barrier((spatial, place))

    def second_gather(slabs):
        return [jnp.concatenate([s, hop(s, "tm", order[1])]) for s, (_, _, order) in zip(slabs, PARTS)]

    def first_gather(near):
        return [(a, hop(a, "tm", order[0])) for a, (_, _, order) in zip(near, PARTS)]

    pair = jnp.concatenate([spatial, hop(spatial, "tm", START_PARTS[0][2][2])])
    mine = temporal
    for mask in (1, 2):
        mine = jnp.concatenate([mine, hop(mine, "pix", mask)])
    size = lax.axis_size("pix")
    up = [(i, (i + 1) % size) for i in range(size)]
    down = [(j, i) for i, j in up]
    before = lax.ppermute(movie[movie.shape[0] - EDGE :], "pix", up)
    after = lax.ppermute(movie[:EDGE], "pix", down)
    pair, mine, place = lax.optimization_barrier((pair, mine, place))
    near = [pair[:, begin : begin + width] for begin, width, _ in START_PARTS]
    near = [jnp.concatenate([a, hop(a, "tm", order[1])]) for a, (_, _, order) in zip(near, START_PARTS)]
    mine = jnp.concatenate([mine, hop(mine, "pix", 4)])
    blocks = range(strip // BLOCK)
    inner = blocks[1 : 3 * len(blocks) // 4]
    outer = [b for b in blocks if b not in inner]
    contrasted = contrast(functools.partial(stencil_inner, inner), place, offsets, movie)
    near, mine, contrasted = lax.optimization_barrier((near, mine, contrasted))
    pieces = [(a, hop(a, "tm", order[0])) for a, (_, _, order) in zip(near, START_PARTS)]
    far = hop(mine, "pix", 12)
    contrasted = contrast(
        functools.partial(stencil_outer, outer, size), place, offsets, movie, (contrasted, before, after)
    )
    pieces, mine, far, contrasted = lax.optimization_barrier((pieces, mine, far, contrasted))
    factors = (math.sqrt(rank) / pixels, 1.0, math.sqrt(rank) / frames, 1.0)
    steps = [a.reshape(1, rank) for a in (step_temporal, thresh_temporal, step_spatial, thresh_spatial)]

    half = rank // 2
    scratch = [pltpu.VMEM((rank, rank), BF16), pltpu.VMEM((rank, BLOCK), F32)]

    def both(parts):
        return [((half, width), dtype) for _, width, _ in parts for dtype in (BF16, F32)]

    for turn in range(ROUNDS):
        flat = [piece for pair in pieces for piece in pair]
        outs = [((rank, strip), BF16)] + both(FRAME_PARTS)
        if turn == 0:
            outs += [((rank, span), BF16)] + [((half // 2, width), BF16) for _, width, _ in FRAME_PARTS + PARTS]
            outs += [((half // 2, width), F32) for _, width, _ in FRAME_PARTS + PARTS for _ in range(2)]
            full, s0, k0, s1, k1, time, *rest = call(
                functools.partial(temporal_start, factors),
                place,
                flat + [contrasted, mine, far] + steps,
                outs,
                scratch + [pltpu.VMEM((rank, 8), F32)],
            )
            count = len(FRAME_PARTS)
            starts, rules = rest[: count + len(PARTS)], rest[count + len(PARTS) :]
            quads, slabs = starts[:count], starts[count:]
            rules = list(zip(rules[0::2], rules[1::2]))
        else:
            full, s0, k0, s1, k1 = call(temporal_step, place, flat + [contrasted, time], outs, scratch)
        grads = [(s0, k0), (s1, k1)]
        totals = [keep + hop(send, "pix", 1).astype(F32) for send, keep in grads]
        totals = [
            g[: half // 2] + hop(g[half // 2 :].astype(BF16), "pix", order[0]).astype(F32)
            for g, (_, _, order) in zip(totals, FRAME_PARTS)
        ]
        sums = []
        for g, (_, _, order) in zip(totals, FRAME_PARTS):
            g = g.astype(BF16)
            got = hop(g, "pix", order[1])
            got = jnp.concatenate([got[2 * shard :], got[: 2 * shard]])
            sums.append((g.astype(F32) + got.astype(F32)).astype(BF16))
        gots = [hop(g, "pix", order[2]) for g, (_, _, order) in zip(sums, FRAME_PARTS)]
        quads = [update(*each, shard) for each in zip(quads, sums, gots, rules[:count])]
        ends = []
        for q, (_, _, order) in zip(quads, FRAME_PARTS):
            mine = jnp.concatenate([q, hop(q, "pix", order[0])])
            ends += [mine, hop(mine, "pix", 1)]
        time, *grads = call(
            spatial_step, place, [full, contrasted] + ends, [((rank, span), BF16)] + both(PARTS), scratch
        )
        grads = list(zip(grads[0::2], grads[1::2]))
        totals = [
            keep + hop(send, "tm", order[0]).astype(F32) for (send, keep), (_, _, order) in zip(grads, PARTS)
        ]
        totals = [
            total[: 2 * slab] + hop(total[2 * slab :].astype(BF16), "tm", order[1]).astype(F32)
            for total, (_, _, order) in zip(totals, PARTS)
        ]
        last = turn == ROUNDS - 1
        if last:
            sums = [total[:slab] for total in totals]
            gots = [
                hop(total[slab:].astype(BF16), "tm", order[2]) for total, (_, _, order) in zip(totals, PARTS)
            ]
        else:
            sums = [total.astype(BF16) for total in totals]
            gots = [hop(total, "tm", order[2]) for total, (_, _, order) in zip(sums, PARTS)]
        slabs = [update(*each, slab) for each in zip(slabs, sums, gots, rules[count:])]
        if not last:
            pieces = first_gather(second_gather(slabs))
    return jnp.concatenate(slabs, 1), jnp.concatenate([q[:shard] for q in quads], 1)


def solution(mesh):
    placed = (P("pix", "tm"), P(), P("tm", "pix"), P("pix", "tm"), P(), P(), P(), P())
    return jax.shard_map(
        per_device,
        mesh=mesh,
        in_specs=placed,
        out_specs=(P("tm", "pix"), P("pix", "tm")),
        check_vma=False,
    )
```

```python
import functools
import math

import jax
import jax.numpy as jnp
from jax import lax
from jax.experimental import pallas as pl
from jax.experimental.pallas import tpu as pltpu
from jax.sharding import PartitionSpec as P

HALO = 129
EDGE = 144
BLOCK = 256
NBR = 8
ROUNDS = 2
BF16 = jnp.bfloat16
F32 = jnp.float32

PARTS = ((0, 768, (3, 4, 1)), (768, 640, (4, 1, 3)), (1408, 640, (1, 3, 4)))
FRAME_PARTS = ((0, 512, (4, 12, 2)), (512, 512, (12, 2, 4)))
START_PARTS = ((0, 1024, (1, 3, 4)), (1024, 1024, (3, 1, 4)))
LANES = 128
VMEM = pl.BlockSpec(memory_space=pltpu.VMEM)
SMEM = pl.BlockSpec(memory_space=pltpu.SMEM)
HBM = pl.BlockSpec(memory_space=pltpu.HBM)
COPIES = pltpu.SemaphoreType.DMA((16,))
PARAMS = pltpu.CompilerParams(vmem_limit_bytes=12 * 1024 * 1024)


def hop(a, axis, mask):
    size = lax.axis_size(axis)
    return lax.ppermute(a, axis, [(i, i ^ mask) for i in range(size)])


def reach(order, position):
    first, second, third = order
    return first * (position // 4) ^ second * (position // 2 % 2) ^ third * (position % 2)


def soften(values, limit):
    return values - jnp.clip(values, -limit, limit)


def nn(a, b):
    return jnp.dot(a, b, preferred_element_type=F32)


def nt(a, b):
    return lax.dot_general(a, b, (((1,), (1,)), ((), ())), preferred_element_type=F32)


class Copies:
    def __init__(self, sems):
        self.sems = sems
        self.used = 0

    def start(self, source, target):
        copy = pltpu.make_async_copy(source, target, self.sems.at[self.used])
        self.used += 1
        copy.start()
        return copy


def band(offsets_ref, columns, base, inside=None):
    step = (
        lax.broadcasted_iota(jnp.int32, (BLOCK, columns), 1)
        - lax.broadcasted_iota(jnp.int32, (BLOCK, columns), 0)
        + base
    )
    weight = jnp.where(step == 0, 1.0, 0.0).astype(F32)
    for k in range(NBR):
        weight = weight - jnp.where(step == offsets_ref[k], 1.0 / NBR, 0.0).astype(F32)
    if inside is not None:
        weight = jnp.where(inside, weight, 0.0)
    return weight.astype(BF16)


def stencil_blocks(which, place_ref, offsets_ref, movie_ref, edges, out_ref, held_ref, sems):
    count = movie_ref.shape[0] // BLOCK
    copies = Copies(sems)
    loads = {}
    for b in which:
        for n in range(max(b - 1, 0), min(b + 2, count)):
            if n not in loads:
                rows = pl.ds(n * BLOCK, BLOCK)
                loads[n] = copies.start(movie_ref.at[rows, :], held_ref.at[rows, :])
    main = band(offsets_ref, 3 * BLOCK, -BLOCK)
    for b in which:
        low = max(b - 1, 0)
        high = min(b + 2, count)
        for n in range(low, high):
            if n in loads:
                loads.pop(n).wait()
        first = (low - b + 1) * BLOCK
        total = nn(main[:, first : first + (high - low) * BLOCK], held_ref[low * BLOCK : high * BLOCK, :])
        if b == 0:
            total += nn(band(offsets_ref, EDGE, -EDGE, place_ref[1] > 0), edges[0][...])
        if b == count - 1:
            total += nn(band(offsets_ref, EDGE, BLOCK, place_ref[1] < edges[2] - 1), edges[1][...])
        out_ref[b * BLOCK : (b + 1) * BLOCK, :] = total.astype(BF16)


def stencil_inner(which, place_ref, offsets_ref, movie_ref, out_ref, held_ref, sems):
    stencil_blocks(which, place_ref, offsets_ref, movie_ref, None, out_ref, held_ref, sems)


def stencil_outer(
    which, strips, place_ref, offsets_ref, movie_ref, made_ref, before_ref, after_ref, out_ref, held_ref, sems
):
    del made_ref
    stencil_blocks(
        which, place_ref, offsets_ref, movie_ref, (before_ref, after_ref, strips), out_ref, held_ref, sems
    )


def contrast(kernel, place, offsets, movie, made=()):
    return pl.pallas_call(
        kernel,
        out_shape=pltpu.VMEM(movie.shape, BF16),
        in_specs=[SMEM, SMEM, HBM] + [VMEM] * len(made),
        out_specs=VMEM,
        scratch_shapes=[pltpu.VMEM(movie.shape, BF16), COPIES],
        input_output_aliases={3: 0} if made else {},
        compiler_params=PARAMS,
    )(place, offsets, pltpu.with_memory_space_constraint(movie, pltpu.HBM), *[pin(m) for m in made])


def pin(a):
    return pltpu.with_memory_space_constraint(a, pltpu.VMEM)


def place_temporal(begin, order, pix, mine_ref, other_ref, time_ref):
    columns = slice(begin, begin + mine_ref.shape[1])
    for position in range(8):
        piece = slice(position * 32, position * 32 + 32)
        for from_ref, side in ((mine_ref, 0), (other_ref, 1)):
            row = pl.multiple_of((pix ^ side ^ reach(order, position)) * 32, 32)
            time_ref[pl.ds(row, 32), columns] = from_ref[piece, :]


def temporal_blocks(part, pix, full_ref, contrasted_ref, gram_ref, time_ref, send_ref, keep_ref, grad_ref):
    begin, width, order = FRAME_PARTS[part]
    for low in range(0, width, BLOCK):
        columns = slice(begin + low, begin + low + BLOCK)
        target = slice(low, low + BLOCK)
        grad_ref[...] = nn(full_ref[...], contrasted_ref[:, columns]) - nn(gram_ref[...], time_ref[:, columns])
        for position in range(8):
            piece = slice(position * 32, position * 32 + 32)
            row = pl.multiple_of((pix ^ reach(order, position)) * 32, 32)
            keep_ref[piece, target] = grad_ref[pl.ds(row, 32), :]
            row = pl.multiple_of((pix ^ 1 ^ reach(order, position)) * 32, 32)
            send_ref[piece, target] = grad_ref[pl.ds(row, 32), :].astype(BF16)


def make_full(parts, tm, pieces, full_ref):
    for (begin, size, order), near, far in zip(parts, pieces[0::2], pieces[1::2]):
        for position in range(8):
            row = pl.multiple_of((tm ^ reach(order, position)) * 64, 64)
            piece = near if position < 4 else far
            full_ref[pl.ds(row, 64), begin : begin + size] = piece[pl.ds(position % 4 * 64, 64), :]


def make_gram(factor_ref, gram_ref):
    gram_ref[...] = (nt(factor_ref[...], factor_ref[...]) * (1.0 / math.sqrt(factor_ref.shape[0]))).astype(BF16)


def temporal_start(
    factors, place_ref, a0, b0, a1, b1, contrasted_ref, near_ref, far_ref, r0, r1, r2, r3,
    full_ref, s0, k0, s1, k1, time_ref, quad0_ref, quad1_ref, slab0_ref, slab1_ref, slab2_ref,
    tc0, tl0, tc1, tl1, sc0, sl0, sc1, sl1, sc2, sl2, gram_ref, grad_ref, table_ref,
):
    for i in range(8):
        grad_ref[i : i + 1, :] = jnp.zeros((1, grad_ref.shape[1]), F32)
    for low in range(0, table_ref.shape[0], LANES):
        for i, (row_ref, factor) in enumerate(zip((r0, r1, r2, r3), factors)):
            grad_ref[i : i + 1, :LANES] = row_ref[:, low : low + LANES] * factor
        table_ref[low : low + LANES, :] = grad_ref[0:8, :LANES].T
    tm, pix = place_ref[0], place_ref[1]
    for side, from_ref in ((0, near_ref), (12, far_ref)):
        for position in range(8):
            row = pl.multiple_of((pix ^ side ^ reach((4, 2, 1), position)) * 32, 32)
            time_ref[pl.ds(row, 32), :] = from_ref[position * 32 : position * 32 + 32, :]
    make_full(START_PARTS, tm, (a0, b0, a1, b1), full_ref)
    temporal_products(
        place_ref, contrasted_ref, time_ref, full_ref, ((s0, k0), (s1, k1)), gram_ref, grad_ref
    )
    for (begin, width, order), slab_ref in zip(PARTS, (slab0_ref, slab1_ref, slab2_ref)):
        for position in range(2):
            row = pl.multiple_of((tm ^ reach(order, position)) * 64, 64)
            slab_ref[position * 64 : position * 64 + 64, :] = full_ref[pl.ds(row, 64), begin : begin + width]
    for (begin, width, order), quad_ref in zip(FRAME_PARTS, (quad0_ref, quad1_ref)):
        for position in range(4):
            row = pl.multiple_of((pix ^ reach(order, position)) * 32, 32)
            quad_ref[position * 32 : position * 32 + 32, :] = time_ref[pl.ds(row, 32), begin : begin + width]
    lay_out(FRAME_PARTS, pix, 32, table_ref, 0, ((tc0, tl0), (tc1, tl1)))
    lay_out(PARTS, place_ref[0], 64, table_ref, 2, ((sc0, sl0), (sc1, sl1), (sc2, sl2)))


def lay_out(parts, here, size, table_ref, column, targets):
    for (_, width, order), pair in zip(parts, targets):
        for position in range(pair[0].shape[0] // size):
            row = pl.multiple_of((here ^ reach(order, position)) * size, size)
            piece = slice(position * size, position * size + size)
            for i, target in enumerate(pair):
                value = table_ref[pl.ds(row, size), column + i : column + i + 1]
                target[piece, :] = jnp.broadcast_to(value, (size, width))


def temporal_step(
    place_ref, a0, b0, a1, b1, a2, b2, contrasted_ref, time_ref,
    full_ref, s0, k0, s1, k1, gram_ref, grad_ref,
):
    make_full(PARTS, place_ref[0], (a0, b0, a1, b1, a2, b2), full_ref)
    temporal_products(
        place_ref, contrasted_ref, time_ref, full_ref, ((s0, k0), (s1, k1)), gram_ref, grad_ref
    )


def temporal_products(place_ref, contrasted_ref, time_ref, full_ref, targets, gram_ref, grad_ref):
    make_gram(full_ref, gram_ref)
    for part, (send_ref, keep_ref) in enumerate(targets):
        temporal_blocks(
            part, place_ref[1], full_ref, contrasted_ref, gram_ref, time_ref, send_ref, keep_ref, grad_ref
        )


def spatial_blocks(part, tm, full_ref, contrasted_ref, time_ref, gram_ref, send_ref, keep_ref, grad_ref):
    begin, width, order = PARTS[part]
    for low in range(0, width, BLOCK):
        size = min(BLOCK, width - low)
        pixels = slice(begin + low, begin + low + size)
        target = slice(low, low + size)
        grad_ref[:, :size] = nt(time_ref[...], contrasted_ref[pixels, :]) - nn(gram_ref[...], full_ref[:, pixels])
        for position in range(8):
            row = pl.multiple_of((tm ^ reach(order, position)) * 64, 64)
            piece = grad_ref[pl.ds(row, 64), :size]
            if position < 4:
                keep_ref[position * 64 : position * 64 + 64, target] = piece
            else:
                send_ref[position * 64 - 256 : position * 64 - 192, target] = piece.astype(BF16)


def spatial_step(
    place_ref, full_ref, contrasted_ref, mine0_ref, other0_ref, mine1_ref, other1_ref,
    time_ref, s0, k0, s1, k1, s2, k2, gram_ref, grad_ref,
):
    tm, pix = place_ref[0], place_ref[1]
    for (begin, _, order), mine_ref, other_ref in zip(
        FRAME_PARTS, (mine0_ref, mine1_ref), (other0_ref, other1_ref)
    ):
        place_temporal(begin, order, pix, mine_ref, other_ref, time_ref)
    make_gram(time_ref, gram_ref)
    for part, (send_ref, keep_ref) in enumerate(((s0, k0), (s1, k1), (s2, k2))):
        spatial_blocks(
            part, tm, full_ref, contrasted_ref, time_ref, gram_ref, send_ref, keep_ref, grad_ref
        )


def update(values, sums, got, rule, size):
    rows = sums.shape[0]
    if rows > size:
        got = jnp.concatenate([got[(i ^ 1) * size : (i ^ 1) * size + size] for i in range(rows // size)])
    coef, limit = (a[:rows] for a in rule)
    grad = sums.astype(F32) + got.astype(F32)
    return soften(values[:rows].astype(F32) + coef * grad, limit).astype(BF16)


def call(kernel, place, operands, outs, scratch=()):
    return pl.pallas_call(
        kernel,
        out_shape=[pltpu.VMEM(shape, dtype) for shape, dtype in outs],
        in_specs=[SMEM] + [VMEM] * len(operands),
        out_specs=[VMEM] * len(outs),
        scratch_shapes=scratch,
        compiler_params=PARAMS,
    )(place, *[pin(operand) for operand in operands])


def per_device(
    movie, offsets, spatial, temporal, step_spatial, step_temporal, thresh_spatial, thresh_temporal
):
    slab, strip = spatial.shape
    shard, span = temporal.shape
    rank = slab * lax.axis_size("tm")
    pixels = strip * lax.axis_size("pix")
    frames = span * lax.axis_size("tm")
    pix = lax.axis_index("pix")
    tm = lax.axis_index("tm")
    place = jnp.stack([tm, pix]).astype(jnp.int32)

    spatial, place = lax.optimization_barrier((spatial, place))

    def second_gather(slabs):
        return [jnp.concatenate([s, hop(s, "tm", order[1])]) for s, (_, _, order) in zip(slabs, PARTS)]

    def first_gather(near):
        return [(a, hop(a, "tm", order[0])) for a, (_, _, order) in zip(near, PARTS)]

    pair = jnp.concatenate([spatial, hop(spatial, "tm", START_PARTS[0][2][2])])
    mine = temporal
    for mask in (1, 2):
        mine = jnp.concatenate([mine, hop(mine, "pix", mask)])
    size = lax.axis_size("pix")
    up = [(i, (i + 1) % size) for i in range(size)]
    down = [(j, i) for i, j in up]
    before = lax.ppermute(movie[movie.shape[0] - EDGE :], "pix", up)
    after = lax.ppermute(movie[:EDGE], "pix", down)
    pair, mine, place, before, after = lax.optimization_barrier((pair, mine, place, before, after))
    near = [pair[:, begin : begin + width] for begin, width, _ in START_PARTS]
    near = [jnp.concatenate([a, hop(a, "tm", order[1])]) for a, (_, _, order) in zip(near, START_PARTS)]
    mine = jnp.concatenate([mine, hop(mine, "pix", 4)])
    blocks = range(strip // BLOCK)
    inner = blocks[1 : 1 + len(blocks) // 2]
    outer = [b for b in blocks if b not in inner]
    contrasted = contrast(functools.partial(stencil_inner, inner), place, offsets, movie)
    near, mine, contrasted = lax.optimization_barrier((near, mine, contrasted))
    pieces = [(a, hop(a, "tm", order[0])) for a, (_, _, order) in zip(near, START_PARTS)]
    far = hop(mine, "pix", 12)
    contrasted = contrast(
        functools.partial(stencil_outer, outer, size), place, offsets, movie, (contrasted, before, after)
    )
    pieces, mine, far, contrasted = lax.optimization_barrier((pieces, mine, far, contrasted))
    factors = (math.sqrt(rank) / pixels, 1.0, math.sqrt(rank) / frames, 1.0)
    steps = [a.reshape(1, rank) for a in (step_temporal, thresh_temporal, step_spatial, thresh_spatial)]

    half = rank // 2
    scratch = [pltpu.VMEM((rank, rank), BF16), pltpu.VMEM((rank, BLOCK), F32)]

    def both(parts):
        return [((half, width), dtype) for _, width, _ in parts for dtype in (BF16, F32)]

    for turn in range(ROUNDS):
        flat = [piece for pair in pieces for piece in pair]
        outs = [((rank, strip), BF16)] + both(FRAME_PARTS)
        if turn == 0:
            outs += [((rank, span), BF16)] + [((half // 2, width), BF16) for _, width, _ in FRAME_PARTS + PARTS]
            outs += [((half // 2, width), F32) for _, width, _ in FRAME_PARTS + PARTS for _ in range(2)]
            full, s0, k0, s1, k1, time, *rest = call(
                functools.partial(temporal_start, factors),
                place,
                flat + [contrasted, mine, far] + steps,
                outs,
                scratch + [pltpu.VMEM((rank, 8), F32)],
            )
            count = len(FRAME_PARTS)
            starts, rules = rest[: count + len(PARTS)], rest[count + len(PARTS) :]
            quads, slabs = starts[:count], starts[count:]
            rules = list(zip(rules[0::2], rules[1::2]))
        else:
            full, s0, k0, s1, k1 = call(temporal_step, place, flat + [contrasted, time], outs, scratch)
        grads = [(s0, k0), (s1, k1)]
        totals = [keep + hop(send, "pix", 1).astype(F32) for send, keep in grads]
        totals = [
            g[: half // 2] + hop(g[half // 2 :].astype(BF16), "pix", order[0]).astype(F32)
            for g, (_, _, order) in zip(totals, FRAME_PARTS)
        ]
        sums = []
        for g, (_, _, order) in zip(totals, FRAME_PARTS):
            g = g.astype(BF16)
            got = hop(g, "pix", order[1])
            got = jnp.concatenate([got[2 * shard :], got[: 2 * shard]])
            sums.append((g.astype(F32) + got.astype(F32)).astype(BF16))
        gots = [hop(g, "pix", order[2]) for g, (_, _, order) in zip(sums, FRAME_PARTS)]
        quads = [update(*each, shard) for each in zip(quads, sums, gots, rules[:count])]
        ends = []
        for q, (_, _, order) in zip(quads, FRAME_PARTS):
            mine = jnp.concatenate([q, hop(q, "pix", order[0])])
            ends += [mine, hop(mine, "pix", 1)]
        time, *grads = call(
            spatial_step, place, [full, contrasted] + ends, [((rank, span), BF16)] + both(PARTS), scratch
        )
        grads = list(zip(grads[0::2], grads[1::2]))
        totals = [
            keep + hop(send, "tm", order[0]).astype(F32) for (send, keep), (_, _, order) in zip(grads, PARTS)
        ]
        totals = [
            total[: 2 * slab] + hop(total[2 * slab :].astype(BF16), "tm", order[1]).astype(F32)
            for total, (_, _, order) in zip(totals, PARTS)
        ]
        last = turn == ROUNDS - 1
        if last:
            sums = [total[:slab] for total in totals]
            gots = [
                hop(total[slab:].astype(BF16), "tm", order[2]) for total, (_, _, order) in zip(totals, PARTS)
            ]
        else:
            sums = [total.astype(BF16) for total in totals]
            gots = [hop(total, "tm", order[2]) for total, (_, _, order) in zip(sums, PARTS)]
        slabs = [update(*each, slab) for each in zip(slabs, sums, gots, rules[count:])]
        if not last:
            pieces = first_gather(second_gather(slabs))
    return jnp.concatenate(slabs, 1), jnp.concatenate([q[:shard] for q in quads], 1)


def solution(mesh):
    placed = (P("pix", "tm"), P(), P("tm", "pix"), P("pix", "tm"), P(), P(), P(), P())
    return jax.shard_map(
        per_device,
        mesh=mesh,
        in_specs=placed,
        out_specs=(P("tm", "pix"), P("pix", "tm")),
        check_vma=False,
    )
```

```python
import functools
import math

import jax
import jax.numpy as jnp
from jax import lax
from jax.experimental import pallas as pl
from jax.experimental.pallas import tpu as pltpu
from jax.sharding import PartitionSpec as P

HALO = 129
EDGE = 144
BLOCK = 256
NBR = 8
ROUNDS = 2
BF16 = jnp.bfloat16
F32 = jnp.float32

PARTS = ((0, 768, (3, 4, 1)), (768, 640, (4, 1, 3)), (1408, 640, (1, 3, 4)))
FRAME_PARTS = ((0, 512, (4, 12, 2)), (512, 512, (12, 2, 4)))
START_PARTS = ((0, 1024, (1, 3, 4)), (1024, 1024, (3, 1, 4)))
LANES = 128
VMEM = pl.BlockSpec(memory_space=pltpu.VMEM)
SMEM = pl.BlockSpec(memory_space=pltpu.SMEM)
HBM = pl.BlockSpec(memory_space=pltpu.HBM)
COPIES = pltpu.SemaphoreType.DMA((16,))
PARAMS = pltpu.CompilerParams(vmem_limit_bytes=12 * 1024 * 1024)


def hop(a, axis, mask):
    size = lax.axis_size(axis)
    return lax.ppermute(a, axis, [(i, i ^ mask) for i in range(size)])


def reach(order, position):
    first, second, third = order
    return first * (position // 4) ^ second * (position // 2 % 2) ^ third * (position % 2)


def soften(values, limit):
    return values - jnp.clip(values, -limit, limit)


def nn(a, b):
    return jnp.dot(a, b, preferred_element_type=F32)


def nt(a, b):
    return lax.dot_general(a, b, (((1,), (1,)), ((), ())), preferred_element_type=F32)


class Copies:
    def __init__(self, sems):
        self.sems = sems
        self.used = 0

    def start(self, source, target):
        copy = pltpu.make_async_copy(source, target, self.sems.at[self.used])
        self.used += 1
        copy.start()
        return copy


def band(offsets_ref, columns, base, inside=None):
    step = (
        lax.broadcasted_iota(jnp.int32, (BLOCK, columns), 1)
        - lax.broadcasted_iota(jnp.int32, (BLOCK, columns), 0)
        + base
    )
    weight = jnp.where(step == 0, 1.0, 0.0).astype(F32)
    for k in range(NBR):
        weight = weight - jnp.where(step == offsets_ref[k], 1.0 / NBR, 0.0).astype(F32)
    if inside is not None:
        weight = jnp.where(inside, weight, 0.0)
    return weight.astype(BF16)


def stencil_blocks(which, place_ref, offsets_ref, movie_ref, edges, out_ref, held_ref, sems):
    count = movie_ref.shape[0] // BLOCK
    copies = Copies(sems)
    loads = {}
    for b in which:
        for n in range(max(b - 1, 0), min(b + 2, count)):
            if n not in loads:
                rows = pl.ds(n * BLOCK, BLOCK)
                loads[n] = copies.start(movie_ref.at[rows, :], held_ref.at[rows, :])
    main = band(offsets_ref, 3 * BLOCK, -BLOCK)
    for b in which:
        low = max(b - 1, 0)
        high = min(b + 2, count)
        for n in range(low, high):
            if n in loads:
                loads.pop(n).wait()
        first = (low - b + 1) * BLOCK
        total = nn(main[:, first : first + (high - low) * BLOCK], held_ref[low * BLOCK : high * BLOCK, :])
        if b == 0:
            total += nn(band(offsets_ref, EDGE, -EDGE, place_ref[1] > 0), edges[0][...])
        if b == count - 1:
            total += nn(band(offsets_ref, EDGE, BLOCK, place_ref[1] < edges[2] - 1), edges[1][...])
        out_ref[b * BLOCK : (b + 1) * BLOCK, :] = total.astype(BF16)


def stencil_inner(which, place_ref, offsets_ref, movie_ref, out_ref, held_ref, sems):
    stencil_blocks(which, place_ref, offsets_ref, movie_ref, None, out_ref, held_ref, sems)


def stencil_outer(
    which, strips, place_ref, offsets_ref, movie_ref, made_ref, before_ref, after_ref, out_ref, held_ref, sems
):
    del made_ref
    stencil_blocks(
        which, place_ref, offsets_ref, movie_ref, (before_ref, after_ref, strips), out_ref, held_ref, sems
    )


def contrast(kernel, place, offsets, movie, made=()):
    return pl.pallas_call(
        kernel,
        out_shape=pltpu.VMEM(movie.shape, BF16),
        in_specs=[SMEM, SMEM, HBM] + [VMEM] * len(made),
        out_specs=VMEM,
        scratch_shapes=[pltpu.VMEM(movie.shape, BF16), COPIES],
        input_output_aliases={3: 0} if made else {},
        compiler_params=PARAMS,
    )(place, offsets, pltpu.with_memory_space_constraint(movie, pltpu.HBM), *[pin(m) for m in made])


def pin(a):
    return pltpu.with_memory_space_constraint(a, pltpu.VMEM)


def place_temporal(begin, order, pix, mine_ref, other_ref, time_ref):
    columns = slice(begin, begin + mine_ref.shape[1])
    for position in range(8):
        piece = slice(position * 32, position * 32 + 32)
        for from_ref, side in ((mine_ref, 0), (other_ref, 1)):
            row = pl.multiple_of((pix ^ side ^ reach(order, position)) * 32, 32)
            time_ref[pl.ds(row, 32), columns] = from_ref[piece, :]


def temporal_blocks(part, pix, full_ref, contrasted_ref, gram_ref, time_ref, send_ref, keep_ref, grad_ref):
    begin, width, order = FRAME_PARTS[part]
    for low in range(0, width, BLOCK):
        columns = slice(begin + low, begin + low + BLOCK)
        target = slice(low, low + BLOCK)
        grad_ref[...] = nn(full_ref[...], contrasted_ref[:, columns]) - nn(gram_ref[...], time_ref[:, columns])
        for position in range(8):
            piece = slice(position * 32, position * 32 + 32)
            row = pl.multiple_of((pix ^ reach(order, position)) * 32, 32)
            keep_ref[piece, target] = grad_ref[pl.ds(row, 32), :]
            row = pl.multiple_of((pix ^ 1 ^ reach(order, position)) * 32, 32)
            send_ref[piece, target] = grad_ref[pl.ds(row, 32), :].astype(BF16)


def make_full(parts, tm, pieces, full_ref):
    for (begin, size, order), near, far in zip(parts, pieces[0::2], pieces[1::2]):
        for position in range(8):
            row = pl.multiple_of((tm ^ reach(order, position)) * 64, 64)
            piece = near if position < 4 else far
            full_ref[pl.ds(row, 64), begin : begin + size] = piece[pl.ds(position % 4 * 64, 64), :]


def make_gram(factor_ref, gram_ref):
    gram_ref[...] = (nt(factor_ref[...], factor_ref[...]) * (1.0 / math.sqrt(factor_ref.shape[0]))).astype(BF16)


def temporal_start(
    factors, place_ref, a0, b0, a1, b1, contrasted_ref, near_ref, far_ref, r0, r1, r2, r3,
    full_ref, s0, k0, s1, k1, time_ref, quad0_ref, quad1_ref, slab0_ref, slab1_ref, slab2_ref,
    tc0, tl0, tc1, tl1, sc0, sl0, sc1, sl1, sc2, sl2, gram_ref, grad_ref, table_ref,
):
    for i in range(8):
        grad_ref[i : i + 1, :] = jnp.zeros((1, grad_ref.shape[1]), F32)
    for low in range(0, table_ref.shape[0], LANES):
        for i, (row_ref, factor) in enumerate(zip((r0, r1, r2, r3), factors)):
            grad_ref[i : i + 1, :LANES] = row_ref[:, low : low + LANES] * factor
        table_ref[low : low + LANES, :] = grad_ref[0:8, :LANES].T
    tm, pix = place_ref[0], place_ref[1]
    for side, from_ref in ((0, near_ref), (12, far_ref)):
        for position in range(8):
            row = pl.multiple_of((pix ^ side ^ reach((4, 1, 2), position)) * 32, 32)
            time_ref[pl.ds(row, 32), :] = from_ref[position * 32 : position * 32 + 32, :]
    make_full(START_PARTS, tm, (a0, b0, a1, b1), full_ref)
    temporal_products(
        place_ref, contrasted_ref, time_ref, full_ref, ((s0, k0), (s1, k1)), gram_ref, grad_ref
    )
    for (begin, width, order), slab_ref in zip(PARTS, (slab0_ref, slab1_ref, slab2_ref)):
        for position in range(2):
            row = pl.multiple_of((tm ^ reach(order, position)) * 64, 64)
            slab_ref[position * 64 : position * 64 + 64, :] = full_ref[pl.ds(row, 64), begin : begin + width]
    for (begin, width, order), quad_ref in zip(FRAME_PARTS, (quad0_ref, quad1_ref)):
        for position in range(4):
            row = pl.multiple_of((pix ^ reach(order, position)) * 32, 32)
            quad_ref[position * 32 : position * 32 + 32, :] = time_ref[pl.ds(row, 32), begin : begin + width]
    lay_out(FRAME_PARTS, pix, 32, table_ref, 0, ((tc0, tl0), (tc1, tl1)))
    lay_out(PARTS, place_ref[0], 64, table_ref, 2, ((sc0, sl0), (sc1, sl1), (sc2, sl2)))


def lay_out(parts, here, size, table_ref, column, targets):
    for (_, width, order), pair in zip(parts, targets):
        for position in range(pair[0].shape[0] // size):
            row = pl.multiple_of((here ^ reach(order, position)) * size, size)
            piece = slice(position * size, position * size + size)
            for i, target in enumerate(pair):
                value = table_ref[pl.ds(row, size), column + i : column + i + 1]
                target[piece, :] = jnp.broadcast_to(value, (size, width))


def temporal_step(
    place_ref, a0, b0, a1, b1, a2, b2, contrasted_ref, time_ref,
    full_ref, s0, k0, s1, k1, gram_ref, grad_ref,
):
    make_full(PARTS, place_ref[0], (a0, b0, a1, b1, a2, b2), full_ref)
    temporal_products(
        place_ref, contrasted_ref, time_ref, full_ref, ((s0, k0), (s1, k1)), gram_ref, grad_ref
    )


def temporal_products(place_ref, contrasted_ref, time_ref, full_ref, targets, gram_ref, grad_ref):
    make_gram(full_ref, gram_ref)
    for part, (send_ref, keep_ref) in enumerate(targets):
        temporal_blocks(
            part, place_ref[1], full_ref, contrasted_ref, gram_ref, time_ref, send_ref, keep_ref, grad_ref
        )


def spatial_blocks(part, tm, full_ref, contrasted_ref, time_ref, gram_ref, send_ref, keep_ref, grad_ref):
    begin, width, order = PARTS[part]
    for low in range(0, width, BLOCK):
        size = min(BLOCK, width - low)
        pixels = slice(begin + low, begin + low + size)
        target = slice(low, low + size)
        grad_ref[:, :size] = nt(time_ref[...], contrasted_ref[pixels, :]) - nn(gram_ref[...], full_ref[:, pixels])
        for position in range(8):
            row = pl.multiple_of((tm ^ reach(order, position)) * 64, 64)
            piece = grad_ref[pl.ds(row, 64), :size]
            if position < 4:
                keep_ref[position * 64 : position * 64 + 64, target] = piece
            else:
                send_ref[position * 64 - 256 : position * 64 - 192, target] = piece.astype(BF16)


def spatial_step(
    place_ref, full_ref, contrasted_ref, mine0_ref, other0_ref, mine1_ref, other1_ref,
    time_ref, s0, k0, s1, k1, s2, k2, gram_ref, grad_ref,
):
    tm, pix = place_ref[0], place_ref[1]
    for (begin, _, order), mine_ref, other_ref in zip(
        FRAME_PARTS, (mine0_ref, mine1_ref), (other0_ref, other1_ref)
    ):
        place_temporal(begin, order, pix, mine_ref, other_ref, time_ref)
    make_gram(time_ref, gram_ref)
    for part, (send_ref, keep_ref) in enumerate(((s0, k0), (s1, k1), (s2, k2))):
        spatial_blocks(
            part, tm, full_ref, contrasted_ref, time_ref, gram_ref, send_ref, keep_ref, grad_ref
        )


def update(values, sums, got, rule, size):
    rows = sums.shape[0]
    if rows > size:
        got = jnp.concatenate([got[(i ^ 1) * size : (i ^ 1) * size + size] for i in range(rows // size)])
    coef, limit = (a[:rows] for a in rule)
    grad = sums.astype(F32) + got.astype(F32)
    return soften(values[:rows].astype(F32) + coef * grad, limit).astype(BF16)


def call(kernel, place, operands, outs, scratch=()):
    return pl.pallas_call(
        kernel,
        out_shape=[pltpu.VMEM(shape, dtype) for shape, dtype in outs],
        in_specs=[SMEM] + [VMEM] * len(operands),
        out_specs=[VMEM] * len(outs),
        scratch_shapes=scratch,
        compiler_params=PARAMS,
    )(place, *[pin(operand) for operand in operands])


def per_device(
    movie, offsets, spatial, temporal, step_spatial, step_temporal, thresh_spatial, thresh_temporal
):
    slab, strip = spatial.shape
    shard, span = temporal.shape
    rank = slab * lax.axis_size("tm")
    pixels = strip * lax.axis_size("pix")
    frames = span * lax.axis_size("tm")
    pix = lax.axis_index("pix")
    tm = lax.axis_index("tm")
    place = jnp.stack([tm, pix]).astype(jnp.int32)

    spatial, place = lax.optimization_barrier((spatial, place))

    def second_gather(slabs):
        return [jnp.concatenate([s, hop(s, "tm", order[1])]) for s, (_, _, order) in zip(slabs, PARTS)]

    def first_gather(near):
        return [(a, hop(a, "tm", order[0])) for a, (_, _, order) in zip(near, PARTS)]

    pair = jnp.concatenate([spatial, hop(spatial, "tm", START_PARTS[0][2][2])])
    mine = temporal
    for mask in (2, 1):
        mine = jnp.concatenate([mine, hop(mine, "pix", mask)])
    size = lax.axis_size("pix")
    up = [(i, (i + 1) % size) for i in range(size)]
    down = [(j, i) for i, j in up]
    pair, mine, place, low_edge, high_edge = lax.optimization_barrier(
        (pair, mine, place, movie[:EDGE], movie[movie.shape[0] - EDGE :])
    )
    before = lax.ppermute(high_edge, "pix", up)
    after = lax.ppermute(low_edge, "pix", down)
    near = [pair[:, begin : begin + width] for begin, width, _ in START_PARTS]
    near = [jnp.concatenate([a, hop(a, "tm", order[1])]) for a, (_, _, order) in zip(near, START_PARTS)]
    mine = jnp.concatenate([mine, hop(mine, "pix", 4)])
    blocks = range(strip // BLOCK)
    inner = blocks[1 : 1 + len(blocks) // 2]
    outer = [b for b in blocks if b not in inner]
    contrasted = contrast(functools.partial(stencil_inner, inner), place, offsets, movie)
    near, mine, contrasted, before, after = lax.optimization_barrier((near, mine, contrasted, before, after))
    pieces = [(a, hop(a, "tm", order[0])) for a, (_, _, order) in zip(near, START_PARTS)]
    far = hop(mine, "pix", 12)
    contrasted = contrast(
        functools.partial(stencil_outer, outer, size), place, offsets, movie, (contrasted, before, after)
    )
    pieces, mine, far, contrasted = lax.optimization_barrier((pieces, mine, far, contrasted))
    factors = (math.sqrt(rank) / pixels, 1.0, math.sqrt(rank) / frames, 1.0)
    steps = [a.reshape(1, rank) for a in (step_temporal, thresh_temporal, step_spatial, thresh_spatial)]

    half = rank // 2
    scratch = [pltpu.VMEM((rank, rank), BF16), pltpu.VMEM((rank, BLOCK), F32)]

    def both(parts):
        return [((half, width), dtype) for _, width, _ in parts for dtype in (BF16, F32)]

    for turn in range(ROUNDS):
        flat = [piece for pair in pieces for piece in pair]
        outs = [((rank, strip), BF16)] + both(FRAME_PARTS)
        if turn == 0:
            outs += [((rank, span), BF16)] + [((half // 2, width), BF16) for _, width, _ in FRAME_PARTS + PARTS]
            outs += [((half // 2, width), F32) for _, width, _ in FRAME_PARTS + PARTS for _ in range(2)]
            full, s0, k0, s1, k1, time, *rest = call(
                functools.partial(temporal_start, factors),
                place,
                flat + [contrasted, mine, far] + steps,
                outs,
                scratch + [pltpu.VMEM((rank, 8), F32)],
            )
            count = len(FRAME_PARTS)
            starts, rules = rest[: count + len(PARTS)], rest[count + len(PARTS) :]
            quads, slabs = starts[:count], starts[count:]
            rules = list(zip(rules[0::2], rules[1::2]))
        else:
            full, s0, k0, s1, k1 = call(temporal_step, place, flat + [contrasted, time], outs, scratch)
        grads = [(s0, k0), (s1, k1)]
        totals = [keep + hop(send, "pix", 1).astype(F32) for send, keep in grads]
        totals = [
            g[: half // 2] + hop(g[half // 2 :].astype(BF16), "pix", order[0]).astype(F32)
            for g, (_, _, order) in zip(totals, FRAME_PARTS)
        ]
        sums = []
        for g, (_, _, order) in zip(totals, FRAME_PARTS):
            g = g.astype(BF16)
            got = hop(g, "pix", order[1])
            got = jnp.concatenate([got[2 * shard :], got[: 2 * shard]])
            sums.append((g.astype(F32) + got.astype(F32)).astype(BF16))
        gots = [hop(g, "pix", order[2]) for g, (_, _, order) in zip(sums, FRAME_PARTS)]
        quads = [update(*each, shard) for each in zip(quads, sums, gots, rules[:count])]
        ends = []
        for q, (_, _, order) in zip(quads, FRAME_PARTS):
            mine = jnp.concatenate([q, hop(q, "pix", order[0])])
            ends += [mine, hop(mine, "pix", 1)]
        time, *grads = call(
            spatial_step, place, [full, contrasted] + ends, [((rank, span), BF16)] + both(PARTS), scratch
        )
        grads = list(zip(grads[0::2], grads[1::2]))
        totals = [
            keep + hop(send, "tm", order[0]).astype(F32) for (send, keep), (_, _, order) in zip(grads, PARTS)
        ]
        totals = [
            total[: 2 * slab] + hop(total[2 * slab :].astype(BF16), "tm", order[1]).astype(F32)
            for total, (_, _, order) in zip(totals, PARTS)
        ]
        last = turn == ROUNDS - 1
        if last:
            sums = [total[:slab] for total in totals]
            gots = [
                hop(total[slab:].astype(BF16), "tm", order[2]) for total, (_, _, order) in zip(totals, PARTS)
            ]
        else:
            sums = [total.astype(BF16) for total in totals]
            gots = [hop(total, "tm", order[2]) for total, (_, _, order) in zip(sums, PARTS)]
        slabs = [update(*each, slab) for each in zip(slabs, sums, gots, rules[count:])]
        if not last:
            pieces = first_gather(second_gather(slabs))
    return jnp.concatenate(slabs, 1), jnp.concatenate([q[:shard] for q in quads], 1)


def solution(mesh):
    placed = (P("pix", "tm"), P(), P("tm", "pix"), P("pix", "tm"), P(), P(), P(), P())
    return jax.shard_map(
        per_device,
        mesh=mesh,
        in_specs=placed,
        out_specs=(P("tm", "pix"), P("pix", "tm")),
        check_vma=False,
    )
```

```python
import functools
import math

import jax
import jax.numpy as jnp
from jax import lax
from jax.experimental import pallas as pl
from jax.experimental.pallas import tpu as pltpu
from jax.sharding import PartitionSpec as P

HALO = 129
EDGE = 144
BLOCK = 256
NBR = 8
ROUNDS = 2
BF16 = jnp.bfloat16
F32 = jnp.float32

PARTS = ((0, 768, (3, 4, 1)), (768, 640, (4, 1, 3)), (1408, 640, (1, 3, 4)))
FRAME_PARTS = ((0, 512, (4, 12, 2)), (512, 512, (12, 2, 4)))
START_PARTS = ((0, 1024, (1, 3, 4)), (1024, 1024, (3, 1, 4)))
LANES = 128
VMEM = pl.BlockSpec(memory_space=pltpu.VMEM)
SMEM = pl.BlockSpec(memory_space=pltpu.SMEM)
HBM = pl.BlockSpec(memory_space=pltpu.HBM)
COPIES = pltpu.SemaphoreType.DMA((16,))
PARAMS = pltpu.CompilerParams(vmem_limit_bytes=12 * 1024 * 1024)


def hop(a, axis, mask):
    size = lax.axis_size(axis)
    return lax.ppermute(a, axis, [(i, i ^ mask) for i in range(size)])


def reach(order, position):
    first, second, third = order
    return first * (position // 4) ^ second * (position // 2 % 2) ^ third * (position % 2)


def soften(values, limit):
    return values - jnp.clip(values, -limit, limit)


def nn(a, b):
    return jnp.dot(a, b, preferred_element_type=F32)


def nt(a, b):
    return lax.dot_general(a, b, (((1,), (1,)), ((), ())), preferred_element_type=F32)


class Copies:
    def __init__(self, sems):
        self.sems = sems
        self.used = 0

    def start(self, source, target):
        copy = pltpu.make_async_copy(source, target, self.sems.at[self.used])
        self.used += 1
        copy.start()
        return copy


def band(offsets_ref, columns, base, inside=None):
    step = (
        lax.broadcasted_iota(jnp.int32, (BLOCK, columns), 1)
        - lax.broadcasted_iota(jnp.int32, (BLOCK, columns), 0)
        + base
    )
    weight = jnp.where(step == 0, 1.0, 0.0).astype(F32)
    for k in range(NBR):
        weight = weight - jnp.where(step == offsets_ref[k], 1.0 / NBR, 0.0).astype(F32)
    if inside is not None:
        weight = jnp.where(inside, weight, 0.0)
    return weight.astype(BF16)


def stencil_blocks(which, place_ref, offsets_ref, movie_ref, edges, out_ref, held_ref, sems):
    count = movie_ref.shape[0] // BLOCK
    copies = Copies(sems)
    loads = {}
    for b in which:
        for n in range(max(b - 1, 0), min(b + 2, count)):
            if n not in loads:
                rows = pl.ds(n * BLOCK, BLOCK)
                loads[n] = copies.start(movie_ref.at[rows, :], held_ref.at[rows, :])
    main = band(offsets_ref, 3 * BLOCK, -BLOCK)
    for b in which:
        low = max(b - 1, 0)
        high = min(b + 2, count)
        for n in range(low, high):
            if n in loads:
                loads.pop(n).wait()
        first = (low - b + 1) * BLOCK
        total = nn(main[:, first : first + (high - low) * BLOCK], held_ref[low * BLOCK : high * BLOCK, :])
        if b == 0:
            total += nn(band(offsets_ref, EDGE, -EDGE, place_ref[1] > 0), edges[0][...])
        if b == count - 1:
            total += nn(band(offsets_ref, EDGE, BLOCK, place_ref[1] < edges[2] - 1), edges[1][...])
        out_ref[b * BLOCK : (b + 1) * BLOCK, :] = total.astype(BF16)


def stencil_inner(which, place_ref, offsets_ref, movie_ref, out_ref, held_ref, sems):
    stencil_blocks(which, place_ref, offsets_ref, movie_ref, None, out_ref, held_ref, sems)


def stencil_outer(
    which, strips, place_ref, offsets_ref, movie_ref, made_ref, before_ref, after_ref, out_ref, held_ref, sems
):
    del made_ref
    stencil_blocks(
        which, place_ref, offsets_ref, movie_ref, (before_ref, after_ref, strips), out_ref, held_ref, sems
    )


def contrast(kernel, place, offsets, movie, made=()):
    return pl.pallas_call(
        kernel,
        out_shape=pltpu.VMEM(movie.shape, BF16),
        in_specs=[SMEM, SMEM, HBM] + [VMEM] * len(made),
        out_specs=VMEM,
        scratch_shapes=[pltpu.VMEM(movie.shape, BF16), COPIES],
        input_output_aliases={3: 0} if made else {},
        compiler_params=PARAMS,
    )(place, offsets, pltpu.with_memory_space_constraint(movie, pltpu.HBM), *[pin(m) for m in made])


def pin(a):
    return pltpu.with_memory_space_constraint(a, pltpu.VMEM)


def place_temporal(begin, order, pix, mine_ref, other_ref, time_ref):
    columns = slice(begin, begin + mine_ref.shape[1])
    for position in range(8):
        piece = slice(position * 32, position * 32 + 32)
        for from_ref, side in ((mine_ref, 0), (other_ref, 1)):
            row = pl.multiple_of((pix ^ side ^ reach(order, position)) * 32, 32)
            time_ref[pl.ds(row, 32), columns] = from_ref[piece, :]


def temporal_blocks(part, pix, full_ref, contrasted_ref, gram_ref, time_ref, send_ref, keep_ref, grad_ref):
    begin, width, order = FRAME_PARTS[part]
    for low in range(0, width, BLOCK):
        columns = slice(begin + low, begin + low + BLOCK)
        target = slice(low, low + BLOCK)
        grad_ref[...] = nn(full_ref[...], contrasted_ref[:, columns]) - nn(gram_ref[...], time_ref[:, columns])
        for position in range(8):
            piece = slice(position * 32, position * 32 + 32)
            row = pl.multiple_of((pix ^ reach(order, position)) * 32, 32)
            keep_ref[piece, target] = grad_ref[pl.ds(row, 32), :]
            row = pl.multiple_of((pix ^ 1 ^ reach(order, position)) * 32, 32)
            send_ref[piece, target] = grad_ref[pl.ds(row, 32), :].astype(BF16)


def make_full(parts, tm, pieces, full_ref):
    for (begin, size, order), near, far in zip(parts, pieces[0::2], pieces[1::2]):
        for position in range(8):
            row = pl.multiple_of((tm ^ reach(order, position)) * 64, 64)
            piece = near if position < 4 else far
            full_ref[pl.ds(row, 64), begin : begin + size] = piece[pl.ds(position % 4 * 64, 64), :]


def make_gram(factor_ref, gram_ref):
    gram_ref[...] = (nt(factor_ref[...], factor_ref[...]) * (1.0 / math.sqrt(factor_ref.shape[0]))).astype(BF16)


def temporal_start(
    factors, place_ref, a0, b0, a1, b1, contrasted_ref, near_ref, far0_ref, far1_ref, r0, r1, r2, r3,
    full_ref, s0, k0, s1, k1, time_ref, quad0_ref, quad1_ref, slab0_ref, slab1_ref, slab2_ref,
    tc0, tl0, tc1, tl1, sc0, sl0, sc1, sl1, sc2, sl2, gram_ref, grad_ref, table_ref,
):
    for i in range(8):
        grad_ref[i : i + 1, :] = jnp.zeros((1, grad_ref.shape[1]), F32)
    for low in range(0, table_ref.shape[0], LANES):
        for i, (row_ref, factor) in enumerate(zip((r0, r1, r2, r3), factors)):
            grad_ref[i : i + 1, :LANES] = row_ref[:, low : low + LANES] * factor
        table_ref[low : low + LANES, :] = grad_ref[0:8, :LANES].T
    tm, pix = place_ref[0], place_ref[1]
    for position in range(8):
        piece = slice(position * 32, position * 32 + 32)
        row = pl.multiple_of((pix ^ reach((4, 1, 2), position)) * 32, 32)
        time_ref[pl.ds(row, 32), :] = near_ref[piece, :]
        row = pl.multiple_of((pix ^ 12 ^ reach((4, 1, 2), position)) * 32, 32)
        for (begin, width, _), far_ref in zip(FRAME_PARTS, (far0_ref, far1_ref)):
            time_ref[pl.ds(row, 32), begin : begin + width] = far_ref[piece, :]
    make_full(START_PARTS, tm, (a0, b0, a1, b1), full_ref)
    temporal_products(
        place_ref, contrasted_ref, time_ref, full_ref, ((s0, k0), (s1, k1)), gram_ref, grad_ref
    )
    for (begin, width, order), slab_ref in zip(PARTS, (slab0_ref, slab1_ref, slab2_ref)):
        for position in range(2):
            row = pl.multiple_of((tm ^ reach(order, position)) * 64, 64)
            slab_ref[position * 64 : position * 64 + 64, :] = full_ref[pl.ds(row, 64), begin : begin + width]
    for (begin, width, order), quad_ref in zip(FRAME_PARTS, (quad0_ref, quad1_ref)):
        for position in range(4):
            row = pl.multiple_of((pix ^ reach(order, position)) * 32, 32)
            quad_ref[position * 32 : position * 32 + 32, :] = time_ref[pl.ds(row, 32), begin : begin + width]
    lay_out(FRAME_PARTS, pix, 32, table_ref, 0, ((tc0, tl0), (tc1, tl1)))
    lay_out(PARTS, place_ref[0], 64, table_ref, 2, ((sc0, sl0), (sc1, sl1), (sc2, sl2)))


def lay_out(parts, here, size, table_ref, column, targets):
    for (_, width, order), pair in zip(parts, targets):
        for position in range(pair[0].shape[0] // size):
            row = pl.multiple_of((here ^ reach(order, position)) * size, size)
            piece = slice(position * size, position * size + size)
            for i, target in enumerate(pair):
                value = table_ref[pl.ds(row, size), column + i : column + i + 1]
                target[piece, :] = jnp.broadcast_to(value, (size, width))


def temporal_step(
    place_ref, a0, b0, a1, b1, a2, b2, contrasted_ref, time_ref,
    full_ref, s0, k0, s1, k1, gram_ref, grad_ref,
):
    make_full(PARTS, place_ref[0], (a0, b0, a1, b1, a2, b2), full_ref)
    temporal_products(
        place_ref, contrasted_ref, time_ref, full_ref, ((s0, k0), (s1, k1)), gram_ref, grad_ref
    )


def temporal_products(place_ref, contrasted_ref, time_ref, full_ref, targets, gram_ref, grad_ref):
    make_gram(full_ref, gram_ref)
    for part, (send_ref, keep_ref) in enumerate(targets):
        temporal_blocks(
            part, place_ref[1], full_ref, contrasted_ref, gram_ref, time_ref, send_ref, keep_ref, grad_ref
        )


def spatial_blocks(part, tm, full_ref, contrasted_ref, time_ref, gram_ref, send_ref, keep_ref, grad_ref):
    begin, width, order = PARTS[part]
    for low in range(0, width, BLOCK):
        size = min(BLOCK, width - low)
        pixels = slice(begin + low, begin + low + size)
        target = slice(low, low + size)
        grad_ref[:, :size] = nt(time_ref[...], contrasted_ref[pixels, :]) - nn(gram_ref[...], full_ref[:, pixels])
        for position in range(8):
            row = pl.multiple_of((tm ^ reach(order, position)) * 64, 64)
            piece = grad_ref[pl.ds(row, 64), :size]
            if position < 4:
                keep_ref[position * 64 : position * 64 + 64, target] = piece
            else:
                send_ref[position * 64 - 256 : position * 64 - 192, target] = piece.astype(BF16)


def spatial_step(
    place_ref, full_ref, contrasted_ref, mine0_ref, other0_ref, mine1_ref, other1_ref,
    time_ref, s0, k0, s1, k1, s2, k2, gram_ref, grad_ref,
):
    tm, pix = place_ref[0], place_ref[1]
    for (begin, _, order), mine_ref, other_ref in zip(
        FRAME_PARTS, (mine0_ref, mine1_ref), (other0_ref, other1_ref)
    ):
        place_temporal(begin, order, pix, mine_ref, other_ref, time_ref)
    make_gram(time_ref, gram_ref)
    for part, (send_ref, keep_ref) in enumerate(((s0, k0), (s1, k1), (s2, k2))):
        spatial_blocks(
            part, tm, full_ref, contrasted_ref, time_ref, gram_ref, send_ref, keep_ref, grad_ref
        )


def update(values, sums, got, rule, size):
    rows = sums.shape[0]
    if rows > size:
        got = jnp.concatenate([got[(i ^ 1) * size : (i ^ 1) * size + size] for i in range(rows // size)])
    coef, limit = (a[:rows] for a in rule)
    grad = sums.astype(F32) + got.astype(F32)
    return soften(values[:rows].astype(F32) + coef * grad, limit).astype(BF16)


def call(kernel, place, operands, outs, scratch=()):
    return pl.pallas_call(
        kernel,
        out_shape=[pltpu.VMEM(shape, dtype) for shape, dtype in outs],
        in_specs=[SMEM] + [VMEM] * len(operands),
        out_specs=[VMEM] * len(outs),
        scratch_shapes=scratch,
        compiler_params=PARAMS,
    )(place, *[pin(operand) for operand in operands])


def per_device(
    movie, offsets, spatial, temporal, step_spatial, step_temporal, thresh_spatial, thresh_temporal
):
    slab, strip = spatial.shape
    shard, span = temporal.shape
    rank = slab * lax.axis_size("tm")
    pixels = strip * lax.axis_size("pix")
    frames = span * lax.axis_size("tm")
    pix = lax.axis_index("pix")
    tm = lax.axis_index("tm")
    place = jnp.stack([tm, pix]).astype(jnp.int32)

    spatial, place = lax.optimization_barrier((spatial, place))

    def second_gather(slabs):
        return [jnp.concatenate([s, hop(s, "tm", order[1])]) for s, (_, _, order) in zip(slabs, PARTS)]

    def first_gather(near):
        return [(a, hop(a, "tm", order[0])) for a, (_, _, order) in zip(near, PARTS)]

    pair = jnp.concatenate([spatial, hop(spatial, "tm", START_PARTS[0][2][2])])
    mine = temporal
    for mask in (2, 1):
        mine = jnp.concatenate([mine, hop(mine, "pix", mask)])
    size = lax.axis_size("pix")
    up = [(i, (i + 1) % size) for i in range(size)]
    down = [(j, i) for i, j in up]
    pair, mine, place, low_edge, high_edge = lax.optimization_barrier(
        (pair, mine, place, movie[:EDGE], movie[movie.shape[0] - EDGE :])
    )
    before = lax.ppermute(high_edge, "pix", up)
    after = lax.ppermute(low_edge, "pix", down)
    near = [pair[:, begin : begin + width] for begin, width, _ in START_PARTS]
    near = [jnp.concatenate([a, hop(a, "tm", order[1])]) for a, (_, _, order) in zip(near, START_PARTS)]
    mine = jnp.concatenate([mine, hop(mine, "pix", 4)])
    blocks = range(strip // BLOCK)
    inner = blocks[1 : 1 + len(blocks) // 2]
    outer = [b for b in blocks if b not in inner]
    contrasted = contrast(functools.partial(stencil_inner, inner), place, offsets, movie)
    near, mine, contrasted, before, after = lax.optimization_barrier((near, mine, contrasted, before, after))
    pieces = [(a, hop(a, "tm", order[0])) for a, (_, _, order) in zip(near, START_PARTS)]
    far = [hop(mine[:, begin : begin + width], "pix", 12) for begin, width, _ in FRAME_PARTS]
    contrasted = contrast(
        functools.partial(stencil_outer, outer, size), place, offsets, movie, (contrasted, before, after)
    )
    pieces, mine, far, contrasted = lax.optimization_barrier((pieces, mine, far, contrasted))
    factors = (math.sqrt(rank) / pixels, 1.0, math.sqrt(rank) / frames, 1.0)
    steps = [a.reshape(1, rank) for a in (step_temporal, thresh_temporal, step_spatial, thresh_spatial)]

    half = rank // 2
    scratch = [pltpu.VMEM((rank, rank), BF16), pltpu.VMEM((rank, BLOCK), F32)]

    def both(parts):
        return [((half, width), dtype) for _, width, _ in parts for dtype in (BF16, F32)]

    for turn in range(ROUNDS):
        flat = [piece for pair in pieces for piece in pair]
        outs = [((rank, strip), BF16)] + both(FRAME_PARTS)
        if turn == 0:
            outs += [((rank, span), BF16)] + [((half // 2, width), BF16) for _, width, _ in FRAME_PARTS + PARTS]
            outs += [((half // 2, width), F32) for _, width, _ in FRAME_PARTS + PARTS for _ in range(2)]
            full, s0, k0, s1, k1, time, *rest = call(
                functools.partial(temporal_start, factors),
                place,
                flat + [contrasted, mine] + far + steps,
                outs,
                scratch + [pltpu.VMEM((rank, 8), F32)],
            )
            count = len(FRAME_PARTS)
            starts, rules = rest[: count + len(PARTS)], rest[count + len(PARTS) :]
            quads, slabs = starts[:count], starts[count:]
            rules = list(zip(rules[0::2], rules[1::2]))
        else:
            full, s0, k0, s1, k1 = call(temporal_step, place, flat + [contrasted, time], outs, scratch)
        grads = [(s0, k0), (s1, k1)]
        totals = [keep + hop(send, "pix", 1).astype(F32) for send, keep in grads]
        totals = [
            g[: half // 2] + hop(g[half // 2 :].astype(BF16), "pix", order[0]).astype(F32)
            for g, (_, _, order) in zip(totals, FRAME_PARTS)
        ]
        sums = []
        for g, (_, _, order) in zip(totals, FRAME_PARTS):
            g = g.astype(BF16)
            got = hop(g, "pix", order[1])
            got = jnp.concatenate([got[2 * shard :], got[: 2 * shard]])
            sums.append((g.astype(F32) + got.astype(F32)).astype(BF16))
        gots = [hop(g, "pix", order[2]) for g, (_, _, order) in zip(sums, FRAME_PARTS)]
        quads = [update(*each, shard) for each in zip(quads, sums, gots, rules[:count])]
        ends = []
        for q, (_, _, order) in zip(quads, FRAME_PARTS):
            mine = jnp.concatenate([q, hop(q, "pix", order[0])])
            ends += [mine, hop(mine, "pix", 1)]
        time, *grads = call(
            spatial_step, place, [full, contrasted] + ends, [((rank, span), BF16)] + both(PARTS), scratch
        )
        grads = list(zip(grads[0::2], grads[1::2]))
        totals = [
            keep + hop(send, "tm", order[0]).astype(F32) for (send, keep), (_, _, order) in zip(grads, PARTS)
        ]
        totals = [
            total[: 2 * slab] + hop(total[2 * slab :].astype(BF16), "tm", order[1]).astype(F32)
            for total, (_, _, order) in zip(totals, PARTS)
        ]
        last = turn == ROUNDS - 1
        if last:
            sums = [total[:slab] for total in totals]
            gots = [
                hop(total[slab:].astype(BF16), "tm", order[2]) for total, (_, _, order) in zip(totals, PARTS)
            ]
        else:
            sums = [total.astype(BF16) for total in totals]
            gots = [hop(total, "tm", order[2]) for total, (_, _, order) in zip(sums, PARTS)]
        slabs = [update(*each, slab) for each in zip(slabs, sums, gots, rules[count:])]
        if not last:
            pieces = first_gather(second_gather(slabs))
    return jnp.concatenate(slabs, 1), jnp.concatenate([q[:shard] for q in quads], 1)


def solution(mesh):
    placed = (P("pix", "tm"), P(), P("tm", "pix"), P("pix", "tm"), P(), P(), P(), P())
    return jax.shard_map(
        per_device,
        mesh=mesh,
        in_specs=placed,
        out_specs=(P("tm", "pix"), P("pix", "tm")),
        check_vma=False,
    )
```

```python
import functools
import math

import jax
import jax.numpy as jnp
from jax import lax
from jax.experimental import pallas as pl
from jax.experimental.pallas import tpu as pltpu
from jax.sharding import PartitionSpec as P

HALO = 129
EDGE = 144
BLOCK = 256
NBR = 8
ROUNDS = 2
BF16 = jnp.bfloat16
F32 = jnp.float32

PARTS = ((0, 768, (3, 4, 1)), (768, 640, (4, 1, 3)), (1408, 640, (1, 3, 4)))
FRAME_PARTS = ((0, 512, (4, 12, 2)), (512, 512, (12, 2, 4)))
START_PARTS = ((0, 1024, (1, 3, 4)), (1024, 1024, (3, 1, 4)))
LANES = 128
VMEM = pl.BlockSpec(memory_space=pltpu.VMEM)
SMEM = pl.BlockSpec(memory_space=pltpu.SMEM)
HBM = pl.BlockSpec(memory_space=pltpu.HBM)
COPIES = pltpu.SemaphoreType.DMA((16,))
PARAMS = pltpu.CompilerParams(vmem_limit_bytes=12 * 1024 * 1024)


def hop(a, axis, mask):
    size = lax.axis_size(axis)
    return lax.ppermute(a, axis, [(i, i ^ mask) for i in range(size)])


def reach(order, position):
    first, second, third = order
    return first * (position // 4) ^ second * (position // 2 % 2) ^ third * (position % 2)


def soften(values, limit):
    return values - jnp.clip(values, -limit, limit)


def nn(a, b):
    return jnp.dot(a, b, preferred_element_type=F32)


def nt(a, b):
    return lax.dot_general(a, b, (((1,), (1,)), ((), ())), preferred_element_type=F32)


class Copies:
    def __init__(self, sems):
        self.sems = sems
        self.used = 0

    def start(self, source, target):
        copy = pltpu.make_async_copy(source, target, self.sems.at[self.used])
        self.used += 1
        copy.start()
        return copy


def band(offsets_ref, columns, base, inside=None):
    step = (
        lax.broadcasted_iota(jnp.int32, (BLOCK, columns), 1)
        - lax.broadcasted_iota(jnp.int32, (BLOCK, columns), 0)
        + base
    )
    weight = jnp.where(step == 0, 1.0, 0.0).astype(F32)
    for k in range(NBR):
        weight = weight - jnp.where(step == offsets_ref[k], 1.0 / NBR, 0.0).astype(F32)
    if inside is not None:
        weight = jnp.where(inside, weight, 0.0)
    return weight.astype(BF16)


def stencil_blocks(which, place_ref, offsets_ref, movie_ref, edges, out_ref, held_ref, sems):
    count = movie_ref.shape[0] // BLOCK
    copies = Copies(sems)
    loads = {}
    for b in which:
        for n in range(max(b - 1, 0), min(b + 2, count)):
            if n not in loads:
                rows = pl.ds(n * BLOCK, BLOCK)
                loads[n] = copies.start(movie_ref.at[rows, :], held_ref.at[rows, :])
    main = band(offsets_ref, 3 * BLOCK, -BLOCK)
    for b in which:
        low = max(b - 1, 0)
        high = min(b + 2, count)
        for n in range(low, high):
            if n in loads:
                loads.pop(n).wait()
        first = (low - b + 1) * BLOCK
        total = nn(main[:, first : first + (high - low) * BLOCK], held_ref[low * BLOCK : high * BLOCK, :])
        if b == 0:
            total += nn(band(offsets_ref, EDGE, -EDGE, place_ref[1] > 0), edges[0][...])
        if b == count - 1:
            total += nn(band(offsets_ref, EDGE, BLOCK, place_ref[1] < edges[2] - 1), edges[1][...])
        out_ref[b * BLOCK : (b + 1) * BLOCK, :] = total.astype(BF16)


def stencil_inner(which, place_ref, offsets_ref, movie_ref, out_ref, held_ref, sems):
    stencil_blocks(which, place_ref, offsets_ref, movie_ref, None, out_ref, held_ref, sems)


def stencil_outer(
    which, strips, place_ref, offsets_ref, movie_ref, made_ref, before_ref, after_ref, out_ref, held_ref, sems
):
    del made_ref
    stencil_blocks(
        which, place_ref, offsets_ref, movie_ref, (before_ref, after_ref, strips), out_ref, held_ref, sems
    )


def contrast(kernel, place, offsets, movie, made=()):
    return pl.pallas_call(
        kernel,
        out_shape=pltpu.VMEM(movie.shape, BF16),
        in_specs=[SMEM, SMEM, HBM] + [VMEM] * len(made),
        out_specs=VMEM,
        scratch_shapes=[pltpu.VMEM(movie.shape, BF16), COPIES],
        input_output_aliases={3: 0} if made else {},
        compiler_params=PARAMS,
    )(place, offsets, pltpu.with_memory_space_constraint(movie, pltpu.HBM), *[pin(m) for m in made])


def pin(a):
    return pltpu.with_memory_space_constraint(a, pltpu.VMEM)


def place_temporal(begin, order, pix, mine_ref, other_ref, time_ref):
    columns = slice(begin, begin + mine_ref.shape[1])
    for position in range(8):
        piece = slice(position * 32, position * 32 + 32)
        for from_ref, side in ((mine_ref, 0), (other_ref, 1)):
            row = pl.multiple_of((pix ^ side ^ reach(order, position)) * 32, 32)
            time_ref[pl.ds(row, 32), columns] = from_ref[piece, :]


def temporal_blocks(part, pix, full_ref, contrasted_ref, gram_ref, time_ref, send_ref, keep_ref, grad_ref):
    begin, width, order = FRAME_PARTS[part]
    for low in range(0, width, BLOCK):
        columns = slice(begin + low, begin + low + BLOCK)
        target = slice(low, low + BLOCK)
        grad_ref[...] = nn(full_ref[...], contrasted_ref[:, columns]) - nn(gram_ref[...], time_ref[:, columns])
        for position in range(8):
            piece = slice(position * 32, position * 32 + 32)
            row = pl.multiple_of((pix ^ reach(order, position)) * 32, 32)
            keep_ref[piece, target] = grad_ref[pl.ds(row, 32), :]
            row = pl.multiple_of((pix ^ 1 ^ reach(order, position)) * 32, 32)
            send_ref[piece, target] = grad_ref[pl.ds(row, 32), :].astype(BF16)


def make_full(parts, tm, pieces, full_ref):
    for (begin, size, order), near, far in zip(parts, pieces[0::2], pieces[1::2]):
        for position in range(8):
            row = pl.multiple_of((tm ^ reach(order, position)) * 64, 64)
            piece = near if position < 4 else far
            full_ref[pl.ds(row, 64), begin : begin + size] = piece[pl.ds(position % 4 * 64, 64), :]


def make_gram(factor_ref, gram_ref):
    gram_ref[...] = (nt(factor_ref[...], factor_ref[...]) * (1.0 / math.sqrt(factor_ref.shape[0]))).astype(BF16)


def temporal_start(
    factors, place_ref, a0, b0, a1, b1, contrasted_ref, near_ref, far0_ref, far1_ref, r0, r1, r2, r3,
    full_ref, s0, k0, s1, k1, time_ref, quad0_ref, quad1_ref, slab0_ref, slab1_ref, slab2_ref,
    tc0, tl0, tc1, tl1, sc0, sl0, sc1, sl1, sc2, sl2, gram_ref, grad_ref, table_ref,
):
    for i in range(8):
        grad_ref[i : i + 1, :] = jnp.zeros((1, grad_ref.shape[1]), F32)
    for low in range(0, table_ref.shape[0], LANES):
        for i, (row_ref, factor) in enumerate(zip((r0, r1, r2, r3), factors)):
            grad_ref[i : i + 1, :LANES] = row_ref[:, low : low + LANES] * factor
        table_ref[low : low + LANES, :] = grad_ref[0:8, :LANES].T
    tm, pix = place_ref[0], place_ref[1]
    for position in range(8):
        piece = slice(position * 32, position * 32 + 32)
        row = pl.multiple_of((pix ^ reach((4, 1, 2), position)) * 32, 32)
        time_ref[pl.ds(row, 32), :] = near_ref[piece, :]
        row = pl.multiple_of((pix ^ 12 ^ reach((4, 1, 2), position)) * 32, 32)
        for (begin, width, _), far_ref in zip(FRAME_PARTS, (far0_ref, far1_ref)):
            time_ref[pl.ds(row, 32), begin : begin + width] = far_ref[piece, :]
    make_full(START_PARTS, tm, (a0, b0, a1, b1), full_ref)
    temporal_products(
        place_ref, contrasted_ref, time_ref, full_ref, ((s0, k0), (s1, k1)), gram_ref, grad_ref
    )
    for (begin, width, order), slab_ref in zip(PARTS, (slab0_ref, slab1_ref, slab2_ref)):
        for position in range(2):
            row = pl.multiple_of((tm ^ reach(order, position)) * 64, 64)
            slab_ref[position * 64 : position * 64 + 64, :] = full_ref[pl.ds(row, 64), begin : begin + width]
    for (begin, width, order), quad_ref in zip(FRAME_PARTS, (quad0_ref, quad1_ref)):
        for position in range(4):
            row = pl.multiple_of((pix ^ reach(order, position)) * 32, 32)
            quad_ref[position * 32 : position * 32 + 32, :] = time_ref[pl.ds(row, 32), begin : begin + width]
    lay_out(FRAME_PARTS, pix, 32, table_ref, 0, ((tc0, tl0), (tc1, tl1)))
    lay_out(PARTS, place_ref[0], 64, table_ref, 2, ((sc0, sl0), (sc1, sl1), (sc2, sl2)))


def lay_out(parts, here, size, table_ref, column, targets):
    for (_, width, order), pair in zip(parts, targets):
        for position in range(pair[0].shape[0] // size):
            row = pl.multiple_of((here ^ reach(order, position)) * size, size)
            piece = slice(position * size, position * size + size)
            for i, target in enumerate(pair):
                value = table_ref[pl.ds(row, size), column + i : column + i + 1]
                target[piece, :] = jnp.broadcast_to(value, (size, width))


def temporal_step(
    place_ref, a0, b0, a1, b1, a2, b2, contrasted_ref, time_ref,
    full_ref, s0, k0, s1, k1, gram_ref, grad_ref,
):
    make_full(PARTS, place_ref[0], (a0, b0, a1, b1, a2, b2), full_ref)
    temporal_products(
        place_ref, contrasted_ref, time_ref, full_ref, ((s0, k0), (s1, k1)), gram_ref, grad_ref
    )


def temporal_products(place_ref, contrasted_ref, time_ref, full_ref, targets, gram_ref, grad_ref):
    make_gram(full_ref, gram_ref)
    for part, (send_ref, keep_ref) in enumerate(targets):
        temporal_blocks(
            part, place_ref[1], full_ref, contrasted_ref, gram_ref, time_ref, send_ref, keep_ref, grad_ref
        )


def spatial_blocks(part, tm, full_ref, contrasted_ref, time_ref, gram_ref, send_ref, keep_ref, grad_ref):
    begin, width, order = PARTS[part]
    for low in range(0, width, BLOCK):
        size = min(BLOCK, width - low)
        pixels = slice(begin + low, begin + low + size)
        target = slice(low, low + size)
        grad_ref[:, :size] = nt(time_ref[...], contrasted_ref[pixels, :]) - nn(gram_ref[...], full_ref[:, pixels])
        for position in range(8):
            row = pl.multiple_of((tm ^ reach(order, position)) * 64, 64)
            piece = grad_ref[pl.ds(row, 64), :size]
            if position < 4:
                keep_ref[position * 64 : position * 64 + 64, target] = piece
            else:
                send_ref[position * 64 - 256 : position * 64 - 192, target] = piece.astype(BF16)


def spatial_step(
    place_ref, full_ref, contrasted_ref, mine0_ref, other0_ref, mine1_ref, other1_ref,
    time_ref, s0, k0, s1, k1, s2, k2, gram_ref, grad_ref,
):
    tm, pix = place_ref[0], place_ref[1]
    for (begin, _, order), mine_ref, other_ref in zip(
        FRAME_PARTS, (mine0_ref, mine1_ref), (other0_ref, other1_ref)
    ):
        place_temporal(begin, order, pix, mine_ref, other_ref, time_ref)
    make_gram(time_ref, gram_ref)
    for part, (send_ref, keep_ref) in enumerate(((s0, k0), (s1, k1), (s2, k2))):
        spatial_blocks(
            part, tm, full_ref, contrasted_ref, time_ref, gram_ref, send_ref, keep_ref, grad_ref
        )


def update(values, sums, got, rule, size):
    rows = sums.shape[0]
    if rows > size:
        got = jnp.concatenate([got[(i ^ 1) * size : (i ^ 1) * size + size] for i in range(rows // size)])
    coef, limit = (a[:rows] for a in rule)
    grad = sums.astype(F32) + got.astype(F32)
    return soften(values[:rows].astype(F32) + coef * grad, limit).astype(BF16)


def call(kernel, place, operands, outs, scratch=()):
    return pl.pallas_call(
        kernel,
        out_shape=[pltpu.VMEM(shape, dtype) for shape, dtype in outs],
        in_specs=[SMEM] + [VMEM] * len(operands),
        out_specs=[VMEM] * len(outs),
        scratch_shapes=scratch,
        compiler_params=PARAMS,
    )(place, *[pin(operand) for operand in operands])


def per_device(
    movie, offsets, spatial, temporal, step_spatial, step_temporal, thresh_spatial, thresh_temporal
):
    slab, strip = spatial.shape
    shard, span = temporal.shape
    rank = slab * lax.axis_size("tm")
    pixels = strip * lax.axis_size("pix")
    frames = span * lax.axis_size("tm")
    pix = lax.axis_index("pix")
    tm = lax.axis_index("tm")
    place = jnp.stack([tm, pix]).astype(jnp.int32)

    spatial, place = lax.optimization_barrier((spatial, place))

    def second_gather(slabs):
        return [jnp.concatenate([s, hop(s, "tm", order[1])]) for s, (_, _, order) in zip(slabs, PARTS)]

    def first_gather(near):
        return [(a, hop(a, "tm", order[0])) for a, (_, _, order) in zip(near, PARTS)]

    pair = jnp.concatenate([spatial, hop(spatial, "tm", START_PARTS[0][2][2])])
    mine = temporal
    for mask in (2, 1):
        mine = jnp.concatenate([mine, hop(mine, "pix", mask)])
    size = lax.axis_size("pix")
    up = [(i, (i + 1) % size) for i in range(size)]
    down = [(j, i) for i, j in up]
    before = lax.ppermute(movie[movie.shape[0] - EDGE :], "pix", up)
    pair, mine, place, low_edge, before = lax.optimization_barrier((pair, mine, place, movie[:EDGE], before))
    after = lax.ppermute(low_edge, "pix", down)
    near = [pair[:, begin : begin + width] for begin, width, _ in START_PARTS]
    near = [jnp.concatenate([a, hop(a, "tm", order[1])]) for a, (_, _, order) in zip(near, START_PARTS)]
    mine = jnp.concatenate([mine, hop(mine, "pix", 4)])
    blocks = range(strip // BLOCK)
    inner = blocks[1 : 1 + len(blocks) // 2]
    outer = [b for b in blocks if b not in inner]
    contrasted = contrast(functools.partial(stencil_inner, inner), place, offsets, movie)
    near, mine, contrasted, after = lax.optimization_barrier((near, mine, contrasted, after))
    pieces = [(a, hop(a, "tm", order[0])) for a, (_, _, order) in zip(near, START_PARTS)]
    far = [hop(mine[:, begin : begin + width], "pix", 12) for begin, width, _ in FRAME_PARTS]
    contrasted = contrast(
        functools.partial(stencil_outer, outer, size), place, offsets, movie, (contrasted, before, after)
    )
    pieces, mine, far, contrasted = lax.optimization_barrier((pieces, mine, far, contrasted))
    factors = (math.sqrt(rank) / pixels, 1.0, math.sqrt(rank) / frames, 1.0)
    steps = [a.reshape(1, rank) for a in (step_temporal, thresh_temporal, step_spatial, thresh_spatial)]

    half = rank // 2
    scratch = [pltpu.VMEM((rank, rank), BF16), pltpu.VMEM((rank, BLOCK), F32)]

    def both(parts):
        return [((half, width), dtype) for _, width, _ in parts for dtype in (BF16, F32)]

    for turn in range(ROUNDS):
        flat = [piece for pair in pieces for piece in pair]
        outs = [((rank, strip), BF16)] + both(FRAME_PARTS)
        if turn == 0:
            outs += [((rank, span), BF16)] + [((half // 2, width), BF16) for _, width, _ in FRAME_PARTS + PARTS]
            outs += [((half // 2, width), F32) for _, width, _ in FRAME_PARTS + PARTS for _ in range(2)]
            full, s0, k0, s1, k1, time, *rest = call(
                functools.partial(temporal_start, factors),
                place,
                flat + [contrasted, mine] + far + steps,
                outs,
                scratch + [pltpu.VMEM((rank, 8), F32)],
            )
            count = len(FRAME_PARTS)
            starts, rules = rest[: count + len(PARTS)], rest[count + len(PARTS) :]
            quads, slabs = starts[:count], starts[count:]
            rules = list(zip(rules[0::2], rules[1::2]))
        else:
            full, s0, k0, s1, k1 = call(temporal_step, place, flat + [contrasted, time], outs, scratch)
        grads = [(s0, k0), (s1, k1)]
        totals = [keep + hop(send, "pix", 1).astype(F32) for send, keep in grads]
        totals = [
            g[: half // 2] + hop(g[half // 2 :].astype(BF16), "pix", order[0]).astype(F32)
            for g, (_, _, order) in zip(totals, FRAME_PARTS)
        ]
        sums = []
        for g, (_, _, order) in zip(totals, FRAME_PARTS):
            g = g.astype(BF16)
            got = hop(g, "pix", order[1])
            got = jnp.concatenate([got[2 * shard :], got[: 2 * shard]])
            sums.append((g.astype(F32) + got.astype(F32)).astype(BF16))
        gots = [hop(g, "pix", order[2]) for g, (_, _, order) in zip(sums, FRAME_PARTS)]
        quads = [update(*each, shard) for each in zip(quads, sums, gots, rules[:count])]
        ends = []
        for q, (_, _, order) in zip(quads, FRAME_PARTS):
            mine = jnp.concatenate([q, hop(q, "pix", order[0])])
            ends += [mine, hop(mine, "pix", 1)]
        time, *grads = call(
            spatial_step, place, [full, contrasted] + ends, [((rank, span), BF16)] + both(PARTS), scratch
        )
        grads = list(zip(grads[0::2], grads[1::2]))
        totals = [
            keep + hop(send, "tm", order[0]).astype(F32) for (send, keep), (_, _, order) in zip(grads, PARTS)
        ]
        totals = [
            total[: 2 * slab] + hop(total[2 * slab :].astype(BF16), "tm", order[1]).astype(F32)
            for total, (_, _, order) in zip(totals, PARTS)
        ]
        last = turn == ROUNDS - 1
        if last:
            sums = [total[:slab] for total in totals]
            gots = [
                hop(total[slab:].astype(BF16), "tm", order[2]) for total, (_, _, order) in zip(totals, PARTS)
            ]
        else:
            sums = [total.astype(BF16) for total in totals]
            gots = [hop(total, "tm", order[2]) for total, (_, _, order) in zip(sums, PARTS)]
        slabs = [update(*each, slab) for each in zip(slabs, sums, gots, rules[count:])]
        if not last:
            pieces = first_gather(second_gather(slabs))
    return jnp.concatenate(slabs, 1), jnp.concatenate([q[:shard] for q in quads], 1)


def solution(mesh):
    placed = (P("pix", "tm"), P(), P("tm", "pix"), P("pix", "tm"), P(), P(), P(), P())
    return jax.shard_map(
        per_device,
        mesh=mesh,
        in_specs=placed,
        out_specs=(P("tm", "pix"), P("pix", "tm")),
        check_vma=False,
    )
```
